128 devices in a mesh: ctx: 32 (over y, x, core), head: 4 (over z).
Axes of the slice: x: 4, y: 4, z: 4, core: 2. Of those that a mesh axis runs over, the one named last changes fastest.
Arguments:
- queries: bfloat16 [49152, 3072], P('ctx', 'head'), may hold values from -6 to 6
- keys: bfloat16 [49152, 3072], P('ctx', 'head'), may hold values from -6 to 6
- values: bfloat16 [49152, 3072], P('ctx', 'head'), may hold values from -40 to 40
- log_decay: float32 [49152, 32], P('ctx', 'head'), may hold values from -0.75 to 0, as said below
- gain: float32 [3072], P('head'), may hold values from 0.5 to 1.5
- d_out: bfloat16 [49152, 3072], P('ctx', 'head'), may hold values from -6 to 6
Outputs:
- layer_out: bfloat16 [49152, 3072], P('ctx', 'head')
- d_queries: bfloat16 [49152, 3072], P('ctx', 'head')
- d_keys: bfloat16 [49152, 3072], P('ctx', 'head')
- d_values: bfloat16 [49152, 3072], P('ctx', 'head')
- d_gain: float32 [3072], P('head')
The draws below stay inside these ranges and needn't reach their ends.
Inputs may be any that keep to these rules, and one draw needn't show every extreme that they name: `log_decay`: every entry is negative.
All inputs are finite; a program needn't handle non-finite values.
Results may differ from the reference program's by a relative error of at most 0.0018.
Values sent between devices are 32-bit elements; how exact they have to be, the bound alone decides.
A program may use at most 192 MiB of HBM per device.

```python
import math
import jax
import jax.numpy as jnp
from jax import lax

HEAD_SIZE = 96
SEQUENCE_TOKENS = 49152
HEAD_TOTAL = 32
WIDTH = 3072


def draw_values(key, part):
    key = jax.random.fold_in(key, 11)
    random_child_keys = jax.random.split(key, 3)
    head_place = jnp.arange(HEAD_TOTAL, dtype=jnp.float32) / max(HEAD_TOTAL - 1, 1)
    random_perturbation = jax.random.uniform(random_child_keys[0], (HEAD_TOTAL,), minval=-0.15, maxval=0.15)
    head_scale = 0.3 * 10.0 ** jnp.clip(head_place + random_perturbation, 0.0, 1.0)
    column_scale = jnp.repeat(head_scale, HEAD_SIZE)
    row_scale = jnp.exp(jax.random.uniform(random_child_keys[1], (SEQUENCE_TOKENS, 1), minval=-1.15, maxval=1.15))
    noise = jnp.clip(jax.random.normal(random_child_keys[2], (SEQUENCE_TOKENS, WIDTH), jnp.float32), -4.0, 4.0)
    return (noise * row_scale * column_scale[None, :]).astype(jnp.bfloat16)


def draw_log_decay(key, part):
    key = jax.random.fold_in(key, 23)
    random_child_keys = jax.random.split(key, 6)
    fast_count = max(1, HEAD_TOTAL // 2)
    head_order = jax.random.permutation(random_child_keys[0], HEAD_TOTAL)
    is_fast = head_order < fast_count
    fast_rate = jnp.exp(jax.random.uniform(random_child_keys[1], (HEAD_TOTAL,), minval=math.log(1.0 / 50.0), maxval=math.log(1.0 / 30.0)))
    slow_rate = jnp.exp(jax.random.uniform(random_child_keys[2], (HEAD_TOTAL,), minval=math.log(0.05), maxval=math.log(0.5))) / SEQUENCE_TOKENS
    decay_speed = jnp.where(is_fast, fast_rate, slow_rate)
    random_perturbation = jax.random.uniform(random_child_keys[3], (SEQUENCE_TOKENS, HEAD_TOTAL), minval=0.5, maxval=1.5)
    spike_row_list = jax.random.randint(random_child_keys[4], (2,), 0, SEQUENCE_TOKENS)
    row_index_list = jnp.arange(SEQUENCE_TOKENS)
    spike_selected = jnp.any(row_index_list[:, None] == spike_row_list[None, :], axis=1)
    spike_depth = jnp.log(jax.random.uniform(random_child_keys[5], (HEAD_TOTAL,), minval=0.55, maxval=0.8))
    final_output = -decay_speed[None, :] * random_perturbation + jnp.where(spike_selected[:, None], spike_depth[None, :], 0.0)
    return final_output.astype(jnp.float32)


def block_scale(rng, extent, pieces, smallest, top_value):
    def one(axis_at, parts):
        steps = jax.random.uniform(jax.random.fold_in(jax.random.fold_in(rng, 6), axis_at), (parts,), jnp.float32, smallest / len(pieces), top_value / len(pieces))
        return jnp.repeat(jnp.exp(steps), extent[axis_at] // parts).reshape((-1,) + (1,) * (len(extent) - axis_at - 1))

    level = one(*pieces[0])
    for cut in pieces[1:]:
        level = level * one(*cut)
    return level


def scatter_about(key, shape, scale, most, shards=(), held_as=jnp.bfloat16):
    result = jax.random.normal(key, shape, jnp.float32) * scale
    if len(shards) > 0:
        result = block_scale(key, shape, shards, -0.22, 0.18) * result
    return jnp.clip(result, min=-most, max=most).astype(held_as)


def setup_inputs(seed: int = 0) -> dict:
    splits = jax.random.split(jax.random.key(seed), 7)
    queries = scatter_about(splits[0], (SEQUENCE_TOKENS, WIDTH), 1.0, 6.0, ((0, 32), (1, 4)))
    keys = scatter_about(splits[1], (SEQUENCE_TOKENS, WIDTH), 1.0, 6.0, ((0, 32), (1, 4)))
    values = draw_values(jax.random.fold_in(splits[6], 71), 0)
    log_decay = draw_log_decay(jax.random.fold_in(splits[6], 71), 0)
    gain = jnp.clip(1.0 + 0.1 * jax.random.normal(splits[4], (WIDTH,), jnp.float32), 0.5, 1.5)
    d_out = scatter_about(splits[5], (SEQUENCE_TOKENS, WIDTH), 1.0, 6.0, ((0, 32), (1, 4)))
    return dict(queries=queries, keys=keys, values=values, log_decay=log_decay, gain=gain, d_out=d_out)


def block_decay(log_sums):
    block_rows = log_sums.shape[0]
    row_index_list = jnp.arange(block_rows)
    causal = row_index_list[:, None] >= row_index_list[None, :]
    log_gaps = log_sums.T[:, :, None] - log_sums.T[:, None, :]
    return jnp.where(causal[None], jnp.exp(jnp.minimum(log_gaps, 0.0)), 0.0)

def reference(queries, keys, values, log_decay, gain, d_out):
    block_rows = min(256, SEQUENCE_TOKENS)
    block_count = SEQUENCE_TOKENS // block_rows

    def split(matrix):
        return matrix.astype(jnp.float32).reshape(block_count, block_rows, HEAD_TOTAL, HEAD_SIZE)
    q_blocks = split(queries)
    k_blocks = split(keys)
    v_blocks = split(values)
    decay_blocks = log_decay.astype(jnp.float32).reshape(block_count, block_rows, HEAD_TOTAL)
    zero_state = jnp.zeros((HEAD_TOTAL, HEAD_SIZE, HEAD_SIZE), jnp.float32)

    def forward_step(carried, inputs):
        q_rows, k_rows, v_rows, decay_steps = inputs
        log_sums = jnp.cumsum(decay_steps, axis=0)
        shard_sum = log_sums[-1]
        decay_mask = block_decay(log_sums)
        scores = jnp.einsum('thd,shd->hts', q_rows, k_rows) * decay_mask
        attended = jnp.einsum('hts,she->the', scores, v_rows)
        attended = attended + jnp.exp(log_sums)[:, :, None] * jnp.einsum('thd,hde->the', q_rows, carried)
        to_end = jnp.exp(shard_sum[None, :] - log_sums)
        new_state = jnp.exp(shard_sum)[:, None, None] * carried + jnp.einsum('sh,shd,she->hde', to_end, k_rows, v_rows)
        return (new_state, attended)
    _, attended = lax.scan(forward_step, zero_state, (q_blocks, k_blocks, v_blocks, decay_blocks))
    attended = attended.reshape(SEQUENCE_TOKENS, WIDTH)
    rms = jnp.sqrt(lax.optimization_barrier(jnp.mean(attended * attended, axis=1)) + 1e-06)
    normed = attended / rms[:, None]
    gain_float = gain.astype(jnp.float32)
    layer_out = (normed * gain_float).astype(jnp.bfloat16)
    up_grad = d_out.astype(jnp.float32)
    grad_norm = up_grad * gain_float
    d_gain = lax.optimization_barrier(jnp.sum(up_grad * normed, axis=0))
    inner = lax.optimization_barrier(jnp.sum(grad_norm * normed, axis=1)) / WIDTH
    grad_attended = (grad_norm - normed * inner[:, None]) / rms[:, None]
    g_blocks = grad_attended.reshape(block_count, block_rows, HEAD_TOTAL, HEAD_SIZE)

    def query_step(carried, inputs):
        q_rows, k_rows, v_rows, decay_steps, g_rows = inputs
        log_sums = jnp.cumsum(decay_steps, axis=0)
        shard_sum = log_sums[-1]
        decay_mask = block_decay(log_sums)
        grad_scores = jnp.einsum('the,she->hts', g_rows, v_rows) * decay_mask
        grad_q = jnp.einsum('hts,shd->thd', grad_scores, k_rows)
        grad_q = grad_q + jnp.exp(log_sums)[:, :, None] * jnp.einsum('the,hde->thd', g_rows, carried)
        to_end = jnp.exp(shard_sum[None, :] - log_sums)
        new_state = jnp.exp(shard_sum)[:, None, None] * carried + jnp.einsum('sh,shd,she->hde', to_end, k_rows, v_rows)
        return (new_state, grad_q)

    def key_step(carried, inputs):
        q_rows, k_rows, v_rows, decay_steps, g_rows = inputs
        log_sums = jnp.cumsum(decay_steps, axis=0)
        shard_sum = log_sums[-1]
        decay_mask = block_decay(log_sums)
        scores = jnp.einsum('thd,shd->hts', q_rows, k_rows) * decay_mask
        grad_scores = jnp.einsum('the,she->hts', g_rows, v_rows) * decay_mask
        to_end = jnp.exp(shard_sum[None, :] - log_sums)
        grad_k = jnp.einsum('hts,thd->shd', grad_scores, q_rows)
        grad_k = grad_k + to_end[:, :, None] * jnp.einsum('she,hde->shd', v_rows, carried)
        grad_v = jnp.einsum('hts,the->she', scores, g_rows)
        grad_v = grad_v + to_end[:, :, None] * jnp.einsum('shd,hde->she', k_rows, carried)
        new_state = jnp.exp(shard_sum)[:, None, None] * carried + jnp.einsum('th,thd,the->hde', jnp.exp(log_sums), q_rows, g_rows)
        return (new_state, (grad_k, grad_v))
    inputs = (q_blocks, k_blocks, v_blocks, decay_blocks, g_blocks)
    _, grad_q = lax.scan(query_step, zero_state, inputs)
    _, (grad_k, grad_v) = lax.scan(key_step, zero_state, inputs, reverse=True)
    d_queries = grad_q.reshape(SEQUENCE_TOKENS, WIDTH).astype(jnp.bfloat16)
    d_keys = grad_k.reshape(SEQUENCE_TOKENS, WIDTH).astype(jnp.bfloat16)
    d_values = grad_v.reshape(SEQUENCE_TOKENS, WIDTH).astype(jnp.bfloat16)
    return (layer_out, d_queries, d_keys, d_values, d_gain)
```

```python
import functools

import jax
import jax.numpy as jnp
from jax import lax
from jax.experimental import pallas as pl
from jax.experimental.pallas import tpu as pltpu
from jax.sharding import PartitionSpec as P

F32 = jnp.float32
BF16 = jnp.bfloat16
C = 128
HS = 96
GL = 384
NEG = -1e30
MESH = pl.DeviceIdType.MESH


def dot(a, b):
    return lax.dot_general(a, b, (((1,), (0,)), ((), ())), preferred_element_type=F32)


def dot_nt(a, b):
    return lax.dot_general(a, b, (((1,), (1,)), ((), ())), preferred_element_type=F32)


def split(x):
    hi = x.astype(BF16)
    lo = (x - hi.astype(F32)).astype(BF16)
    return hi, lo


def lane_mask(lo, hi, rows, dtype):
    lane = lax.broadcasted_iota(jnp.int32, (rows, 128), 1)
    return jnp.where((lane >= lo) & (lane < hi), 1.0, 0.0).astype(dtype)


def head_tiles(x, parity, dtype):
    rows = x.shape[0]
    t0, t1 = x[:, :128], x[:, 128:]
    zero = jnp.zeros((rows, 128), dtype)
    if parity == 0:
        a = [t0 * lane_mask(0, 96, rows, dtype), zero]
        b = [t0 * lane_mask(96, 128, rows, dtype), t1 * lane_mask(0, 64, rows, dtype)]
    else:
        a = [t0 * lane_mask(64, 128, rows, dtype), t1 * lane_mask(0, 32, rows, dtype)]
        b = [zero, t1 * lane_mask(32, 128, rows, dtype)]
    return jnp.concatenate(a, axis=1), jnp.concatenate(b, axis=1)


def stacked(x, parity):
    a, b = head_tiles(x, parity, x.dtype)
    return jnp.concatenate([a, b], axis=0)


def block_state(s, parity):
    a, b = head_tiles(s, parity, s.dtype)
    pad = jnp.zeros((64, 256), s.dtype)
    return jnp.concatenate([a, b, pad] if parity == 0 else [pad, a, b], axis=0)


def compact(u, parity):
    a, _ = head_tiles(u[:HS], parity, F32)
    _, b = head_tiles(u[HS:], parity, F32)
    return a + b


def merge(w0, w1):
    return jnp.concatenate([w0[:, :128], w0[:, 128:] + w1[:, :128], w1[:, 128:]], axis=1)


def group_lanes(cols):
    rows = cols[0].shape[0]
    lane = lax.broadcasted_iota(jnp.int32, (rows, 128), 1)
    return jnp.concatenate(
        [
            jnp.where(lane < 96, cols[0], cols[1]),
            jnp.where(lane < 64, cols[1], cols[2]),
            jnp.where(lane < 32, cols[2], cols[3]),
        ],
        axis=1,
    )


def columns_of(ct):
    full = jnp.concatenate([ct, jnp.zeros((C - 8, C), F32)], axis=0).T
    return [jnp.broadcast_to(full[:, h : h + 1], (C, C)) for h in range(8)]


def window(parity):
    return slice(128 * parity, 128 * parity + 256)


def causal_bias(transposed):
    row = lax.broadcasted_iota(jnp.int32, (C, C), 0)
    col = lax.broadcasted_iota(jnp.int32, (C, C), 1)
    keep = row <= col if transposed else row >= col
    return jnp.where(keep, 0.0, NEG)


def pair_decay(ct, cols, heads, bias):
    parts = [jnp.exp(cols[h] - ct[h : h + 1, :] + bias) for h in heads]
    return jnp.concatenate(parts, axis=1)


def pair_decay_t(ct, cols, heads, bias):
    parts = [jnp.exp(ct[h : h + 1, :] - cols[h] + bias) for h in heads]
    return jnp.concatenate(parts, axis=1)


def first_kernel(q_ref, k_ref, v_ref, ld_ref, ct_ref, u_ref, own_ref, tot_ref, part_ref):
    step = pl.program_id(0)

    @pl.when(step == 0)
    def _():
        own_ref[...] = jnp.zeros_like(own_ref)
        tot_ref[...] = jnp.zeros_like(tot_ref)

    row = lax.broadcasted_iota(jnp.int32, (C, C), 0)
    col = lax.broadcasted_iota(jnp.int32, (C, C), 1)
    upper = jnp.where(row <= col, 1.0, 0.0)
    ct = lax.dot_general(
        ld_ref[0], upper, (((1,), (0,)), ((), ())), preferred_element_type=F32,
        precision=lax.Precision.HIGHEST,
    )
    ct_ref[0] = ct
    tot_ref[...] += jnp.broadcast_to(ct[:, C - 1 : C], (8, 128))
    cols = columns_of(ct)
    bias = causal_bias(False)
    for g in range(2):
        lanes = slice(GL * g, GL * (g + 1))
        q, k, v = q_ref[:, lanes], k_ref[:, lanes], v_ref[:, lanes]
        cexp = group_lanes(cols[4 * g : 4 * g + 4])
        end = cexp[C - 1 : C, :]
        v_hi, v_lo = split(v.astype(F32) * jnp.exp(end - cexp))
        v_tail = jnp.concatenate([v_hi, v_lo], axis=0)
        kt = k.T
        outs, states = [], []
        for p in range(2):
            w = window(p)
            heads = (4 * g + 2 * p, 4 * g + 2 * p + 1)
            scores = dot_nt(q[:, w], stacked(k[:, w], p)) * pair_decay(ct, cols, heads, bias)
            hi, lo = split(scores)
            vs = stacked(v[:, w], p)
            outs.append(dot(hi, vs) + dot(lo, vs))
            kp = kt[192 * p : 192 * p + 192]
            states.append(compact(dot(jnp.concatenate([kp, kp], axis=1), v_tail[:, w]), p))
        part_ref[:, lanes] = merge(*outs)
        u = merge(*states)
        u_ref[0, :, lanes] = u
        own_ref[:, lanes] = jnp.exp(end) * own_ref[:, lanes] + u


def token_sums(x):
    acc = x[:, :128]
    for i in range(1, 6):
        acc = acc + x[:, 128 * i : 128 * i + 128]
    return jnp.sum(acc.T, axis=0, keepdims=True)


def second_kernel(q_ref, do_ref, gain_ref, ct_ref, u_ref, in_ref, part_ref, att_ref, sums_ref, st_ref):
    step = pl.program_id(0)

    @pl.when(step == 0)
    def _():
        st_ref[...] = in_ref[...]

    cols = columns_of(ct_ref[0])
    for g in range(2):
        lanes = slice(GL * g, GL * (g + 1))
        q = q_ref[:, lanes]
        cexp = group_lanes(cols[4 * g : 4 * g + 4])
        end = cexp[C - 1 : C, :]
        s = st_ref[:, lanes]
        s_hi, s_lo = split(s)
        outs = []
        for p in range(2):
            w = window(p)
            outs.append(dot(q[:, w], block_state(s_hi[:, w], p)) + dot(q[:, w], block_state(s_lo[:, w], p)))
        att_ref[:, lanes] = part_ref[:, lanes] + jnp.exp(cexp) * merge(*outs)
        st_ref[:, lanes] = jnp.exp(end) * s + u_ref[0, :, lanes]
    att = att_ref[...]
    grown = do_ref[...].astype(F32) * gain_ref[...]
    sums_ref[0] = jnp.concatenate(
        [token_sums(att * att), token_sums(grown * att), jnp.zeros((6, C), F32)], axis=0
    )


def third_kernel(
    width, q_ref, k_ref, v_ref, do_ref, gain_ref, ct_ref, u_ref, in_ref, att_ref, sums_ref,
    out_ref, dq_ref, dk_ref, dv_ref, dgain_ref, w_ref, back_ref, st_ref, start_ref,
):
    step = pl.program_id(0)

    @pl.when(step == 0)
    def _():
        st_ref[...] = in_ref[...]
        start_ref[...] = jnp.zeros_like(start_ref)
        back_ref[...] = jnp.zeros_like(back_ref)
        dgain_ref[...] = jnp.zeros_like(dgain_ref)

    ct = ct_ref[0]
    cols = columns_of(ct)
    bias, bias_t = causal_bias(False), causal_bias(True)
    rms = jnp.sqrt(sums_ref[0, 0:1, :] / width + 1e-06)
    inv = 1.0 / rms
    mean = sums_ref[0, 1:2, :] * inv / width
    inv_c = jnp.broadcast_to(inv, (C, C)).T
    coef_c = jnp.broadcast_to(mean * inv * inv, (C, C)).T
    inv_c = jnp.concatenate([inv_c] * 3, axis=1)
    coef_c = jnp.concatenate([coef_c] * 3, axis=1)
    for g in range(2):
        lanes = slice(GL * g, GL * (g + 1))
        q, k, v = q_ref[:, lanes], k_ref[:, lanes], v_ref[:, lanes]
        att = att_ref[:, lanes]
        up = do_ref[:, lanes].astype(F32)
        gain = gain_ref[:, lanes]
        normed = att * inv_c
        out_ref[:, lanes] = (normed * gain).astype(BF16)
        dgain_ref[:, lanes] += jnp.sum((up * normed).reshape(C // 8, 8, GL), axis=0)
        grad = up * gain * inv_c - att * coef_c
        g_hi, g_lo = split(grad)
        cexp = group_lanes(cols[4 * g : 4 * g + 4])
        from_start = jnp.exp(cexp)
        end = cexp[C - 1 : C, :]
        e_hi, e_lo = split(grad * from_start)
        e_both = jnp.concatenate([e_hi, e_lo], axis=0)
        s = st_ref[:, lanes]
        s_hi, s_lo = split(s)
        qt = q.T
        dqs, dks, dvs, ws = [], [], [], []
        for p in range(2):
            w = window(p)
            heads = (4 * g + 2 * p, 4 * g + 2 * p + 1)
            qw, kw, vw, hw, lw = q[:, w], k[:, w], v[:, w], g_hi[:, w], g_lo[:, w]
            ks, qs, vs = stacked(kw, p), stacked(qw, p), stacked(vw, p)
            hs, ls = stacked(hw, p), stacked(lw, p)
            decay = pair_decay(ct, cols, heads, bias)
            decay_t = pair_decay_t(ct, cols, heads, bias_t)
            b_hi, b_lo = block_state(s_hi[:, w], p), block_state(s_lo[:, w], p)
            d_hi, d_lo = split((dot_nt(hw, vs) + dot_nt(lw, vs)) * decay)
            dqs.append(dot(d_hi, ks) + dot(d_lo, ks) + (
                dot_nt(e_hi[:, w], b_hi) + dot_nt(e_lo[:, w], b_hi) + dot_nt(e_hi[:, w], b_lo)))
            t_hi, t_lo = split((dot_nt(vw, hs) + dot_nt(vw, ls)) * decay_t)
            dks.append(dot(t_hi, qs) + dot(t_lo, qs))
            p_hi, p_lo = split(dot_nt(kw, qs) * decay_t)
            dvs.append(dot(p_hi, hs) + dot(p_lo, hs) + dot(p_hi, ls))
            qp = qt[192 * p : 192 * p + 192]
            ws.append(compact(dot(jnp.concatenate([qp, qp], axis=1), e_both[:, w]), p))
        dq_ref[:, lanes] = merge(*dqs).astype(BF16)
        dk_ref[:, lanes] = merge(*dks)
        dv_ref[:, lanes] = merge(*dvs)
        wst = merge(*ws)
        w_ref[0, :, lanes] = wst
        back_ref[:, lanes] += jnp.exp(start_ref[0:1, lanes]) * wst
        start_ref[0:1, lanes] += end
        st_ref[:, lanes] = jnp.exp(end) * s + u_ref[0, :, lanes]


def fourth_kernel(k_ref, v_ref, ct_ref, w_ref, in_ref, dk_ref, dv_ref, dk_out, dv_out, st_ref):
    step = pl.program_id(0)

    @pl.when(step == 0)
    def _():
        st_ref[...] = in_ref[...]

    cols = columns_of(ct_ref[0])
    for g in range(2):
        lanes = slice(GL * g, GL * (g + 1))
        k, v = k_ref[:, lanes], v_ref[:, lanes]
        cexp = group_lanes(cols[4 * g : 4 * g + 4])
        end = cexp[C - 1 : C, :]
        tail = jnp.exp(end - cexp)
        s = st_ref[:, lanes]
        s_hi, s_lo = split(s)
        dks, dvs = [], []
        for p in range(2):
            w = window(p)
            b_hi, b_lo = block_state(s_hi[:, w], p), block_state(s_lo[:, w], p)
            dks.append(dot_nt(v[:, w], b_hi) + dot_nt(v[:, w], b_lo))
            dvs.append(dot(k[:, w], b_hi) + dot(k[:, w], b_lo))
        dk_out[:, lanes] = (dk_ref[:, lanes] + tail * merge(*dks)).astype(BF16)
        dv_out[:, lanes] = (dv_ref[:, lanes] + tail * merge(*dvs)).astype(BF16)
        st_ref[:, lanes] = jnp.exp(end) * s + w_ref[0, :, lanes]


def rows_spec(width, back=None):
    if back is None:
        return pl.BlockSpec((C, width), lambda i: (i, 0))
    return pl.BlockSpec((C, width), lambda i: (back - 1 - i, 0))


def chunk_spec(shape, back=None):
    if back is None:
        return pl.BlockSpec((1,) + shape, lambda i: (i, 0, 0))
    return pl.BlockSpec((1,) + shape, lambda i: (back - 1 - i, 0, 0))


def whole_spec(shape):
    return pl.BlockSpec(shape, lambda i: (0,) * len(shape))


def shape_of(*shape, dtype=F32):
    return jax.ShapeDtypeStruct(shape, dtype)


PARAMS = dict(vmem_limit_bytes=48 * 1024 * 1024)


def first(q, k, v, ld_t):
    n, width = q.shape
    chunks = n // C
    return pl.pallas_call(
        first_kernel,
        grid=(chunks,),
        in_specs=[rows_spec(width)] * 3 + [chunk_spec((8, C))],
        out_specs=[
            chunk_spec((8, C)), chunk_spec((HS, width)), whole_spec((HS, width)),
            whole_spec((8, 128)), rows_spec(width),
        ],
        out_shape=[
            shape_of(chunks, 8, C), shape_of(chunks, HS, width), shape_of(HS, width),
            shape_of(8, 128), shape_of(n, width),
        ],
        compiler_params=pltpu.CompilerParams(**PARAMS),
        name="first",
    )(q, k, v, ld_t)


def second(q, do, gain, ct, u, incoming, part):
    n, width = q.shape
    chunks = n // C
    return pl.pallas_call(
        second_kernel,
        grid=(chunks,),
        in_specs=[
            rows_spec(width), rows_spec(width), whole_spec((1, width)), chunk_spec((8, C)),
            chunk_spec((HS, width)), whole_spec((HS, width)), rows_spec(width),
        ],
        out_specs=[rows_spec(width), chunk_spec((8, C))],
        out_shape=[shape_of(n, width), shape_of(chunks, 8, C)],
        scratch_shapes=[pltpu.VMEM((HS, width), F32)],
        compiler_params=pltpu.CompilerParams(**PARAMS),
        name="second",
    )(q, do, gain, ct, u, incoming, part)


def third(total_width, q, k, v, do, gain, ct, u, incoming, att, sums):
    n, width = q.shape
    chunks = n // C
    rows = rows_spec(width)
    return pl.pallas_call(
        functools.partial(third_kernel, float(total_width)),
        grid=(chunks,),
        in_specs=[rows] * 4 + [
            whole_spec((1, width)), chunk_spec((8, C)), chunk_spec((HS, width)),
            whole_spec((HS, width)), rows, chunk_spec((8, C)),
        ],
        out_specs=[rows] * 4 + [
            whole_spec((8, width)), chunk_spec((HS, width)), whole_spec((HS, width)),
        ],
        out_shape=[
            shape_of(n, width, dtype=BF16), shape_of(n, width, dtype=BF16), shape_of(n, width),
            shape_of(n, width), shape_of(8, width), shape_of(chunks, HS, width), shape_of(HS, width),
        ],
        scratch_shapes=[pltpu.VMEM((HS, width), F32), pltpu.VMEM((8, width), F32)],
        compiler_params=pltpu.CompilerParams(**PARAMS),
        name="third",
    )(q, k, v, do, gain, ct, u, incoming, att, sums)


def fourth(k, v, ct, w, incoming, dk, dv):
    n, width = k.shape
    chunks = n // C
    rows = rows_spec(width, chunks)
    return pl.pallas_call(
        fourth_kernel,
        grid=(chunks,),
        in_specs=[
            rows, rows, chunk_spec((8, C), chunks), chunk_spec((HS, width), chunks),
            whole_spec((HS, width)), rows, rows,
        ],
        out_specs=[rows, rows],
        out_shape=[shape_of(n, width, dtype=BF16)] * 2,
        scratch_shapes=[pltpu.VMEM((HS, width), F32)],
        compiler_params=pltpu.CompilerParams(**PARAMS),
        name="fourth",
    )(k, v, ct, w, incoming, dk, dv)


OWNERS = 24


def greet(axis, count, me):
    barrier = pltpu.get_barrier_semaphore()

    @pl.loop(1, count)
    def _(i):
        pl.semaphore_signal(
            barrier, inc=1, device_id={axis: lax.rem(me + i, count)}, device_id_type=MESH
        )

    pl.semaphore_wait(barrier, count - 1)


def wait_bytes(ref, sem):
    pltpu.make_async_copy(ref, ref, sem).wait()


def scan_kernel(reverse, count, *refs):
    if reverse:
        (state_ref, tot_ref, gain_ref, out_ref, gain_out, send, taken, made, given,
         sems, gsend, gtaken, gsems) = refs
    else:
        state_ref, tot_ref, out_ref, send, taken, made, given, sems = refs
    me = lax.axis_index("ctx")
    is_owner = lax.rem(me, 4) != 3
    mine = (me // 4) * 3 + jnp.minimum(lax.rem(me, 4), 2)

    for o in range(OWNERS):
        r, half = o // 2, o % 2
        send[o, :, :GL] = state_ref[8 * r : 8 * r + 8, GL * half : GL * half + GL]
        tot = tot_ref[4 * half : 4 * half + 4, :]
        send[o, :, GL:] = jnp.concatenate([tot, tot], axis=0)
    greet("ctx", count, me)

    def copy_out(target):
        owner = (target // 4) * 3 + jnp.minimum(lax.rem(target, 4), 2)
        return pltpu.make_async_remote_copy(
            src_ref=send.at[owner], dst_ref=taken.at[me], send_sem=sems.at[0], recv_sem=sems.at[1],
            device_id={"ctx": target}, device_id_type=MESH,
        )

    @pl.loop(1, count)
    def _(i):
        target = lax.rem(me + i, count)

        @pl.when(lax.rem(target, 4) != 3)
        def _():
            copy_out(target).start()

    if reverse:
        sums = jnp.sum(gain_ref[...], axis=0, keepdims=True)
        parts = [sums[:, 128 * i : 128 * i + 128] for i in range(6)]
        tile = jnp.concatenate(parts + [jnp.zeros((2, 128), F32)], axis=0)
        gsend[...] = tile
        gtaken[me] = tile

        @pl.loop(1, count)
        def _(i):
            target = lax.rem(me + i, count)
            pltpu.make_async_remote_copy(
                src_ref=gsend, dst_ref=gtaken.at[me], send_sem=gsems.at[0], recv_sem=gsems.at[1],
                device_id={"ctx": target}, device_id_type=MESH,
            ).start()

    @pl.when(is_owner)
    def _():
        taken[me] = send[mine]
        wait_bytes(taken.at[pl.ds(0, count - 1)], sems.at[1])

        def step(i, acc):
            j = count - 1 - i if reverse else i
            made[j] = acc
            rows = [jnp.broadcast_to(taken[j, h : h + 1, GL:], (8, 128)) for h in range(4)]
            return jnp.exp(group_lanes(rows)) * acc + taken[j, :, :GL]

        lax.fori_loop(0, count, step, jnp.zeros((8, GL), F32), unroll=4)

        @pl.loop(1, count)
        def _(i):
            target = lax.rem(me + i, count)
            pltpu.make_async_remote_copy(
                src_ref=made.at[target], dst_ref=given.at[mine], send_sem=sems.at[2],
                recv_sem=sems.at[3], device_id={"ctx": target}, device_id_type=MESH,
            ).start()

        given[mine] = made[me]
        wait_bytes(given.at[pl.ds(0, OWNERS - 1)], sems.at[3])
        wait_bytes(send.at[pl.ds(0, OWNERS - 1)], sems.at[0])
        wait_bytes(made.at[pl.ds(0, count - 1)], sems.at[2])

    @pl.when(jnp.logical_not(is_owner))
    def _():
        wait_bytes(given, sems.at[3])
        wait_bytes(send, sems.at[0])

    for o in range(OWNERS):
        r, half = o // 2, o % 2
        out_ref[8 * r : 8 * r + 8, GL * half : GL * half + GL] = given[o]
    if reverse:
        wait_bytes(gtaken.at[pl.ds(0, count - 1)], gsems.at[1])
        gain_out[...] = lax.fori_loop(
            0, count, lambda i, acc: acc + gtaken[i], jnp.zeros((8, 128), F32)
        )
        wait_bytes(gtaken.at[pl.ds(0, count - 1)], gsems.at[0])


def scan_over_shards(state, tot, gain=None):
    reverse = gain is not None
    count = lax.axis_size("ctx")
    vmem = pl.BlockSpec(memory_space=pltpu.VMEM)
    scratch = [
        pltpu.VMEM((OWNERS, 8, 512), F32),
        pltpu.VMEM((count, 8, 512), F32),
        pltpu.VMEM((count, 8, GL), F32),
        pltpu.VMEM((OWNERS, 8, GL), F32),
        pltpu.SemaphoreType.DMA((4,)),
    ]
    outs, args = [shape_of(*state.shape)], [state, tot]
    if reverse:
        scratch += [
            pltpu.VMEM((8, 128), F32),
            pltpu.VMEM((count, 8, 128), F32),
            pltpu.SemaphoreType.DMA((2,)),
        ]
        outs.append(shape_of(8, 128))
        args.append(gain)
    return pl.pallas_call(
        functools.partial(scan_kernel, reverse, count),
        in_specs=[vmem] * len(args),
        out_specs=[vmem] * len(outs),
        out_shape=outs,
        scratch_shapes=scratch,
        compiler_params=pltpu.CompilerParams(
            collective_id=1 if reverse else 0, has_side_effects=True, **PARAMS
        ),
        name="scan_back" if reverse else "scan_on",
    )(*args)


def sums_kernel(count, sums_ref, out_ref, taken, sems):
    me = lax.axis_index("head")
    greet("head", count, me)

    @pl.loop(1, count)
    def _(i):
        pltpu.make_async_remote_copy(
            src_ref=sums_ref, dst_ref=taken.at[me], send_sem=sems.at[0], recv_sem=sems.at[1],
            device_id={"head": lax.rem(me + i, count)}, device_id_type=MESH,
        ).start()

    taken[me] = sums_ref[...]
    wait_bytes(taken.at[pl.ds(0, count - 1)], sems.at[1])
    total = taken[0]
    for i in range(1, count):
        total = total + taken[i]
    out_ref[...] = total
    wait_bytes(taken.at[pl.ds(0, count - 1)], sems.at[0])


def sum_over_heads(sums):
    count = lax.axis_size("head")
    vmem = pl.BlockSpec(memory_space=pltpu.VMEM)
    return pl.pallas_call(
        functools.partial(sums_kernel, count),
        in_specs=[vmem],
        out_specs=vmem,
        out_shape=shape_of(*sums.shape),
        scratch_shapes=[pltpu.VMEM((count,) + sums.shape, F32), pltpu.SemaphoreType.DMA((2,))],
        compiler_params=pltpu.CompilerParams(collective_id=2, has_side_effects=True, **PARAMS),
        name="sum_heads",
    )(sums)


def body(queries, keys, values, log_decay, gain, d_out):
    width = queries.shape[1]
    total_width = width * lax.axis_size("head")
    ld_t = log_decay.reshape(-1, C, 8).transpose(0, 2, 1)
    gain = gain[None]
    ct, u, own, tot, part = first(queries, keys, values, ld_t)
    (incoming,) = scan_over_shards(own, tot)
    att, sums = second(queries, d_out, gain, ct, u, incoming, part)
    sums = sum_over_heads(sums)
    out, dq, dk, dv, d_gain, w, back = third(
        total_width, queries, keys, values, d_out, gain, ct, u, incoming, att, sums
    )
    later, d_gain = scan_over_shards(back, tot, d_gain)
    dk, dv = fourth(keys, values, ct, w, later, dk, dv)
    return out, dq, dk, dv, d_gain[:6].reshape(width)


def solution(mesh):
    rows = P("ctx", "head")
    return jax.shard_map(
        body,
        mesh=mesh,
        in_specs=(rows, rows, rows, rows, P("head"), rows),
        out_specs=(rows, rows, rows, rows, P("head")),
        check_vma=False,
    )
```

```python
import functools

import jax
import jax.numpy as jnp
from jax import lax
from jax.experimental import pallas as pl
from jax.experimental.pallas import tpu as pltpu
from jax.sharding import PartitionSpec as P

F32 = jnp.float32
BF16 = jnp.bfloat16
C = 128
HS = 96
GL = 384
PIECES = 3
OWNERS = 24
NEG = -1e30
LOG2E = 1.4426950408889634
MESH = pl.DeviceIdType.MESH


def dot(a, b):
    return lax.dot_general(a, b, (((1,), (0,)), ((), ())), preferred_element_type=F32)


def dot_nt(a, b):
    return lax.dot_general(a, b, (((1,), (1,)), ((), ())), preferred_element_type=F32)


def both(hi, lo, w):
    r = dot(jnp.concatenate([hi, lo], axis=0), w)
    return r[: hi.shape[0]] + r[hi.shape[0] :]


def both_nt(hi, lo, w):
    r = dot_nt(jnp.concatenate([hi, lo], axis=0), w)
    return r[: hi.shape[0]] + r[hi.shape[0] :]


def split(x):
    hi = x.astype(BF16)
    lo = (x - hi.astype(F32)).astype(BF16)
    return hi, lo


def lane_mask(lo, hi, rows, dtype):
    lane = lax.broadcasted_iota(jnp.int32, (rows, 128), 1)
    return jnp.where((lane >= lo) & (lane < hi), 1.0, 0.0).astype(dtype)


def head_tiles(x, parity, dtype):
    rows = x.shape[0]
    t0, t1 = x[:, :128], x[:, 128:]
    zero = jnp.zeros((rows, 128), dtype)
    if parity == 0:
        a = [t0 * lane_mask(0, 96, rows, dtype), zero]
        b = [t0 * lane_mask(96, 128, rows, dtype), t1 * lane_mask(0, 64, rows, dtype)]
    else:
        a = [t0 * lane_mask(64, 128, rows, dtype), t1 * lane_mask(0, 32, rows, dtype)]
        b = [zero, t1 * lane_mask(32, 128, rows, dtype)]
    return jnp.concatenate(a, axis=1), jnp.concatenate(b, axis=1)


def stacked(x, parity):
    a, b = head_tiles(x, parity, x.dtype)
    return jnp.concatenate([a, b], axis=0)


def block_state(s, parity):
    a, b = head_tiles(s, parity, s.dtype)
    pad = jnp.zeros((64, 256), s.dtype)
    return jnp.concatenate([a, b, pad] if parity == 0 else [pad, a, b], axis=0)


def compact(u, parity):
    a, _ = head_tiles(u[:HS], parity, F32)
    _, b = head_tiles(u[HS:], parity, F32)
    return a + b


def merge(w0, w1):
    return jnp.concatenate([w0[:, :128], w0[:, 128:] + w1[:, :128], w1[:, 128:]], axis=1)


def group_lanes(cols):
    rows = cols[0].shape[0]
    lane = lax.broadcasted_iota(jnp.int32, (rows, 128), 1)
    return jnp.concatenate(
        [
            jnp.where(lane < 96, cols[0], cols[1]),
            jnp.where(lane < 64, cols[1], cols[2]),
            jnp.where(lane < 32, cols[2], cols[3]),
        ],
        axis=1,
    )


def columns_of(ct):
    full = jnp.concatenate([ct, jnp.zeros((C - 8, C), F32)], axis=0).T
    return [jnp.broadcast_to(full[:, h : h + 1], (C, C)) for h in range(8)]


def window(parity):
    return slice(128 * parity, 128 * parity + 256)


def causal_bias(transposed):
    row = lax.broadcasted_iota(jnp.int32, (C, C), 0)
    col = lax.broadcasted_iota(jnp.int32, (C, C), 1)
    keep = row <= col if transposed else row >= col
    return jnp.where(keep, 0.0, NEG)


def pair_decay(ct, cols, heads, bias):
    parts = [jnp.exp2(cols[h] - ct[h : h + 1, :] + bias) for h in heads]
    return jnp.concatenate(parts, axis=1)


def pair_decay_t(ct, cols, heads, bias):
    parts = [jnp.exp2(ct[h : h + 1, :] - cols[h] + bias) for h in heads]
    return jnp.concatenate(parts, axis=1)


def token_sums(x):
    acc = x[:, :128]
    for i in range(1, 6):
        acc = acc + x[:, 128 * i : 128 * i + 128]
    return jnp.sum(acc.T, axis=0, keepdims=True)


def wait_bytes(ref, sem):
    pltpu.make_async_copy(ref, ref, sem).wait()


def owner_of(device):
    return (device // 4) * 3 + jnp.minimum(lax.rem(device, 4), 2)


class Scan:
    def __init__(self, count, me, reverse, send, taken, made, given, sems):
        self.count, self.me, self.reverse = count, me, reverse
        self.send, self.taken, self.made, self.given, self.sems = send, taken, made, given, sems
        self.is_owner = lax.rem(me, 4) != 3
        self.mine = owner_of(me)

    def start(self, state_ref, tot_ref):
        for o in range(OWNERS):
            r, half = o // 2, o % 2
            self.send[o, :, :GL] = state_ref[8 * r : 8 * r + 8, GL * half : GL * half + GL]
            tot = tot_ref[4 * half : 4 * half + 4, :]
            self.send[o, :, GL:] = jnp.concatenate([tot, tot], axis=0)

        @pl.loop(1, self.count)
        def _(i):
            target = lax.rem(self.me + i, self.count)

            @pl.when(lax.rem(target, 4) != 3)
            def _():
                pltpu.make_async_remote_copy(
                    src_ref=self.send.at[owner_of(target)], dst_ref=self.taken.at[self.me],
                    send_sem=self.sems.at[0], recv_sem=self.sems.at[1],
                    device_id={"ctx": target}, device_id_type=MESH,
                ).start()

    def middle(self):
        count, me, mine = self.count, self.me, self.mine

        @pl.when(self.is_owner)
        def _():
            self.taken[me] = self.send[mine]
            wait_bytes(self.taken.at[pl.ds(0, count - 1)], self.sems.at[1])

            def step(i, acc):
                j = count - 1 - i if self.reverse else i
                self.made[j] = acc
                rows = [jnp.broadcast_to(self.taken[j, h : h + 1, GL:], (8, 128)) for h in range(4)]
                return jnp.exp2(group_lanes(rows)) * acc + self.taken[j, :, :GL]

            lax.fori_loop(0, count, step, jnp.zeros((8, GL), F32), unroll=4)

            @pl.loop(1, count)
            def _(i):
                target = lax.rem(me + i, count)
                pltpu.make_async_remote_copy(
                    src_ref=self.made.at[target], dst_ref=self.given.at[mine],
                    send_sem=self.sems.at[2], recv_sem=self.sems.at[3],
                    device_id={"ctx": target}, device_id_type=MESH,
                ).start()

            self.given[mine] = self.made[me]

    def finish(self, out_ref):
        @pl.when(self.is_owner)
        def _():
            wait_bytes(self.given.at[pl.ds(0, OWNERS - 1)], self.sems.at[3])
            wait_bytes(self.send.at[pl.ds(0, OWNERS - 1)], self.sems.at[0])
            wait_bytes(self.made.at[pl.ds(0, self.count - 1)], self.sems.at[2])

        @pl.when(jnp.logical_not(self.is_owner))
        def _():
            wait_bytes(self.given, self.sems.at[3])
            wait_bytes(self.send, self.sems.at[0])

        for o in range(OWNERS):
            r, half = o // 2, o % 2
            out_ref[8 * r : 8 * r + 8, GL * half : GL * half + GL] = self.given[o]


def layer_kernel(
    shards, head_shards, total_width, chunks, q_in, k_in, v_in, do_in, gain_ref, ld_ref,
    out_ref, dq_ref, dk_ref, dv_ref, dgain_ref,
    q_s, k_s, v_s, do_s, in_sems, ct_s, cexp_s, att_s, u_s, shi_s, slo_s, ghi_s, glo_s, ehi_s, elo_s,
    dv_s, own_s, tot_s, run_s, start_s, dg_s, sums_s, sums_t, sums_sems,
    gsend, gtaken, gsems, *scan_refs,
):
    remote = shards > 1
    dk_s = att_s
    if remote:
        me, my_head = lax.axis_index("ctx"), lax.axis_index("head")
        on = Scan(shards, me, False, *scan_refs[:5])
        back = Scan(shards, me, True, *scan_refs[5:])
        barrier = pltpu.get_barrier_semaphore()

        @pl.loop(1, shards)
        def _(i):
            pl.semaphore_signal(
                barrier, inc=1, device_id={"ctx": lax.rem(me + i, shards)}, device_id_type=MESH
            )

        @pl.loop(1, head_shards)
        def _(i):
            pl.semaphore_signal(
                barrier, inc=1, device_id={"head": lax.rem(my_head + i, head_shards)},
                device_id_type=MESH,
            )

    per = chunks // PIECES
    inputs = [(k_in, k_s), (v_in, v_s), (q_in, q_s), (do_in, do_s)]

    def arrival(a, b):
        rows = pl.ds(b * per * C, per * C)
        return pltpu.make_async_copy(inputs[a][0].at[rows], inputs[a][1].at[rows], in_sems.at[a, b])

    for b in range(PIECES):
        arrival(0, b).start()
        arrival(1, b).start()
    for a in (2, 3):
        for b in range(PIECES):
            arrival(a, b).start()

    def rows_of(i):
        return pl.ds(pl.multiple_of(i * C, C), C)

    groups = [slice(GL * g, GL * (g + 1)) for g in range(2)]

    row = lax.broadcasted_iota(jnp.int32, (C, C), 0)
    col = lax.broadcasted_iota(jnp.int32, (C, C), 1)
    upper = jnp.where(row <= col, 1.0, 0.0)
    ct_s[...] = LOG2E * lax.dot_general(
        ld_ref[...], upper, (((1,), (0,)), ((), ())), preferred_element_type=F32,
        precision=lax.Precision.HIGHEST,
    )
    own_s[...] = jnp.zeros_like(own_s)
    tot_s[...] = jnp.zeros_like(tot_s)

    def ct_of(i):
        return ct_s[pl.ds(pl.multiple_of(i * 8, 8), 8), :]

    def states(i):
        rows = rows_of(i)
        ct = ct_of(i)
        tot_s[...] += jnp.broadcast_to(ct[:, C - 1 : C], (8, 128))
        cols = columns_of(ct)
        for g, lanes in enumerate(groups):
            cexp = group_lanes(cols[4 * g : 4 * g + 4])
            cexp_s[rows, lanes] = cexp
            end = cexp[C - 1 : C, :]
            v_hi, v_lo = split(v_s[rows, lanes].astype(F32) * jnp.exp2(end - cexp))
            v_tail = jnp.concatenate([v_hi, v_lo], axis=0)
            kt = k_s[rows, lanes].T
            parts = []
            for p in range(2):
                kp = kt[192 * p : 192 * p + 192]
                parts.append(compact(dot(jnp.concatenate([kp, kp], axis=1), v_tail[:, window(p)]), p))
            u = merge(*parts)
            u_s[i, :, lanes] = u
            own_s[:, lanes] = jnp.exp2(end) * own_s[:, lanes] + u

    def local_rows(i):
        rows = rows_of(i)
        ct = ct_of(i)
        cols = columns_of(ct)
        bias = causal_bias(False)
        for g, lanes in enumerate(groups):
            q, k, v = q_s[rows, lanes], k_s[rows, lanes], v_s[rows, lanes]
            outs = []
            for p in range(2):
                w = window(p)
                heads = (4 * g + 2 * p, 4 * g + 2 * p + 1)
                scores = dot_nt(q[:, w], stacked(k[:, w], p)) * pair_decay(ct, cols, heads, bias)
                outs.append(both(*split(scores), stacked(v[:, w], p)))
            att_s[rows, lanes] = merge(*outs)

    def whole_rows(i):
        rows = rows_of(i)
        for g, lanes in enumerate(groups):
            q = q_s[rows, lanes]
            cexp = cexp_s[rows, lanes]
            end = cexp[C - 1 : C, :]
            s = run_s[:, lanes]
            s_hi, s_lo = split(s)
            shi_s[i, :, lanes] = s_hi
            slo_s[i, :, lanes] = s_lo
            outs = []
            for p in range(2):
                w = window(p)
                outs.append(dot(q[:, w], block_state(s_hi[:, w], p)) + dot(q[:, w], block_state(s_lo[:, w], p)))
            att_s[rows, lanes] += jnp.exp2(cexp) * merge(*outs)
            run_s[:, lanes] = jnp.exp2(end) * s + u_s[i, :, lanes]
        att = att_s[rows, :]
        grown = do_s[rows, :].astype(F32) * gain_ref[...]
        sums_s[i] = jnp.concatenate(
            [token_sums(att * att), token_sums(grown * att), jnp.zeros((6, C), F32)], axis=0
        )

    def sums_copy(b, target):
        part = pl.ds(b * per, per)
        return pltpu.make_async_remote_copy(
            src_ref=sums_s.at[part], dst_ref=sums_t.at[my_head, part], send_sem=sums_sems.at[0, b],
            recv_sem=sums_sems.at[1, b], device_id={"head": target}, device_id_type=MESH,
        )

    def norm_rows(i):
        rows = rows_of(i)
        if remote:
            sums = sums_t[0, i]
            for j in range(1, head_shards):
                sums = sums + sums_t[j, i]
        else:
            sums = sums_s[i]
        rms = jnp.sqrt(sums[0:1, :] / total_width + 1e-06)
        inv = 1.0 / rms
        mean = sums[1:2, :] * inv / total_width
        inv_c = jnp.broadcast_to(inv, (C, C)).T
        coef_c = jnp.broadcast_to(mean * inv * inv, (C, C)).T
        inv_c = jnp.concatenate([inv_c] * 3, axis=1)
        coef_c = jnp.concatenate([coef_c] * 3, axis=1)
        for g, lanes in enumerate(groups):
            att = att_s[rows, lanes]
            up = do_s[rows, lanes].astype(F32)
            gain = gain_ref[:, lanes]
            normed = att * inv_c
            out_ref[rows, lanes] = (normed * gain).astype(BF16)
            dg_s[:, lanes] += jnp.sum((up * normed).reshape(C // 8, 8, GL), axis=0)
            grad = up * gain * inv_c - att * coef_c
            g_hi, g_lo = split(grad)
            ghi_s[rows, lanes] = g_hi
            glo_s[rows, lanes] = g_lo
            cexp = cexp_s[rows, lanes]
            end = cexp[C - 1 : C, :]
            e_hi, e_lo = split(grad * jnp.exp2(cexp))
            ehi_s[rows, lanes] = e_hi
            elo_s[rows, lanes] = e_lo
            e_both = jnp.concatenate([e_hi, e_lo], axis=0)
            qt = q_s[rows, lanes].T
            parts = []
            for p in range(2):
                qp = qt[192 * p : 192 * p + 192]
                parts.append(compact(dot(jnp.concatenate([qp, qp], axis=1), e_both[:, window(p)]), p))
            w = merge(*parts)
            u_s[i, :, lanes] = w
            own_s[:, lanes] += jnp.exp2(start_s[0:1, lanes]) * w
            start_s[0:1, lanes] += end

    def grad_rows(i):
        rows = rows_of(i)
        ct = ct_of(i)
        cols = columns_of(ct)
        bias, bias_t = causal_bias(False), causal_bias(True)
        for g, lanes in enumerate(groups):
            q, k, v = q_s[rows, lanes], k_s[rows, lanes], v_s[rows, lanes]
            g_hi, g_lo = ghi_s[rows, lanes], glo_s[rows, lanes]
            e_hi, e_lo = ehi_s[rows, lanes], elo_s[rows, lanes]
            s_hi, s_lo = shi_s[i, :, lanes], slo_s[i, :, lanes]
            dqs, dks, dvs = [], [], []
            for p in range(2):
                w = window(p)
                heads = (4 * g + 2 * p, 4 * g + 2 * p + 1)
                qw, kw, vw, hw, lw = q[:, w], k[:, w], v[:, w], g_hi[:, w], g_lo[:, w]
                ks, qs, vs = stacked(kw, p), stacked(qw, p), stacked(vw, p)
                hs, ls = stacked(hw, p), stacked(lw, p)
                decay = pair_decay(ct, cols, heads, bias)
                decay_t = pair_decay_t(ct, cols, heads, bias_t)
                b_hi, b_lo = block_state(s_hi[:, w], p), block_state(s_lo[:, w], p)
                d_hi, d_lo = split(both_nt(hw, lw, vs) * decay)
                dqs.append(
                    both(d_hi, d_lo, ks)
                    + (both_nt(e_hi[:, w], e_lo[:, w], b_hi) + dot_nt(e_hi[:, w], b_lo))
                )
                t_hi, t_lo = split((dot_nt(vw, hs) + dot_nt(vw, ls)) * decay_t)
                dks.append(both(t_hi, t_lo, qs))
                p_hi, p_lo = split(dot_nt(kw, qs) * decay_t)
                dvs.append(both(p_hi, p_lo, hs) + dot(p_hi, ls))
            dq_ref[rows, lanes] = merge(*dqs).astype(BF16)
            dk_s[rows, lanes] = merge(*dks)
            dv_s[rows, lanes] = merge(*dvs)

    def last_rows(i):
        rows = rows_of(i)
        for g, lanes in enumerate(groups):
            k, v = k_s[rows, lanes], v_s[rows, lanes]
            cexp = cexp_s[rows, lanes]
            end = cexp[C - 1 : C, :]
            tail = jnp.exp2(end - cexp)
            s = run_s[:, lanes]
            s_hi, s_lo = split(s)
            dks, dvs = [], []
            for p in range(2):
                w = window(p)
                b_hi, b_lo = block_state(s_hi[:, w], p), block_state(s_lo[:, w], p)
                dks.append(dot_nt(v[:, w], b_hi) + dot_nt(v[:, w], b_lo))
                dvs.append(dot(k[:, w], b_hi) + dot(k[:, w], b_lo))
            dk_ref[rows, lanes] = (dk_s[rows, lanes] + tail * merge(*dks)).astype(BF16)
            dv_ref[rows, lanes] = (dv_s[rows, lanes] + tail * merge(*dvs)).astype(BF16)
            run_s[:, lanes] = jnp.exp2(end) * s + u_s[i, :, lanes]

    def over(lo, hi, f):
        pl.loop(lo, hi)(f)

    for b in range(PIECES):
        arrival(0, b).wait()
        arrival(1, b).wait()
        over(b * per, (b + 1) * per, states)
    if remote:
        pl.semaphore_wait(barrier, shards + head_shards - 2)
        on.start(own_s, tot_s)
    for b in range(PIECES):
        arrival(2, b).wait()
        arrival(3, b).wait()
    split_at = chunks // 2
    over(0, split_at, local_rows)
    if remote:
        on.middle()
    over(split_at, chunks, local_rows)
    if remote:
        on.finish(run_s)
    else:
        run_s[...] = jnp.zeros_like(run_s)
    for b in range(PIECES):
        over(b * per, (b + 1) * per, whole_rows)
        if remote:
            part = pl.ds(b * per, per)
            sums_t[my_head, part] = sums_s[part]

            @pl.loop(1, head_shards)
            def _(i):
                sums_copy(b, lax.rem(my_head + i, head_shards)).start()

    own_s[...] = jnp.zeros_like(own_s)
    start_s[...] = jnp.zeros_like(start_s)
    dg_s[...] = jnp.zeros_like(dg_s)
    for b in range(PIECES):
        if remote:
            moved = sums_t.at[pl.ds(0, head_shards - 1), pl.ds(b * per, per)]
            wait_bytes(moved, sums_sems.at[1, b])
            wait_bytes(moved, sums_sems.at[0, b])
        over(b * per, (b + 1) * per, norm_rows)

    sums = jnp.sum(dg_s[...], axis=0, keepdims=True)
    tile = jnp.concatenate(
        [sums[:, 128 * i : 128 * i + 128] for i in range(6)] + [jnp.zeros((2, 128), F32)], axis=0
    )
    if remote:
        back.start(own_s, tot_s)
        gsend[...] = tile
        gtaken[me] = tile

        @pl.loop(1, shards)
        def _(i):
            pltpu.make_async_remote_copy(
                src_ref=gsend, dst_ref=gtaken.at[me], send_sem=gsems.at[0], recv_sem=gsems.at[1],
                device_id={"ctx": lax.rem(me + i, shards)}, device_id_type=MESH,
            ).start()

    over(0, split_at, grad_rows)
    if remote:
        back.middle()
    over(split_at, chunks, grad_rows)
    if remote:
        wait_bytes(gtaken.at[pl.ds(0, shards - 1)], gsems.at[1])
        wait_bytes(gtaken.at[pl.ds(0, shards - 1)], gsems.at[0])
        dgain_ref[...] = lax.fori_loop(
            0, shards, lambda i, acc: acc + gtaken[i], jnp.zeros((8, 128), F32)
        )
        back.finish(run_s)
    else:
        dgain_ref[...] = tile
        run_s[...] = jnp.zeros_like(run_s)
    over(0, chunks, lambda i: last_rows(chunks - 1 - i))


def body(shards, head_shards, queries, keys, values, log_decay, gain, d_out):
    n, width = queries.shape
    chunks = n // C
    ld_t = log_decay.reshape(chunks, C, 8).transpose(0, 2, 1).reshape(chunks * 8, C)
    hbm, vmem = pl.BlockSpec(memory_space=pl.ANY), pl.BlockSpec(memory_space=pltpu.VMEM)
    rows = lambda dtype: pltpu.VMEM((n, width), dtype)
    scan = [
        pltpu.VMEM((OWNERS, 8, 512), F32),
        pltpu.VMEM((shards, 8, 512), F32),
        pltpu.VMEM((shards, 8, GL), F32),
        pltpu.VMEM((OWNERS, 8, GL), F32),
        pltpu.SemaphoreType.DMA((4,)),
    ]
    scratch = [rows(BF16)] * 4 + [
        pltpu.SemaphoreType.DMA((4, PIECES)),
        pltpu.VMEM((chunks * 8, C), F32),
        rows(F32),
        rows(F32),
        pltpu.VMEM((chunks, HS, width), F32),
        pltpu.VMEM((chunks, HS, width), BF16),
        pltpu.VMEM((chunks, HS, width), BF16),
        rows(BF16), rows(BF16), rows(BF16), rows(BF16),
        rows(F32),
        pltpu.VMEM((HS, width), F32),
        pltpu.VMEM((8, 128), F32),
        pltpu.VMEM((HS, width), F32),
        pltpu.VMEM((8, width), F32),
        pltpu.VMEM((8, width), F32),
        pltpu.VMEM((chunks, 8, C), F32),
        pltpu.VMEM((head_shards, chunks, 8, C), F32),
        pltpu.SemaphoreType.DMA((2, PIECES)),
        pltpu.VMEM((8, 128), F32),
        pltpu.VMEM((shards, 8, 128), F32),
        pltpu.SemaphoreType.DMA((2,)),
    ] + scan + scan
    params = dict(vmem_limit_bytes=VMEM_LIMIT)
    if shards > 1:
        params.update(collective_id=0, has_side_effects=True)
    out = OUT((n, width), BF16)
    outs = pl.pallas_call(
        functools.partial(
            layer_kernel, shards, head_shards, float(width * head_shards), chunks
        ),
        in_specs=[hbm] * 4 + [vmem, vmem],
        out_specs=[vmem] * 5,
        out_shape=[out] * 4 + [jax.ShapeDtypeStruct((8, 128), F32)],
        scratch_shapes=scratch,
        compiler_params=pltpu.CompilerParams(**params),
        name="layer",
    )(queries, keys, values, d_out, gain[None], ld_t)
    return (*outs[:4], outs[4][:6].reshape(width))


VMEM_LIMIT = 60 * 1024 * 1024
OUT = jax.ShapeDtypeStruct


def solution(mesh):
    rows = P("ctx", "head")
    return jax.shard_map(
        functools.partial(body, mesh.shape["ctx"], mesh.shape["head"]),
        mesh=mesh,
        in_specs=(rows, rows, rows, rows, P("head"), rows),
        out_specs=(rows, rows, rows, rows, P("head")),
        check_vma=False,
    )
```

```python
import functools

import jax
import jax.numpy as jnp
from jax import lax
from jax.experimental import pallas as pl
from jax.experimental.pallas import tpu as pltpu
from jax.sharding import PartitionSpec as P

F32 = jnp.float32
BF16 = jnp.bfloat16
C = 128
HS = 96
GL = 384
PIECES = 3
OWNERS = 24
NEG = -1e30
LOG2E = 1.4426950408889634
MESH = pl.DeviceIdType.MESH


def dot(a, b):
    return lax.dot_general(a, b, (((1,), (0,)), ((), ())), preferred_element_type=F32)


def dot_nt(a, b):
    return lax.dot_general(a, b, (((1,), (1,)), ((), ())), preferred_element_type=F32)


def both(hi, lo, w):
    r = dot(jnp.concatenate([hi, lo], axis=0), w)
    return r[: hi.shape[0]] + r[hi.shape[0] :]


def both_nt(hi, lo, w):
    r = dot_nt(jnp.concatenate([hi, lo], axis=0), w)
    return r[: hi.shape[0]] + r[hi.shape[0] :]


def split(x):
    hi = x.astype(BF16)
    lo = (x - hi.astype(F32)).astype(BF16)
    return hi, lo


def lane_mask(lo, hi, rows, dtype):
    lane = lax.broadcasted_iota(jnp.int32, (rows, 128), 1)
    return jnp.where((lane >= lo) & (lane < hi), 1.0, 0.0).astype(dtype)


def head_tiles(x, parity, dtype):
    rows = x.shape[0]
    t0, t1 = x[:, :128], x[:, 128:]
    zero = jnp.zeros((rows, 128), dtype)
    if parity == 0:
        a = [t0 * lane_mask(0, 96, rows, dtype), zero]
        b = [t0 * lane_mask(96, 128, rows, dtype), t1 * lane_mask(0, 64, rows, dtype)]
    else:
        a = [t0 * lane_mask(64, 128, rows, dtype), t1 * lane_mask(0, 32, rows, dtype)]
        b = [zero, t1 * lane_mask(32, 128, rows, dtype)]
    return jnp.concatenate(a, axis=1), jnp.concatenate(b, axis=1)


def stacked(x, parity):
    a, b = head_tiles(x, parity, x.dtype)
    return jnp.concatenate([a, b], axis=0)


def block_state(s, parity):
    a, b = head_tiles(s, parity, s.dtype)
    pad = jnp.zeros((64, 256), s.dtype)
    return jnp.concatenate([a, b, pad] if parity == 0 else [pad, a, b], axis=0)


def compact(u, parity):
    a, _ = head_tiles(u[:HS], parity, F32)
    _, b = head_tiles(u[HS:], parity, F32)
    return a + b


def merge(w0, w1):
    return jnp.concatenate([w0[:, :128], w0[:, 128:] + w1[:, :128], w1[:, 128:]], axis=1)


def group_lanes(cols):
    rows = cols[0].shape[0]
    lane = lax.broadcasted_iota(jnp.int32, (rows, 128), 1)
    return jnp.concatenate(
        [
            jnp.where(lane < 96, cols[0], cols[1]),
            jnp.where(lane < 64, cols[1], cols[2]),
            jnp.where(lane < 32, cols[2], cols[3]),
        ],
        axis=1,
    )


def columns_of(ct):
    full = jnp.concatenate([ct, jnp.zeros((C - 8, C), F32)], axis=0).T
    return [jnp.broadcast_to(full[:, h : h + 1], (C, C)) for h in range(8)]


def window(parity):
    return slice(128 * parity, 128 * parity + 256)


def causal_bias(transposed):
    row = lax.broadcasted_iota(jnp.int32, (C, C), 0)
    col = lax.broadcasted_iota(jnp.int32, (C, C), 1)
    keep = row <= col if transposed else row >= col
    return jnp.where(keep, 0.0, NEG)


def pair_decay(ct, cols, heads, bias):
    parts = [jnp.exp2(cols[h] - ct[h : h + 1, :] + bias) for h in heads]
    return jnp.concatenate(parts, axis=1)


def pair_decay_t(ct, cols, heads, bias):
    parts = [jnp.exp2(ct[h : h + 1, :] - cols[h] + bias) for h in heads]
    return jnp.concatenate(parts, axis=1)


def token_sums(x):
    acc = x[:, :128]
    for i in range(1, 6):
        acc = acc + x[:, 128 * i : 128 * i + 128]
    return jnp.sum(acc.T, axis=0, keepdims=True)


def wait_bytes(ref, sem):
    pltpu.make_async_copy(ref, ref, sem).wait()


def owner_of(device):
    return (device // 4) * 3 + jnp.minimum(lax.rem(device, 4), 2)


class Scan:
    def __init__(self, count, me, reverse, send, taken, made, given, sems):
        self.count, self.me, self.reverse = count, me, reverse
        self.send, self.taken, self.made, self.given, self.sems = send, taken, made, given, sems
        self.is_owner = lax.rem(me, 4) != 3
        self.mine = owner_of(me)

    def start(self, state_ref, tot_ref):
        for o in range(OWNERS):
            r, half = o // 2, o % 2
            self.send[o, :, :GL] = state_ref[8 * r : 8 * r + 8, GL * half : GL * half + GL]
            tot = tot_ref[4 * half : 4 * half + 4, :]
            self.send[o, :, GL:] = jnp.concatenate([tot, tot], axis=0)

        @pl.loop(1, self.count)
        def _(i):
            target = lax.rem(self.me + i, self.count)

            @pl.when(lax.rem(target, 4) != 3)
            def _():
                pltpu.make_async_remote_copy(
                    src_ref=self.send.at[owner_of(target)], dst_ref=self.taken.at[self.me],
                    send_sem=self.sems.at[0], recv_sem=self.sems.at[1],
                    device_id={"ctx": target}, device_id_type=MESH,
                ).start()

    def middle(self):
        count, me, mine = self.count, self.me, self.mine

        @pl.when(self.is_owner)
        def _():
            self.taken[me] = self.send[mine]
            wait_bytes(self.taken.at[pl.ds(0, count - 1)], self.sems.at[1])

            def step(i, acc):
                j = count - 1 - i if self.reverse else i
                self.made[j] = acc
                rows = [jnp.broadcast_to(self.taken[j, h : h + 1, GL:], (8, 128)) for h in range(4)]
                return jnp.exp2(group_lanes(rows)) * acc + self.taken[j, :, :GL]

            lax.fori_loop(0, count, step, jnp.zeros((8, GL), F32), unroll=4)

            @pl.loop(1, count)
            def _(i):
                target = lax.rem(me + i, count)
                pltpu.make_async_remote_copy(
                    src_ref=self.made.at[target], dst_ref=self.given.at[mine],
                    send_sem=self.sems.at[2], recv_sem=self.sems.at[3],
                    device_id={"ctx": target}, device_id_type=MESH,
                ).start()

            self.given[mine] = self.made[me]

    def finish(self, out_ref):
        @pl.when(self.is_owner)
        def _():
            wait_bytes(self.given.at[pl.ds(0, OWNERS - 1)], self.sems.at[3])
            wait_bytes(self.send.at[pl.ds(0, OWNERS - 1)], self.sems.at[0])
            wait_bytes(self.made.at[pl.ds(0, self.count - 1)], self.sems.at[2])

        @pl.when(jnp.logical_not(self.is_owner))
        def _():
            wait_bytes(self.given, self.sems.at[3])
            wait_bytes(self.send, self.sems.at[0])

        for o in range(OWNERS):
            r, half = o // 2, o % 2
            out_ref[8 * r : 8 * r + 8, GL * half : GL * half + GL] = self.given[o]


def rows_of(i):
    return pl.ds(pl.multiple_of(i * C, C), C)


groups = [slice(GL * g, GL * (g + 1)) for g in range(2)]


def layer_kernel(
    shards, head_shards, total_width, chunks, q_in, k_in, v_in, do_in, gain_in, ld_ref,
    out_ref, dq_ref, k_s, v_s, att_s, dv_s, u_s, cexp_s, run_s, dgain_ref,
    q_s, do_s, in_sems, ct_s, shi_s, slo_s, ghi_s, glo_s, ehi_s, elo_s,
    own_s, tot_s, start_s, dg_s, gain_ref, sums_s, sums_t, sums_sems,
    gsend, gtaken, gsems, *scan_refs,
):
    remote = shards > 1
    dk_s = att_s
    if remote:
        me, my_head = lax.axis_index("ctx"), lax.axis_index("head")
        on = Scan(shards, me, False, *scan_refs[:5])
        back = Scan(shards, me, True, *scan_refs[5:])
        barrier = pltpu.get_barrier_semaphore()

        @pl.loop(1, shards)
        def _(i):
            pl.semaphore_signal(
                barrier, inc=1, device_id={"ctx": lax.rem(me + i, shards)}, device_id_type=MESH
            )

        @pl.loop(1, head_shards)
        def _(i):
            pl.semaphore_signal(
                barrier, inc=1, device_id={"head": lax.rem(my_head + i, head_shards)},
                device_id_type=MESH,
            )

    per = chunks // PIECES
    inputs = [(k_in, k_s), (v_in, v_s), (q_in, q_s), (do_in, do_s)]

    def arrival(a, b):
        rows = pl.ds(b * per * C, per * C)
        return pltpu.make_async_copy(inputs[a][0].at[rows], inputs[a][1].at[rows], in_sems.at[a, b])

    for b in range(PIECES):
        arrival(0, b).start()
        arrival(1, b).start()
    for a in (2, 3):
        for b in range(PIECES):
            arrival(a, b).start()
    for j in range(gain_ref.shape[1] // 128):
        gain_ref[:, 128 * j : 128 * j + 128] = gain_in[128 * j : 128 * j + 128].reshape(1, 128)

    row = lax.broadcasted_iota(jnp.int32, (C, C), 0)
    col = lax.broadcasted_iota(jnp.int32, (C, C), 1)
    upper = jnp.where(row <= col, 1.0, 0.0)
    ct_s[...] = LOG2E * lax.dot_general(
        ld_ref[...], upper, (((1,), (0,)), ((), ())), preferred_element_type=F32,
        precision=lax.Precision.HIGHEST,
    )
    own_s[...] = jnp.zeros_like(own_s)
    tot_s[...] = jnp.zeros_like(tot_s)

    def ct_of(i):
        return ct_s[pl.ds(pl.multiple_of(i * 8, 8), 8), :]

    def states(i):
        rows = rows_of(i)
        ct = ct_of(i)
        tot_s[...] += jnp.broadcast_to(ct[:, C - 1 : C], (8, 128))
        cols = columns_of(ct)
        for g, lanes in enumerate(groups):
            cexp = group_lanes(cols[4 * g : 4 * g + 4])
            cexp_s[rows, lanes] = cexp
            end = cexp[C - 1 : C, :]
            v_hi, v_lo = split(v_s[rows, lanes].astype(F32) * jnp.exp2(end - cexp))
            v_tail = jnp.concatenate([v_hi, v_lo], axis=0)
            kt = k_s[rows, lanes].T
            parts = []
            for p in range(2):
                kp = kt[192 * p : 192 * p + 192]
                parts.append(compact(dot(jnp.concatenate([kp, kp], axis=1), v_tail[:, window(p)]), p))
            u = merge(*parts)
            u_s[i, :, lanes] = u
            own_s[:, lanes] = jnp.exp2(end) * own_s[:, lanes] + u

    def local_rows(i):
        rows = rows_of(i)
        ct = ct_of(i)
        cols = columns_of(ct)
        bias = causal_bias(False)
        for g, lanes in enumerate(groups):
            q, k, v = q_s[rows, lanes], k_s[rows, lanes], v_s[rows, lanes]
            outs = []
            for p in range(2):
                w = window(p)
                heads = (4 * g + 2 * p, 4 * g + 2 * p + 1)
                scores = dot_nt(q[:, w], stacked(k[:, w], p)) * pair_decay(ct, cols, heads, bias)
                hi, lo = split(scores)
                vs = stacked(v[:, w], p)
                outs.append(dot(hi, vs) + dot(lo, vs))
            att_s[rows, lanes] = merge(*outs)

    def whole_rows(i):
        rows = rows_of(i)
        for g, lanes in enumerate(groups):
            q = q_s[rows, lanes]
            cexp = cexp_s[rows, lanes]
            end = cexp[C - 1 : C, :]
            s = run_s[:, lanes]
            s_hi, s_lo = split(s)
            shi_s[i, :, lanes] = s_hi
            slo_s[i, :, lanes] = s_lo
            outs = []
            for p in range(2):
                w = window(p)
                outs.append(dot(q[:, w], block_state(s_hi[:, w], p)) + dot(q[:, w], block_state(s_lo[:, w], p)))
            att_s[rows, lanes] += jnp.exp2(cexp) * merge(*outs)
            run_s[:, lanes] = jnp.exp2(end) * s + u_s[i, :, lanes]
        att = att_s[rows, :]
        grown = do_s[rows, :].astype(F32) * gain_ref[...]
        sums_s[i] = jnp.concatenate(
            [token_sums(att * att), token_sums(grown * att), jnp.zeros((6, C), F32)], axis=0
        )

    def sums_copy(b, target):
        part = pl.ds(b * per, per)
        return pltpu.make_async_remote_copy(
            src_ref=sums_s.at[part], dst_ref=sums_t.at[my_head, part], send_sem=sums_sems.at[0, b],
            recv_sem=sums_sems.at[1, b], device_id={"head": target}, device_id_type=MESH,
        )

    def norm_rows(i):
        rows = rows_of(i)
        if remote:
            sums = sums_t[0, i]
            for j in range(1, head_shards):
                sums = sums + sums_t[j, i]
        else:
            sums = sums_s[i]
        rms = jnp.sqrt(sums[0:1, :] / total_width + 1e-06)
        inv = 1.0 / rms
        mean = sums[1:2, :] * inv / total_width
        inv_c = jnp.broadcast_to(inv, (C, C)).T
        coef_c = jnp.broadcast_to(mean * inv * inv, (C, C)).T
        inv_c = jnp.concatenate([inv_c] * 3, axis=1)
        coef_c = jnp.concatenate([coef_c] * 3, axis=1)
        for g, lanes in enumerate(groups):
            att = att_s[rows, lanes]
            up = do_s[rows, lanes].astype(F32)
            gain = gain_ref[:, lanes]
            normed = att * inv_c
            out_ref[rows, lanes] = (normed * gain).astype(BF16)
            dg_s[:, lanes] += jnp.sum((up * normed).reshape(C // 8, 8, GL), axis=0)
            grad = up * gain * inv_c - att * coef_c
            g_hi, g_lo = split(grad)
            ghi_s[rows, lanes] = g_hi
            glo_s[rows, lanes] = g_lo
            cexp = cexp_s[rows, lanes]
            end = cexp[C - 1 : C, :]
            e_hi, e_lo = split(grad * jnp.exp2(cexp))
            ehi_s[rows, lanes] = e_hi
            elo_s[rows, lanes] = e_lo
            e_both = jnp.concatenate([e_hi, e_lo], axis=0)
            qt = q_s[rows, lanes].T
            parts = []
            for p in range(2):
                qp = qt[192 * p : 192 * p + 192]
                parts.append(compact(dot(jnp.concatenate([qp, qp], axis=1), e_both[:, window(p)]), p))
            w = merge(*parts)
            u_s[i, :, lanes] = w
            own_s[:, lanes] += jnp.exp2(start_s[0:1, lanes]) * w
            start_s[0:1, lanes] += end

    def grad_rows(i):
        rows = rows_of(i)
        ct = ct_of(i)
        cols = columns_of(ct)
        bias, bias_t = causal_bias(False), causal_bias(True)
        for g, lanes in enumerate(groups):
            q, k, v = q_s[rows, lanes], k_s[rows, lanes], v_s[rows, lanes]
            g_hi, g_lo = ghi_s[rows, lanes], glo_s[rows, lanes]
            e_hi, e_lo = ehi_s[rows, lanes], elo_s[rows, lanes]
            s_hi, s_lo = shi_s[i, :, lanes], slo_s[i, :, lanes]
            dqs, dks, dvs = [], [], []
            for p in range(2):
                w = window(p)
                heads = (4 * g + 2 * p, 4 * g + 2 * p + 1)
                qw, kw, vw, hw, lw = q[:, w], k[:, w], v[:, w], g_hi[:, w], g_lo[:, w]
                ks, qs, vs = stacked(kw, p), stacked(qw, p), stacked(vw, p)
                hs, ls = stacked(hw, p), stacked(lw, p)
                decay = pair_decay(ct, cols, heads, bias)
                decay_t = pair_decay_t(ct, cols, heads, bias_t)
                b_hi, b_lo = block_state(s_hi[:, w], p), block_state(s_lo[:, w], p)
                d_hi, d_lo = split(both_nt(hw, lw, vs) * decay)
                dqs.append(
                    both(d_hi, d_lo, ks)
                    + (both_nt(e_hi[:, w], e_lo[:, w], b_hi) + dot_nt(e_hi[:, w], b_lo))
                )
                t_hi, t_lo = split((dot_nt(vw, hs) + dot_nt(vw, ls)) * decay_t)
                dks.append(both(t_hi, t_lo, qs))
                p_hi, p_lo = split(dot_nt(kw, qs) * decay_t)
                dvs.append(both(p_hi, p_lo, hs) + dot(p_hi, ls))
            dq_ref[rows, lanes] = merge(*dqs).astype(BF16)
            dk_s[rows, lanes] = merge(*dks)
            dv_s[rows, lanes] = merge(*dvs)

    def over(lo, hi, f):
        pl.loop(lo, hi)(f)

    for b in range(PIECES):
        arrival(0, b).wait()
        arrival(1, b).wait()
        over(b * per, (b + 1) * per, states)
    if remote:
        pl.semaphore_wait(barrier, shards + head_shards - 2)
        on.start(own_s, tot_s)
    for b in range(PIECES):
        arrival(2, b).wait()
        arrival(3, b).wait()
    split_at = chunks // 2
    over(0, split_at, local_rows)
    if remote:
        on.middle()
    over(split_at, chunks, local_rows)
    if remote:
        on.finish(run_s)
    else:
        run_s[...] = jnp.zeros_like(run_s)
    for b in range(PIECES):
        over(b * per, (b + 1) * per, whole_rows)
        if remote:
            part = pl.ds(b * per, per)
            sums_t[my_head, part] = sums_s[part]

            @pl.loop(1, head_shards)
            def _(i):
                sums_copy(b, lax.rem(my_head + i, head_shards)).start()

    own_s[...] = jnp.zeros_like(own_s)
    start_s[...] = jnp.zeros_like(start_s)
    dg_s[...] = jnp.zeros_like(dg_s)
    for b in range(PIECES):
        if remote:
            moved = sums_t.at[pl.ds(0, head_shards - 1), pl.ds(b * per, per)]
            wait_bytes(moved, sums_sems.at[1, b])
            wait_bytes(moved, sums_sems.at[0, b])
        over(b * per, (b + 1) * per, norm_rows)

    sums = jnp.sum(dg_s[...], axis=0, keepdims=True)
    tile = jnp.concatenate(
        [sums[:, 128 * i : 128 * i + 128] for i in range(6)] + [jnp.zeros((2, 128), F32)], axis=0
    )
    if remote:
        back.start(own_s, tot_s)
        gsend[...] = tile
        gtaken[me] = tile

        @pl.loop(1, shards)
        def _(i):
            pltpu.make_async_remote_copy(
                src_ref=gsend, dst_ref=gtaken.at[me], send_sem=gsems.at[0], recv_sem=gsems.at[1],
                device_id={"ctx": lax.rem(me + i, shards)}, device_id_type=MESH,
            ).start()

    over(0, split_at, grad_rows)
    if remote:
        back.middle()
    over(split_at, chunks, grad_rows)
    if remote:
        wait_bytes(gtaken.at[pl.ds(0, shards - 1)], gsems.at[1])
        wait_bytes(gtaken.at[pl.ds(0, shards - 1)], gsems.at[0])
        dgain_ref[...] = lax.fori_loop(
            0, shards, lambda i, acc: acc + gtaken[i], jnp.zeros((8, 128), F32)
        )
        back.finish(run_s)
    else:
        dgain_ref[...] = tile
        run_s[...] = jnp.zeros_like(run_s)


def last_kernel(
    chunks, out_v, dq_v, k_s, v_s, dk_s, dv_s, u_s, cexp_s, state_ref, dgain_v,
    out_hbm, dq_hbm, dk_hbm, dv_hbm, dgain_ref, dk_ref, dv_ref, run_s, sems,
):
    first = [(out_v, out_hbm), (dq_v, dq_hbm)]
    for j, (src, dst) in enumerate(first):
        pltpu.make_async_copy(src, dst, sems.at[j, 0]).start()
    for j in range(dgain_ref.shape[0] // 128):
        dgain_ref[128 * j : 128 * j + 128] = dgain_v[j : j + 1, :].reshape(128)
    run_s[...] = state_ref[...]

    def copies(i):
        rows = rows_of(i)
        return [
            pltpu.make_async_copy(src.at[rows], dst.at[rows], sems.at[2 + j, i])
            for j, (src, dst) in enumerate([(dk_ref, dk_hbm), (dv_ref, dv_hbm)])
        ]

    def last_rows(i):
        rows = rows_of(i)
        for g, lanes in enumerate(groups):
            k, v = k_s[rows, lanes], v_s[rows, lanes]
            cexp = cexp_s[rows, lanes]
            end = cexp[C - 1 : C, :]
            tail = jnp.exp2(end - cexp)
            s = run_s[:, lanes]
            s_hi, s_lo = split(s)
            dks, dvs = [], []
            for p in range(2):
                w = window(p)
                b_hi, b_lo = block_state(s_hi[:, w], p), block_state(s_lo[:, w], p)
                dks.append(dot_nt(v[:, w], b_hi) + dot_nt(v[:, w], b_lo))
                dvs.append(dot(k[:, w], b_hi) + dot(k[:, w], b_lo))
            dk_ref[rows, lanes] = (dk_s[rows, lanes] + tail * merge(*dks)).astype(BF16)
            dv_ref[rows, lanes] = (dv_s[rows, lanes] + tail * merge(*dvs)).astype(BF16)
            run_s[:, lanes] = jnp.exp2(end) * s + u_s[i, :, lanes]
        for copy in copies(i):
            copy.start()

    pl.loop(0, chunks)(lambda i: last_rows(chunks - 1 - i))
    for j, (src, dst) in enumerate(first):
        pltpu.make_async_copy(src, dst, sems.at[j, 0]).wait()

    @pl.loop(0, chunks)
    def _(i):
        for copy in copies(i):
            copy.wait()


def body(shards, head_shards, queries, keys, values, log_decay, gain, d_out):
    n, width = queries.shape
    chunks = n // C
    ld_t = log_decay.reshape(chunks, C, 8).transpose(0, 2, 1).reshape(chunks * 8, C)
    hbm, vmem = pl.BlockSpec(memory_space=pl.ANY), pl.BlockSpec(memory_space=pltpu.VMEM)
    rows = lambda dtype: pltpu.VMEM((n, width), dtype)
    scan = [
        pltpu.VMEM((OWNERS, 8, 512), F32),
        pltpu.VMEM((shards, 8, 512), F32),
        pltpu.VMEM((shards, 8, GL), F32),
        pltpu.VMEM((OWNERS, 8, GL), F32),
        pltpu.SemaphoreType.DMA((4,)),
    ]
    scratch = [
        rows(BF16), rows(BF16),
        pltpu.SemaphoreType.DMA((4, PIECES)),
        pltpu.VMEM((chunks * 8, C), F32),
        pltpu.VMEM((chunks, HS, width), BF16),
        pltpu.VMEM((chunks, HS, width), BF16),
        rows(BF16), rows(BF16), rows(BF16), rows(BF16),
        pltpu.VMEM((HS, width), F32),
        pltpu.VMEM((8, 128), F32),
        pltpu.VMEM((8, width), F32),
        pltpu.VMEM((8, width), F32),
        pltpu.VMEM((1, width), F32),
        pltpu.VMEM((chunks, 8, C), F32),
        pltpu.VMEM((head_shards, chunks, 8, C), F32),
        pltpu.SemaphoreType.DMA((2, PIECES)),
        pltpu.VMEM((8, 128), F32),
        pltpu.VMEM((shards, 8, 128), F32),
        pltpu.SemaphoreType.DMA((2,)),
    ] + scan + scan
    params = dict(vmem_limit_bytes=VMEM_LIMIT)
    if shards > 1:
        params.update(collective_id=0, has_side_effects=True)
    held = [rows(BF16)] * 4 + [
        rows(F32), rows(F32), pltpu.VMEM((chunks, HS, width), F32), rows(F32),
        pltpu.VMEM((HS, width), F32), pltpu.VMEM((8, 128), F32),
    ]
    held = pl.pallas_call(
        functools.partial(
            layer_kernel, shards, head_shards, float(width * head_shards), chunks
        ),
        in_specs=[hbm] * 4 + [vmem, vmem],
        out_specs=[vmem] * len(held),
        out_shape=held,
        scratch_shapes=scratch,
        compiler_params=pltpu.CompilerParams(**params),
        name="layer",
    )(queries, keys, values, d_out, gain, ld_t)
    out = jax.ShapeDtypeStruct((n, width), BF16)
    return pl.pallas_call(
        functools.partial(last_kernel, chunks),
        in_specs=[vmem] * len(held),
        out_specs=[hbm] * 4 + [vmem],
        out_shape=[out] * 4 + [jax.ShapeDtypeStruct((width,), F32)],
        scratch_shapes=[
            rows(BF16), rows(BF16), pltpu.VMEM((HS, width), F32), pltpu.SemaphoreType.DMA((4, chunks))
        ],
        compiler_params=pltpu.CompilerParams(vmem_limit_bytes=LAST_LIMIT),
        name="last",
    )(*held)


VMEM_LIMIT = 30 * 1024 * 1024
LAST_LIMIT = 12 * 1024 * 1024


def solution(mesh):
    rows = P("ctx", "head")
    return jax.shard_map(
        functools.partial(body, mesh.shape["ctx"], mesh.shape["head"]),
        mesh=mesh,
        in_specs=(rows, rows, rows, rows, P("head"), rows),
        out_specs=(rows, rows, rows, rows, P("head")),
        check_vma=False,
    )
```

```python
import functools

import jax
import jax.numpy as jnp
from jax import lax
from jax.experimental import pallas as pl
from jax.experimental.pallas import tpu as pltpu
from jax.sharding import PartitionSpec as P

F32 = jnp.float32
BF16 = jnp.bfloat16
C = 128
HS = 96
GL = 384
PIECES = 3
OWNERS = 24
NEG = -1e30
LOG2E = 1.4426950408889634
MESH = pl.DeviceIdType.MESH


def dot(a, b):
    return lax.dot_general(a, b, (((1,), (0,)), ((), ())), preferred_element_type=F32)


def dot_nt(a, b):
    return lax.dot_general(a, b, (((1,), (1,)), ((), ())), preferred_element_type=F32)


def both(hi, lo, w):
    r = dot(jnp.concatenate([hi, lo], axis=0), w)
    return r[: hi.shape[0]] + r[hi.shape[0] :]


def both_nt(hi, lo, w):
    r = dot_nt(jnp.concatenate([hi, lo], axis=0), w)
    return r[: hi.shape[0]] + r[hi.shape[0] :]


def split(x):
    hi = x.astype(BF16)
    lo = (x - hi.astype(F32)).astype(BF16)
    return hi, lo


def lane_mask(lo, hi, rows, dtype):
    lane = lax.broadcasted_iota(jnp.int32, (rows, 128), 1)
    return jnp.where((lane >= lo) & (lane < hi), 1.0, 0.0).astype(dtype)


def head_tiles(x, parity, dtype):
    rows = x.shape[0]
    t0, t1 = x[:, :128], x[:, 128:]
    zero = jnp.zeros((rows, 128), dtype)
    if parity == 0:
        a = [t0 * lane_mask(0, 96, rows, dtype), zero]
        b = [t0 * lane_mask(96, 128, rows, dtype), t1 * lane_mask(0, 64, rows, dtype)]
    else:
        a = [t0 * lane_mask(64, 128, rows, dtype), t1 * lane_mask(0, 32, rows, dtype)]
        b = [zero, t1 * lane_mask(32, 128, rows, dtype)]
    return jnp.concatenate(a, axis=1), jnp.concatenate(b, axis=1)


def stacked(x, parity):
    a, b = head_tiles(x, parity, x.dtype)
    return jnp.concatenate([a, b], axis=0)


def block_state(s, parity):
    a, b = head_tiles(s, parity, s.dtype)
    pad = jnp.zeros((64, 256), s.dtype)
    return jnp.concatenate([a, b, pad] if parity == 0 else [pad, a, b], axis=0)


def compact(u, parity):
    a, _ = head_tiles(u[:HS], parity, F32)
    _, b = head_tiles(u[HS:], parity, F32)
    return a + b


def merge(w0, w1):
    return jnp.concatenate([w0[:, :128], w0[:, 128:] + w1[:, :128], w1[:, 128:]], axis=1)


def group_lanes(cols):
    rows = cols[0].shape[0]
    lane = lax.broadcasted_iota(jnp.int32, (rows, 128), 1)
    return jnp.concatenate(
        [
            jnp.where(lane < 96, cols[0], cols[1]),
            jnp.where(lane < 64, cols[1], cols[2]),
            jnp.where(lane < 32, cols[2], cols[3]),
        ],
        axis=1,
    )


def columns_of(ct):
    full = jnp.concatenate([ct, jnp.zeros((C - 8, C), F32)], axis=0).T
    return [jnp.broadcast_to(full[:, h : h + 1], (C, C)) for h in range(8)]


def window(parity):
    return slice(128 * parity, 128 * parity + 256)


def causal_bias():
    row = lax.broadcasted_iota(jnp.int32, (C, C), 0)
    col = lax.broadcasted_iota(jnp.int32, (C, C), 1)
    return jnp.where(row >= col, 0.0, NEG)


def pair_decay(ct, cols, heads, bias):
    parts = [jnp.exp2(cols[h] - ct[h : h + 1, :] + bias) for h in heads]
    return jnp.concatenate(parts, axis=1)


def turned(x):
    return jnp.concatenate([x[:, :C].T, x[:, C:].T], axis=1)


def token_sums(x):
    acc = x[:, :128]
    for i in range(1, 6):
        acc = acc + x[:, 128 * i : 128 * i + 128]
    return jnp.sum(acc.T, axis=0, keepdims=True)


def wait_bytes(ref, sem):
    pltpu.make_async_copy(ref, ref, sem).wait()


def owner_of(device):
    return (device // 4) * 3 + jnp.minimum(lax.rem(device, 4), 2)


class Scan:
    def __init__(self, count, me, reverse, send, taken, made, given, sems):
        self.count, self.me, self.reverse = count, me, reverse
        self.send, self.taken, self.made, self.given, self.sems = send, taken, made, given, sems
        self.is_owner = lax.rem(me, 4) != 3
        self.mine = owner_of(me)

    def start(self, state_ref, tot_ref):
        for o in range(OWNERS):
            r, half = o // 2, o % 2
            self.send[o, :, :GL] = state_ref[8 * r : 8 * r + 8, GL * half : GL * half + GL]
            tot = tot_ref[4 * half : 4 * half + 4, :]
            self.send[o, :, GL:] = jnp.concatenate([tot, tot], axis=0)

        @pl.loop(1, self.count)
        def _(i):
            target = lax.rem(self.me + i, self.count)

            @pl.when(lax.rem(target, 4) != 3)
            def _():
                pltpu.make_async_remote_copy(
                    src_ref=self.send.at[owner_of(target)], dst_ref=self.taken.at[self.me],
                    send_sem=self.sems.at[0], recv_sem=self.sems.at[1],
                    device_id={"ctx": target}, device_id_type=MESH,
                ).start()

    def middle(self):
        count, me, mine = self.count, self.me, self.mine

        @pl.when(self.is_owner)
        def _():
            self.taken[me] = self.send[mine]
            wait_bytes(self.taken.at[pl.ds(0, count - 1)], self.sems.at[1])

            def step(i, acc):
                j = count - 1 - i if self.reverse else i
                self.made[j] = acc
                rows = [jnp.broadcast_to(self.taken[j, h : h + 1, GL:], (8, 128)) for h in range(4)]
                return jnp.exp2(group_lanes(rows)) * acc + self.taken[j, :, :GL]

            lax.fori_loop(0, count, step, jnp.zeros((8, GL), F32), unroll=4)

            @pl.loop(1, count)
            def _(i):
                target = lax.rem(me + i, count)
                pltpu.make_async_remote_copy(
                    src_ref=self.made.at[target], dst_ref=self.given.at[mine],
                    send_sem=self.sems.at[2], recv_sem=self.sems.at[3],
                    device_id={"ctx": target}, device_id_type=MESH,
                ).start()

            self.given[mine] = self.made[me]

    def finish(self, out_ref):
        @pl.when(self.is_owner)
        def _():
            wait_bytes(self.given.at[pl.ds(0, OWNERS - 1)], self.sems.at[3])
            wait_bytes(self.send.at[pl.ds(0, OWNERS - 1)], self.sems.at[0])
            wait_bytes(self.made.at[pl.ds(0, self.count - 1)], self.sems.at[2])

        @pl.when(jnp.logical_not(self.is_owner))
        def _():
            wait_bytes(self.given, self.sems.at[3])
            wait_bytes(self.send, self.sems.at[0])

        for o in range(OWNERS):
            r, half = o // 2, o % 2
            out_ref[8 * r : 8 * r + 8, GL * half : GL * half + GL] = self.given[o]


def rows_of(i):
    return pl.ds(pl.multiple_of(i * C, C), C)


groups = [slice(GL * g, GL * (g + 1)) for g in range(2)]


def layer_kernel(
    shards, head_shards, total_width, chunks, q_in, k_in, v_in, do_in, gain_in, ld_ref,
    out_ref, dq_ref, k_s, v_s, att_s, dv_s, u_s, cexp_s, run_s, dgain_ref,
    q_s, do_s, in_sems, ct_s, shi_s, slo_s, ghi_s, glo_s, phi_s, plo_s,
    own_s, tot_s, start_s, dg_s, gain_ref, sums_s, sums_t, sums_sems,
    gsend, gtaken, gsems, *scan_refs,
):
    remote = shards > 1
    dk_s = att_s
    if remote:
        me, my_head = lax.axis_index("ctx"), lax.axis_index("head")
        on = Scan(shards, me, False, *scan_refs[:5])
        back = Scan(shards, me, True, *scan_refs[5:])
        barrier = pltpu.get_barrier_semaphore()

        @pl.loop(1, shards)
        def _(i):
            pl.semaphore_signal(
                barrier, inc=1, device_id={"ctx": lax.rem(me + i, shards)}, device_id_type=MESH
            )

        @pl.loop(1, head_shards)
        def _(i):
            pl.semaphore_signal(
                barrier, inc=1, device_id={"head": lax.rem(my_head + i, head_shards)},
                device_id_type=MESH,
            )

    per = chunks // PIECES
    inputs = [(k_in, k_s), (v_in, v_s), (q_in, q_s), (do_in, do_s)]

    def arrival(a, b):
        rows = pl.ds(b * per * C, per * C)
        return pltpu.make_async_copy(inputs[a][0].at[rows], inputs[a][1].at[rows], in_sems.at[a, b])

    for b in range(PIECES):
        arrival(0, b).start()
        arrival(1, b).start()
    for a in (2, 3):
        for b in range(PIECES):
            arrival(a, b).start()
    for j in range(gain_ref.shape[1] // 128):
        gain_ref[:, 128 * j : 128 * j + 128] = gain_in[128 * j : 128 * j + 128].reshape(1, 128)

    row = lax.broadcasted_iota(jnp.int32, (C, C), 0)
    col = lax.broadcasted_iota(jnp.int32, (C, C), 1)
    upper = jnp.where(row <= col, 1.0, 0.0)
    ct_s[...] = LOG2E * lax.dot_general(
        ld_ref[...], upper, (((1,), (0,)), ((), ())), preferred_element_type=F32,
        precision=lax.Precision.HIGHEST,
    )
    own_s[...] = jnp.zeros_like(own_s)
    tot_s[...] = jnp.zeros_like(tot_s)

    def ct_of(i):
        return ct_s[pl.ds(pl.multiple_of(i * 8, 8), 8), :]

    def states(i):
        rows = rows_of(i)
        ct = ct_of(i)
        tot_s[...] += jnp.broadcast_to(ct[:, C - 1 : C], (8, 128))
        cols = columns_of(ct)
        for g, lanes in enumerate(groups):
            cexp = group_lanes(cols[4 * g : 4 * g + 4])
            cexp_s[rows, lanes] = cexp
            end = cexp[C - 1 : C, :]
            v_hi, v_lo = split(v_s[rows, lanes].astype(F32) * jnp.exp2(end - cexp))
            v_tail = jnp.concatenate([v_hi, v_lo], axis=0)
            kt = k_s[rows, lanes].T
            parts = []
            for p in range(2):
                kp = kt[192 * p : 192 * p + 192]
                parts.append(compact(dot(jnp.concatenate([kp, kp], axis=1), v_tail[:, window(p)]), p))
            u = merge(*parts)
            u_s[i, :, lanes] = u
            own_s[:, lanes] = jnp.exp2(end) * own_s[:, lanes] + u

    def local_rows(i):
        rows = rows_of(i)
        ct = ct_of(i)
        cols = columns_of(ct)
        bias = causal_bias()
        for g, lanes in enumerate(groups):
            q, k, v = q_s[rows, lanes], k_s[rows, lanes], v_s[rows, lanes]
            outs = []
            for p in range(2):
                w = window(p)
                heads = (4 * g + 2 * p, 4 * g + 2 * p + 1)
                scores = dot_nt(q[:, w], stacked(k[:, w], p)) * pair_decay(ct, cols, heads, bias)
                hi, lo = split(scores)
                vs = stacked(v[:, w], p)
                outs.append(dot(hi, vs) + dot(lo, vs))
                pair = slice(256 * (2 * g + p), 256 * (2 * g + p) + 256)
                phi_s[rows, pair] = turned(hi)
                plo_s[rows, pair] = turned(lo)
            att_s[rows, lanes] = merge(*outs)

    def whole_rows(i):
        rows = rows_of(i)
        for g, lanes in enumerate(groups):
            q = q_s[rows, lanes]
            cexp = cexp_s[rows, lanes]
            end = cexp[C - 1 : C, :]
            s = run_s[:, lanes]
            s_hi, s_lo = split(s)
            shi_s[i, :, lanes] = s_hi
            slo_s[i, :, lanes] = s_lo
            outs = []
            for p in range(2):
                w = window(p)
                outs.append(dot(q[:, w], block_state(s_hi[:, w], p)) + dot(q[:, w], block_state(s_lo[:, w], p)))
            att_s[rows, lanes] += jnp.exp2(cexp) * merge(*outs)
            run_s[:, lanes] = jnp.exp2(end) * s + u_s[i, :, lanes]
        att = att_s[rows, :]
        grown = do_s[rows, :].astype(F32) * gain_ref[...]
        sums_s[i] = jnp.concatenate(
            [token_sums(att * att), token_sums(grown * att), jnp.zeros((6, C), F32)], axis=0
        )

    def sums_copy(b, target):
        part = pl.ds(b * per, per)
        return pltpu.make_async_remote_copy(
            src_ref=sums_s.at[part], dst_ref=sums_t.at[my_head, part], send_sem=sums_sems.at[0, b],
            recv_sem=sums_sems.at[1, b], device_id={"head": target}, device_id_type=MESH,
        )

    def norm_rows(i):
        rows = rows_of(i)
        if remote:
            sums = sums_t[0, i]
            for j in range(1, head_shards):
                sums = sums + sums_t[j, i]
        else:
            sums = sums_s[i]
        rms = jnp.sqrt(sums[0:1, :] / total_width + 1e-06)
        inv = 1.0 / rms
        mean = sums[1:2, :] * inv / total_width
        inv_c = jnp.broadcast_to(inv, (C, C)).T
        coef_c = jnp.broadcast_to(mean * inv * inv, (C, C)).T
        inv_c = jnp.concatenate([inv_c] * 3, axis=1)
        coef_c = jnp.concatenate([coef_c] * 3, axis=1)
        for g, lanes in enumerate(groups):
            att = att_s[rows, lanes]
            up = do_s[rows, lanes].astype(F32)
            gain = gain_ref[:, lanes]
            normed = att * inv_c
            out_ref[rows, lanes] = (normed * gain).astype(BF16)
            dg_s[:, lanes] += jnp.sum((up * normed).reshape(C // 8, 8, GL), axis=0)
            grad = up * gain * inv_c - att * coef_c
            g_hi, g_lo = split(grad)
            ghi_s[rows, lanes] = g_hi
            glo_s[rows, lanes] = g_lo
            cexp = cexp_s[rows, lanes]
            end = cexp[C - 1 : C, :]
            e_hi, e_lo = split(grad * jnp.exp2(cexp))
            e_both = jnp.concatenate([e_hi, e_lo], axis=0)
            qt = q_s[rows, lanes].T
            parts = []
            for p in range(2):
                qp = qt[192 * p : 192 * p + 192]
                parts.append(compact(dot(jnp.concatenate([qp, qp], axis=1), e_both[:, window(p)]), p))
            w = merge(*parts)
            u_s[i, :, lanes] = w
            own_s[:, lanes] += jnp.exp2(start_s[0:1, lanes]) * w
            start_s[0:1, lanes] += end

    def grad_rows(i):
        rows = rows_of(i)
        ct = ct_of(i)
        cols = columns_of(ct)
        bias = causal_bias()
        for g, lanes in enumerate(groups):
            q, k, v = q_s[rows, lanes], k_s[rows, lanes], v_s[rows, lanes]
            g_hi, g_lo = ghi_s[rows, lanes], glo_s[rows, lanes]
            from_start = jnp.exp2(cexp_s[rows, lanes])
            s_hi, s_lo = shi_s[i, :, lanes], slo_s[i, :, lanes]
            dqs, olds, dks, dvs = [], [], [], []
            for p in range(2):
                w = window(p)
                heads = (4 * g + 2 * p, 4 * g + 2 * p + 1)
                pair = slice(256 * (2 * g + p), 256 * (2 * g + p) + 256)
                hw, lw = g_hi[:, w], g_lo[:, w]
                hs, ls = stacked(hw, p), stacked(lw, p)
                decay = pair_decay(ct, cols, heads, bias)
                b_hi, b_lo = block_state(s_hi[:, w], p), block_state(s_lo[:, w], p)
                d_hi, d_lo = split(both_nt(hw, lw, stacked(v[:, w], p)) * decay)
                ks = stacked(k[:, w], p)
                dqs.append(dot(d_hi, ks) + dot(d_lo, ks))
                olds.append(both_nt(hw, lw, b_hi) + dot_nt(hw, b_lo))
                dks.append(both(turned(d_hi), turned(d_lo), stacked(q[:, w], p)))
                p_hi, p_lo = phi_s[rows, pair], plo_s[rows, pair]
                dvs.append(both(p_hi, p_lo, hs) + dot(p_hi, ls))
            dq_ref[rows, lanes] = (merge(*dqs) + from_start * merge(*olds)).astype(BF16)
            dk_s[rows, lanes] = merge(*dks)
            dv_s[rows, lanes] = merge(*dvs)

    def over(lo, hi, f):
        pl.loop(lo, hi)(f)

    for b in range(PIECES):
        arrival(0, b).wait()
        arrival(1, b).wait()
        over(b * per, (b + 1) * per, states)
    if remote:
        pl.semaphore_wait(barrier, shards + head_shards - 2)
        on.start(own_s, tot_s)
    for b in range(PIECES):
        arrival(2, b).wait()
        arrival(3, b).wait()
    split_at = chunks // 2
    over(0, split_at, local_rows)
    if remote:
        on.middle()
    over(split_at, chunks, local_rows)
    if remote:
        on.finish(run_s)
    else:
        run_s[...] = jnp.zeros_like(run_s)
    for b in range(PIECES):
        over(b * per, (b + 1) * per, whole_rows)
        if remote:
            part = pl.ds(b * per, per)
            sums_t[my_head, part] = sums_s[part]

            @pl.loop(1, head_shards)
            def _(i):
                sums_copy(b, lax.rem(my_head + i, head_shards)).start()

    own_s[...] = jnp.zeros_like(own_s)
    start_s[...] = jnp.zeros_like(start_s)
    dg_s[...] = jnp.zeros_like(dg_s)
    for b in range(PIECES):
        if remote:
            moved = sums_t.at[pl.ds(0, head_shards - 1), pl.ds(b * per, per)]
            wait_bytes(moved, sums_sems.at[1, b])
            wait_bytes(moved, sums_sems.at[0, b])
        over(b * per, (b + 1) * per, norm_rows)

    sums = jnp.sum(dg_s[...], axis=0, keepdims=True)
    tile = jnp.concatenate(
        [sums[:, 128 * i : 128 * i + 128] for i in range(6)] + [jnp.zeros((2, 128), F32)], axis=0
    )
    if remote:
        back.start(own_s, tot_s)
        gsend[...] = tile
        gtaken[me] = tile

        @pl.loop(1, shards)
        def _(i):
            pltpu.make_async_remote_copy(
                src_ref=gsend, dst_ref=gtaken.at[me], send_sem=gsems.at[0], recv_sem=gsems.at[1],
                device_id={"ctx": lax.rem(me + i, shards)}, device_id_type=MESH,
            ).start()

    over(0, split_at, grad_rows)
    if remote:
        back.middle()
    over(split_at, chunks, grad_rows)
    if remote:
        wait_bytes(gtaken.at[pl.ds(0, shards - 1)], gsems.at[1])
        wait_bytes(gtaken.at[pl.ds(0, shards - 1)], gsems.at[0])
        dgain_ref[...] = lax.fori_loop(
            0, shards, lambda i, acc: acc + gtaken[i], jnp.zeros((8, 128), F32)
        )
        back.finish(run_s)
    else:
        dgain_ref[...] = tile
        run_s[...] = jnp.zeros_like(run_s)


def last_kernel(
    chunks, out_v, dq_v, k_s, v_s, dk_s, dv_s, u_s, cexp_s, state_ref, dgain_v,
    out_hbm, dq_hbm, dk_hbm, dv_hbm, dgain_ref, dk_ref, dv_ref, run_s, sems,
):
    first = [(out_v, out_hbm), (dq_v, dq_hbm)]
    for j, (src, dst) in enumerate(first):
        pltpu.make_async_copy(src, dst, sems.at[j, 0]).start()
    for j in range(dgain_ref.shape[0] // 128):
        dgain_ref[128 * j : 128 * j + 128] = dgain_v[j : j + 1, :].reshape(128)
    run_s[...] = state_ref[...]

    def copies(i):
        rows = rows_of(i)
        return [
            pltpu.make_async_copy(src.at[rows], dst.at[rows], sems.at[2 + j, i])
            for j, (src, dst) in enumerate([(dk_ref, dk_hbm), (dv_ref, dv_hbm)])
        ]

    def last_rows(i):
        rows = rows_of(i)
        for g, lanes in enumerate(groups):
            k, v = k_s[rows, lanes], v_s[rows, lanes]
            cexp = cexp_s[rows, lanes]
            end = cexp[C - 1 : C, :]
            tail = jnp.exp2(end - cexp)
            s = run_s[:, lanes]
            s_hi, s_lo = split(s)
            dks, dvs = [], []
            for p in range(2):
                w = window(p)
                b_hi, b_lo = block_state(s_hi[:, w], p), block_state(s_lo[:, w], p)
                dks.append(dot_nt(v[:, w], b_hi) + dot_nt(v[:, w], b_lo))
                dvs.append(dot(k[:, w], b_hi) + dot(k[:, w], b_lo))
            dk_ref[rows, lanes] = (dk_s[rows, lanes] + tail * merge(*dks)).astype(BF16)
            dv_ref[rows, lanes] = (dv_s[rows, lanes] + tail * merge(*dvs)).astype(BF16)
            run_s[:, lanes] = jnp.exp2(end) * s + u_s[i, :, lanes]
        for copy in copies(i):
            copy.start()

    pl.loop(0, chunks)(lambda i: last_rows(chunks - 1 - i))
    for j, (src, dst) in enumerate(first):
        pltpu.make_async_copy(src, dst, sems.at[j, 0]).wait()

    @pl.loop(0, chunks)
    def _(i):
        for copy in copies(i):
            copy.wait()


def body(shards, head_shards, queries, keys, values, log_decay, gain, d_out):
    n, width = queries.shape
    chunks = n // C
    ld_t = log_decay.reshape(chunks, C, 8).transpose(0, 2, 1).reshape(chunks * 8, C)
    hbm, vmem = pl.BlockSpec(memory_space=pl.ANY), pl.BlockSpec(memory_space=pltpu.VMEM)
    rows = lambda dtype: pltpu.VMEM((n, width), dtype)
    scan = [
        pltpu.VMEM((OWNERS, 8, 512), F32),
        pltpu.VMEM((shards, 8, 512), F32),
        pltpu.VMEM((shards, 8, GL), F32),
        pltpu.VMEM((OWNERS, 8, GL), F32),
        pltpu.SemaphoreType.DMA((4,)),
    ]
    scratch = [
        rows(BF16), rows(BF16),
        pltpu.SemaphoreType.DMA((4, PIECES)),
        pltpu.VMEM((chunks * 8, C), F32),
        pltpu.VMEM((chunks, HS, width), BF16),
        pltpu.VMEM((chunks, HS, width), BF16),
        rows(BF16), rows(BF16),
        pltpu.VMEM((n, 1024), BF16), pltpu.VMEM((n, 1024), BF16),
        pltpu.VMEM((HS, width), F32),
        pltpu.VMEM((8, 128), F32),
        pltpu.VMEM((8, width), F32),
        pltpu.VMEM((8, width), F32),
        pltpu.VMEM((1, width), F32),
        pltpu.VMEM((chunks, 8, C), F32),
        pltpu.VMEM((head_shards, chunks, 8, C), F32),
        pltpu.SemaphoreType.DMA((2, PIECES)),
        pltpu.VMEM((8, 128), F32),
        pltpu.VMEM((shards, 8, 128), F32),
        pltpu.SemaphoreType.DMA((2,)),
    ] + scan + scan
    params = dict(vmem_limit_bytes=VMEM_LIMIT)
    if shards > 1:
        params.update(collective_id=0, has_side_effects=True)
    held = [rows(BF16)] * 4 + [
        rows(F32), rows(F32), pltpu.VMEM((chunks, HS, width), F32), rows(F32),
        pltpu.VMEM((HS, width), F32), pltpu.VMEM((8, 128), F32),
    ]
    held = pl.pallas_call(
        functools.partial(
            layer_kernel, shards, head_shards, float(width * head_shards), chunks
        ),
        in_specs=[hbm] * 4 + [vmem, vmem],
        out_specs=[vmem] * len(held),
        out_shape=held,
        scratch_shapes=scratch,
        compiler_params=pltpu.CompilerParams(**params),
        name="layer",
    )(queries, keys, values, d_out, gain, ld_t)
    out = jax.ShapeDtypeStruct((n, width), BF16)
    return pl.pallas_call(
        functools.partial(last_kernel, chunks),
        in_specs=[vmem] * len(held),
        out_specs=[hbm] * 4 + [vmem],
        out_shape=[out] * 4 + [jax.ShapeDtypeStruct((width,), F32)],
        scratch_shapes=[
            rows(BF16), rows(BF16), pltpu.VMEM((HS, width), F32), pltpu.SemaphoreType.DMA((4, chunks))
        ],
        compiler_params=pltpu.CompilerParams(vmem_limit_bytes=LAST_LIMIT),
        name="last",
    )(*held)


VMEM_LIMIT = 33 * 1024 * 1024
LAST_LIMIT = 12 * 1024 * 1024


def solution(mesh):
    rows = P("ctx", "head")
    return jax.shard_map(
        functools.partial(body, mesh.shape["ctx"], mesh.shape["head"]),
        mesh=mesh,
        in_specs=(rows, rows, rows, rows, P("head"), rows),
        out_specs=(rows, rows, rows, rows, P("head")),
        check_vma=False,
    )
```

```python
import functools

import jax
import jax.numpy as jnp
from jax import lax
from jax.experimental import pallas as pl
from jax.experimental.pallas import tpu as pltpu
from jax.sharding import PartitionSpec as P

F32 = jnp.float32
BF16 = jnp.bfloat16
C = 128
HS = 96
GL = 384
PIECES = 3
OWNERS = HS // 8
NEG = -1e30
LOG2E = 1.4426950408889634
MESH = pl.DeviceIdType.MESH


def dot(a, b):
    return lax.dot_general(a, b, (((1,), (0,)), ((), ())), preferred_element_type=F32)


def dot_nt(a, b):
    return lax.dot_general(a, b, (((1,), (1,)), ((), ())), preferred_element_type=F32)


def both(hi, lo, w):
    r = dot(jnp.concatenate([hi, lo], axis=0), w)
    return r[: hi.shape[0]] + r[hi.shape[0] :]


def both_nt(hi, lo, w):
    r = dot_nt(jnp.concatenate([hi, lo], axis=0), w)
    return r[: hi.shape[0]] + r[hi.shape[0] :]


def split(x):
    hi = x.astype(BF16)
    lo = (x - hi.astype(F32)).astype(BF16)
    return hi, lo


def lane_mask(lo, hi, rows, dtype):
    lane = lax.broadcasted_iota(jnp.int32, (rows, 128), 1)
    return jnp.where((lane >= lo) & (lane < hi), 1.0, 0.0).astype(dtype)


def head_tiles(x, parity, dtype):
    rows = x.shape[0]
    t0, t1 = x[:, :128], x[:, 128:]
    zero = jnp.zeros((rows, 128), dtype)
    if parity == 0:
        a = [t0 * lane_mask(0, 96, rows, dtype), zero]
        b = [t0 * lane_mask(96, 128, rows, dtype), t1 * lane_mask(0, 64, rows, dtype)]
    else:
        a = [t0 * lane_mask(64, 128, rows, dtype), t1 * lane_mask(0, 32, rows, dtype)]
        b = [zero, t1 * lane_mask(32, 128, rows, dtype)]
    return jnp.concatenate(a, axis=1), jnp.concatenate(b, axis=1)


def stacked(x, parity):
    a, b = head_tiles(x, parity, x.dtype)
    return jnp.concatenate([a, b], axis=0)


def block_state(s, parity):
    a, b = head_tiles(s, parity, s.dtype)
    pad = jnp.zeros((64, 256), s.dtype)
    return jnp.concatenate([a, b, pad] if parity == 0 else [pad, a, b], axis=0)


def compact(u, parity):
    a, _ = head_tiles(u[:HS], parity, F32)
    _, b = head_tiles(u[HS:], parity, F32)
    return a + b


def merge(w0, w1):
    return jnp.concatenate([w0[:, :128], w0[:, 128:] + w1[:, :128], w1[:, 128:]], axis=1)


def group_lanes(cols):
    rows = cols[0].shape[0]
    lane = lax.broadcasted_iota(jnp.int32, (rows, 128), 1)
    return jnp.concatenate(
        [
            jnp.where(lane < 96, cols[0], cols[1]),
            jnp.where(lane < 64, cols[1], cols[2]),
            jnp.where(lane < 32, cols[2], cols[3]),
        ],
        axis=1,
    )


def columns_of(ct):
    full = jnp.concatenate([ct, jnp.zeros((C - 8, C), F32)], axis=0).T
    return [jnp.broadcast_to(full[:, h : h + 1], (C, C)) for h in range(8)]


def window(parity):
    return slice(128 * parity, 128 * parity + 256)


def causal_bias():
    row = lax.broadcasted_iota(jnp.int32, (C, C), 0)
    col = lax.broadcasted_iota(jnp.int32, (C, C), 1)
    return jnp.where(row >= col, 0.0, NEG)


def pair_decay(ct, cols, heads, bias):
    parts = [jnp.exp2(cols[h] - ct[h : h + 1, :] + bias) for h in heads]
    return jnp.concatenate(parts, axis=1)


def turned(x):
    return jnp.concatenate([x[:, :C].T, x[:, C:].T], axis=1)


def token_sums(x):
    acc = x[:, :128]
    for i in range(1, 6):
        acc = acc + x[:, 128 * i : 128 * i + 128]
    return jnp.sum(acc.T, axis=0, keepdims=True)


def wait_bytes(ref, sem):
    pltpu.make_async_copy(ref, ref, sem).wait()


def owner_of(chip):
    y, x = chip // 4, lax.rem(chip, 4)
    return 3 * y + jnp.minimum(lax.rem(x - y + 3, 4), 2), lax.rem(x - y + 4, 4) != 0


class Scan:
    def __init__(self, chips, me, reverse, tots, refs):
        self.chips, self.reverse, self.tots = chips, reverse, tots
        self.swap, self.swapped, self.send, self.taken, self.made, self.given = refs[:6]
        self.turn, self.turned, self.sems = refs[6:]
        self.chip, self.core = me // 2, lax.rem(me, 2)
        self.mine, self.is_owner = owner_of(self.chip)

    def other_core(self, src, dst, j):
        return pltpu.make_async_remote_copy(
            src_ref=src, dst_ref=dst, send_sem=self.sems.at[j], recv_sem=self.sems.at[j + 1],
            device_id={"ctx": 2 * self.chip + 1 - self.core}, device_id_type=MESH,
        )

    def other_chip(self, src, dst, j, chip):
        return pltpu.make_async_remote_copy(
            src_ref=src, dst_ref=dst, send_sem=self.sems.at[j], recv_sem=self.sems.at[j + 1],
            device_id={"ctx": 2 * chip + self.core}, device_id_type=MESH,
        )

    def start(self, state_ref, extra):
        self.swap[:HS, :] = state_ref[1 - self.core]
        self.swap[HS:, :] = extra
        self.other_core(self.swap, self.swapped, 0).start()

    def combine(self, state_ref, extra):
        self.other_core(self.swap, self.swapped, 0).wait_recv()
        low = self.core == 0
        mine, theirs = state_ref[self.core], self.swapped[:HS, :]
        a, b = jnp.where(low, mine, theirs), jnp.where(low, theirs, mine)
        ea, eb = jnp.where(low, extra, self.swapped[HS:, :]), jnp.where(low, self.swapped[HS:, :], extra)
        if self.reverse:
            both_cores = a + jnp.exp2(self.tots[0, 0:1, :]) * b
            tile = (ea + eb)[:, :128]
            self.turn[...] = b
        else:
            self.tots[0] = ea
            self.tots[1] = eb
            both_cores = jnp.exp2(eb[0:1, :]) * a + b
            total = ea[0:1, :] + eb[0:1, :]
            tile = jnp.concatenate(
                [total[:, 128 * i : 128 * i + 128] for i in range(3)] + [jnp.zeros((5, 128), F32)], axis=0
            )
            self.turn[...] = a
        for r in range(OWNERS):
            self.send[r, :, :GL] = both_cores[8 * r : 8 * r + 8]
            self.send[r, :, GL:] = tile

        @pl.loop(1, self.chips)
        def _(i):
            chip = lax.rem(self.chip + i, self.chips)
            r, owns = owner_of(chip)

            @pl.when(owns)
            def _():
                self.other_chip(self.send.at[r], self.taken.at[self.chip], 2, chip).start()

    def middle(self, totals):
        chips, chip, mine = self.chips, self.chip, self.mine

        @pl.when(self.is_owner)
        def _():
            self.taken[chip] = self.send[mine]
            wait_bytes(self.taken.at[pl.ds(0, chips - 1)], self.sems.at[3])

            def step(i, carry):
                acc, tile = carry
                j = chips - 1 - i if self.reverse else i
                self.made[j, :, :GL] = acc
                total = jnp.concatenate([totals[j, t : t + 1, GL:] for t in range(3)], axis=1)
                if self.reverse:
                    tile = tile + self.taken[j, :, GL:]
                return jnp.exp2(total) * acc + self.taken[j, :, :GL], tile

            _, tile = lax.fori_loop(
                0, chips, step, (jnp.zeros((8, GL), F32), jnp.zeros((8, 128), F32)), unroll=4
            )
            for j in range(chips):
                self.made[j, :, GL:] = tile

            @pl.loop(1, chips)
            def _(i):
                to = lax.rem(chip + i, chips)
                self.other_chip(self.made.at[to], self.given.at[mine], 4, to).start()

            self.given[mine] = self.made[chip]

    def gather(self, keep):
        @pl.when(self.is_owner)
        def _():
            wait_bytes(self.given.at[pl.ds(0, OWNERS - 1)], self.sems.at[5])
            wait_bytes(self.send.at[pl.ds(0, OWNERS - 1)], self.sems.at[2])
            wait_bytes(self.made.at[pl.ds(0, self.chips - 1)], self.sems.at[4])

        @pl.when(jnp.logical_not(self.is_owner))
        def _():
            wait_bytes(self.given, self.sems.at[5])
            wait_bytes(self.send, self.sems.at[2])

        low = self.core == 0
        outer = jnp.concatenate([self.given[r, :, :GL] for r in range(OWNERS)], axis=0)
        if self.reverse:
            inner = self.turn[...] + jnp.exp2(self.tots[1, 0:1, :]) * outer
            mine, theirs = jnp.where(low, inner, outer), jnp.where(low, outer, inner)
        else:
            inner = self.turn[...] + jnp.exp2(self.tots[0, 0:1, :]) * outer
            mine, theirs = jnp.where(low, outer, inner), jnp.where(low, inner, outer)
        keep[self.core] = mine
        self.turn[...] = theirs
        self.other_core(self.turn, self.turned, 6).start()

    def finish(self, keep):
        self.other_core(self.turn, self.turned, 6).wait()
        self.other_core(self.swap, self.swapped, 0).wait_send()
        keep[1 - self.core] = self.turned[...]


def rows_of(i):
    return pl.ds(pl.multiple_of(i * C, C), C)


groups = [slice(GL * g, GL * (g + 1)) for g in range(2)]


def layer_kernel(
    shards, head_shards, total_width, chunks, q_in, k_in, v_in, do_in, gain_in, ld_ref,
    out_ref, dq_ref, k_s, v_s, att_s, dv_s, u_s, cexp_s, run_s, dgain_ref,
    q_s, do_s, in_sems, ct_s, shi_s, slo_s, ghi_s, glo_s, phi_s, plo_s,
    own_s, tot_s, start_s, dg_s, gain_ref, sums_s, sums_t, sums_sems,
    tots_s, *scan_refs,
):
    remote = shards > 1
    dk_s = att_s
    if remote:
        me, my_head = lax.axis_index("ctx"), lax.axis_index("head")
        chips = shards // 2
        core = lax.rem(me, 2)
        on = Scan(chips, me, False, tots_s, scan_refs[:9])
        back = Scan(chips, me, True, tots_s, scan_refs[9:])
        barrier = pltpu.get_barrier_semaphore()
        pl.semaphore_signal(
            barrier, inc=1, device_id={"ctx": me + 1 - 2 * core}, device_id_type=MESH
        )

        @pl.loop(1, chips)
        def _(i):
            pl.semaphore_signal(
                barrier, inc=1, device_id={"ctx": lax.rem(me + 2 * i, shards)}, device_id_type=MESH
            )

        @pl.loop(1, head_shards)
        def _(i):
            pl.semaphore_signal(
                barrier, inc=1, device_id={"head": lax.rem(my_head + i, head_shards)},
                device_id_type=MESH,
            )

    per = chunks // PIECES
    inputs = [(k_in, k_s), (v_in, v_s), (q_in, q_s), (do_in, do_s)]

    def arrival(a, b):
        rows = pl.ds(b * per * C, per * C)
        return pltpu.make_async_copy(inputs[a][0].at[rows], inputs[a][1].at[rows], in_sems.at[a, b])

    for b in range(PIECES):
        arrival(0, b).start()
        arrival(1, b).start()
    for a in (2, 3):
        for b in range(PIECES):
            arrival(a, b).start()
    for j in range(gain_ref.shape[1] // 128):
        gain_ref[:, 128 * j : 128 * j + 128] = gain_in[128 * j : 128 * j + 128].reshape(1, 128)

    row = lax.broadcasted_iota(jnp.int32, (C, C), 0)
    col = lax.broadcasted_iota(jnp.int32, (C, C), 1)
    upper = jnp.where(row <= col, 1.0, 0.0)
    ct_s[...] = LOG2E * lax.dot_general(
        ld_ref[...], upper, (((1,), (0,)), ((), ())), preferred_element_type=F32,
        precision=lax.Precision.HIGHEST,
    )
    own_s[...] = jnp.zeros_like(own_s)
    tot_s[...] = jnp.zeros_like(tot_s)

    def ct_of(i):
        return ct_s[pl.ds(pl.multiple_of(i * 8, 8), 8), :]

    def states(i):
        rows = rows_of(i)
        ct = ct_of(i)
        tot_s[...] += jnp.broadcast_to(ct[:, C - 1 : C], (8, 128))
        cols = columns_of(ct)
        for g, lanes in enumerate(groups):
            cexp = group_lanes(cols[4 * g : 4 * g + 4])
            cexp_s[rows, lanes] = cexp
            end = cexp[C - 1 : C, :]
            v_hi, v_lo = split(v_s[rows, lanes].astype(F32) * jnp.exp2(end - cexp))
            v_tail = jnp.concatenate([v_hi, v_lo], axis=0)
            kt = k_s[rows, lanes].T
            parts = []
            for p in range(2):
                kp = kt[192 * p : 192 * p + 192]
                parts.append(compact(dot(jnp.concatenate([kp, kp], axis=1), v_tail[:, window(p)]), p))
            u = merge(*parts)
            u_s[i, :, lanes] = u
            own_s[g] = jnp.exp2(end) * own_s[g] + u

    def local_rows(i):
        rows = rows_of(i)
        ct = ct_of(i)
        cols = columns_of(ct)
        bias = causal_bias()
        for g, lanes in enumerate(groups):
            q, k, v = q_s[rows, lanes], k_s[rows, lanes], v_s[rows, lanes]
            outs = []
            for p in range(2):
                w = window(p)
                heads = (4 * g + 2 * p, 4 * g + 2 * p + 1)
                scores = dot_nt(q[:, w], stacked(k[:, w], p)) * pair_decay(ct, cols, heads, bias)
                hi, lo = split(scores)
                vs = stacked(v[:, w], p)
                outs.append(dot(hi, vs) + dot(lo, vs))
                pair = slice(256 * (2 * g + p), 256 * (2 * g + p) + 256)
                phi_s[rows, pair] = turned(hi)
                plo_s[rows, pair] = turned(lo)
            att_s[rows, lanes] = merge(*outs)

    def whole_rows(i):
        rows = rows_of(i)
        for g, lanes in enumerate(groups):
            q = q_s[rows, lanes]
            cexp = cexp_s[rows, lanes]
            end = cexp[C - 1 : C, :]
            s = run_s[g]
            s_hi, s_lo = split(s)
            shi_s[i, :, lanes] = s_hi
            slo_s[i, :, lanes] = s_lo
            outs = []
            for p in range(2):
                w = window(p)
                outs.append(dot(q[:, w], block_state(s_hi[:, w], p)) + dot(q[:, w], block_state(s_lo[:, w], p)))
            att_s[rows, lanes] += jnp.exp2(cexp) * merge(*outs)
            run_s[g] = jnp.exp2(end) * s + u_s[i, :, lanes]
        att = att_s[rows, :]
        grown = do_s[rows, :].astype(F32) * gain_ref[...]
        sums_s[i] = jnp.concatenate(
            [token_sums(att * att), token_sums(grown * att), jnp.zeros((6, C), F32)], axis=0
        )

    def sums_copy(b, target):
        part = pl.ds(b * per, per)
        return pltpu.make_async_remote_copy(
            src_ref=sums_s.at[part], dst_ref=sums_t.at[my_head, part], send_sem=sums_sems.at[0, b],
            recv_sem=sums_sems.at[1, b], device_id={"head": target}, device_id_type=MESH,
        )

    def norm_rows(i):
        rows = rows_of(i)
        if remote:
            sums = sums_t[0, i]
            for j in range(1, head_shards):
                sums = sums + sums_t[j, i]
        else:
            sums = sums_s[i]
        rms = jnp.sqrt(sums[0:1, :] / total_width + 1e-06)
        inv = 1.0 / rms
        mean = sums[1:2, :] * inv / total_width
        inv_c = jnp.broadcast_to(inv, (C, C)).T
        coef_c = jnp.broadcast_to(mean * inv * inv, (C, C)).T
        inv_c = jnp.concatenate([inv_c] * 3, axis=1)
        coef_c = jnp.concatenate([coef_c] * 3, axis=1)
        for g, lanes in enumerate(groups):
            att = att_s[rows, lanes]
            up = do_s[rows, lanes].astype(F32)
            gain = gain_ref[:, lanes]
            normed = att * inv_c
            out_ref[rows, lanes] = (normed * gain).astype(BF16)
            dg_s[:, lanes] += jnp.sum((up * normed).reshape(C // 8, 8, GL), axis=0)
            grad = up * gain * inv_c - att * coef_c
            g_hi, g_lo = split(grad)
            ghi_s[rows, lanes] = g_hi
            glo_s[rows, lanes] = g_lo
            cexp = cexp_s[rows, lanes]
            end = cexp[C - 1 : C, :]
            e_hi, e_lo = split(grad * jnp.exp2(cexp))
            e_both = jnp.concatenate([e_hi, e_lo], axis=0)
            qt = q_s[rows, lanes].T
            parts = []
            for p in range(2):
                qp = qt[192 * p : 192 * p + 192]
                parts.append(compact(dot(jnp.concatenate([qp, qp], axis=1), e_both[:, window(p)]), p))
            w = merge(*parts)
            u_s[i, :, lanes] = w
            own_s[g] += jnp.exp2(start_s[0:1, lanes]) * w
            start_s[0:1, lanes] += end

    def grad_rows(i):
        rows = rows_of(i)
        ct = ct_of(i)
        cols = columns_of(ct)
        bias = causal_bias()
        for g, lanes in enumerate(groups):
            q, k, v = q_s[rows, lanes], k_s[rows, lanes], v_s[rows, lanes]
            g_hi, g_lo = ghi_s[rows, lanes], glo_s[rows, lanes]
            from_start = jnp.exp2(cexp_s[rows, lanes])
            s_hi, s_lo = shi_s[i, :, lanes], slo_s[i, :, lanes]
            dqs, olds, dks, dvs = [], [], [], []
            for p in range(2):
                w = window(p)
                heads = (4 * g + 2 * p, 4 * g + 2 * p + 1)
                pair = slice(256 * (2 * g + p), 256 * (2 * g + p) + 256)
                hw, lw = g_hi[:, w], g_lo[:, w]
                hs, ls = stacked(hw, p), stacked(lw, p)
                decay = pair_decay(ct, cols, heads, bias)
                b_hi, b_lo = block_state(s_hi[:, w], p), block_state(s_lo[:, w], p)
                d_hi, d_lo = split(both_nt(hw, lw, stacked(v[:, w], p)) * decay)
                ks = stacked(k[:, w], p)
                dqs.append(dot(d_hi, ks) + dot(d_lo, ks))
                olds.append(both_nt(hw, lw, b_hi) + dot_nt(hw, b_lo))
                dks.append(both(turned(d_hi), turned(d_lo), stacked(q[:, w], p)))
                p_hi, p_lo = phi_s[rows, pair], plo_s[rows, pair]
                dvs.append(both(p_hi, p_lo, hs) + dot(p_hi, ls))
            dq_ref[rows, lanes] = (merge(*dqs) + from_start * merge(*olds)).astype(BF16)
            dk_s[rows, lanes] = merge(*dks)
            dv_s[rows, lanes] = merge(*dvs)

    def over(lo, hi, f):
        pl.loop(lo, hi)(f)

    for b in range(PIECES):
        arrival(0, b).wait()
        arrival(1, b).wait()
        over(b * per, (b + 1) * per, states)
    totals = [
        group_lanes([jnp.broadcast_to(tot_s[h : h + 1, :], (8, 128)) for h in range(4 * g, 4 * g + 4)])
        for g in range(2)
    ]
    if remote:
        low = core == 0
        own_total, other_total = jnp.where(low, *totals), jnp.where(low, *totals[::-1])
        pl.semaphore_wait(barrier, chips + head_shards - 1)
        on.start(own_s, other_total)
    for b in range(PIECES):
        arrival(2, b).wait()
        arrival(3, b).wait()
    cuts = [chunks * c // 12 for c in LOCAL_CUTS]
    over(0, cuts[0], local_rows)
    if remote:
        on.combine(own_s, own_total)
    over(cuts[0], cuts[1], local_rows)
    if remote:
        on.middle(on.taken)
    over(cuts[1], cuts[2], local_rows)
    if remote:
        on.gather(run_s)
    over(cuts[2], chunks, local_rows)
    if remote:
        on.finish(run_s)
    else:
        run_s[...] = jnp.zeros_like(run_s)
    for b in range(PIECES):
        over(b * per, (b + 1) * per, whole_rows)
        if remote:
            part = pl.ds(b * per, per)
            sums_t[my_head, part] = sums_s[part]

            @pl.loop(1, head_shards)
            def _(i):
                sums_copy(b, lax.rem(my_head + i, head_shards)).start()

    own_s[...] = jnp.zeros_like(own_s)
    start_s[...] = jnp.zeros_like(start_s)
    dg_s[...] = jnp.zeros_like(dg_s)
    for b in range(PIECES):
        if remote:
            moved = sums_t.at[pl.ds(0, head_shards - 1), pl.ds(b * per, per)]
            wait_bytes(moved, sums_sems.at[1, b])
            wait_bytes(moved, sums_sems.at[0, b])
        over(b * per, (b + 1) * per, norm_rows)

    sums = jnp.sum(dg_s[...], axis=0, keepdims=True)
    tile = jnp.concatenate(
        [sums[:, 128 * i : 128 * i + 128] for i in range(6)] + [jnp.zeros((2, 128), F32)], axis=0
    )
    cuts = [chunks * c // 12 for c in GRAD_CUTS]
    if remote:
        tile = jnp.concatenate([tile, jnp.zeros((8, GL - 128), F32)], axis=1)
        back.start(own_s, tile)
    over(0, cuts[0], grad_rows)
    if remote:
        back.combine(own_s, tile)
    over(cuts[0], cuts[1], grad_rows)
    if remote:
        back.middle(on.taken)
    over(cuts[1], cuts[2], grad_rows)
    if remote:
        back.gather(run_s)
        dgain_ref[...] = back.given[0, :, GL:]
    over(cuts[2], chunks, grad_rows)
    if remote:
        back.finish(run_s)
    else:
        dgain_ref[...] = tile
        run_s[...] = jnp.zeros_like(run_s)


def last_kernel(
    chunks, out_v, dq_v, k_s, v_s, dk_s, dv_s, u_s, cexp_s, state_ref, dgain_v,
    out_hbm, dq_hbm, dk_hbm, dv_hbm, dgain_ref, dk_ref, dv_ref, run_s, sems,
):
    first = [(out_v, out_hbm), (dq_v, dq_hbm)]
    for j, (src, dst) in enumerate(first):
        pltpu.make_async_copy(src, dst, sems.at[j, 0]).start()
    for j in range(dgain_ref.shape[0] // 128):
        dgain_ref[128 * j : 128 * j + 128] = dgain_v[j : j + 1, :].reshape(128)
    run_s[...] = state_ref[...]

    def copies(i):
        rows = rows_of(i)
        return [
            pltpu.make_async_copy(src.at[rows], dst.at[rows], sems.at[2 + j, i])
            for j, (src, dst) in enumerate([(dk_ref, dk_hbm), (dv_ref, dv_hbm)])
        ]

    def last_rows(i):
        rows = rows_of(i)
        for g, lanes in enumerate(groups):
            k, v = k_s[rows, lanes], v_s[rows, lanes]
            cexp = cexp_s[rows, lanes]
            end = cexp[C - 1 : C, :]
            tail = jnp.exp2(end - cexp)
            s = run_s[g]
            s_hi, s_lo = split(s)
            dks, dvs = [], []
            for p in range(2):
                w = window(p)
                b_hi, b_lo = block_state(s_hi[:, w], p), block_state(s_lo[:, w], p)
                dks.append(dot_nt(v[:, w], b_hi) + dot_nt(v[:, w], b_lo))
                dvs.append(dot(k[:, w], b_hi) + dot(k[:, w], b_lo))
            dk_ref[rows, lanes] = (dk_s[rows, lanes] + tail * merge(*dks)).astype(BF16)
            dv_ref[rows, lanes] = (dv_s[rows, lanes] + tail * merge(*dvs)).astype(BF16)
            run_s[g] = jnp.exp2(end) * s + u_s[i, :, lanes]
        for copy in copies(i):
            copy.start()

    pl.loop(0, chunks)(lambda i: last_rows(chunks - 1 - i))
    for j, (src, dst) in enumerate(first):
        pltpu.make_async_copy(src, dst, sems.at[j, 0]).wait()

    @pl.loop(0, chunks)
    def _(i):
        for copy in copies(i):
            copy.wait()


def body(shards, head_shards, queries, keys, values, log_decay, gain, d_out):
    n, width = queries.shape
    chunks = n // C
    ld_t = log_decay.reshape(chunks, C, 8).transpose(0, 2, 1).reshape(chunks * 8, C)
    hbm, vmem = pl.BlockSpec(memory_space=pl.ANY), pl.BlockSpec(memory_space=pltpu.VMEM)
    rows = lambda dtype: pltpu.VMEM((n, width), dtype)
    chips = max(shards // 2, 1)
    scan = [
        pltpu.VMEM((HS + 8, GL), F32),
        pltpu.VMEM((HS + 8, GL), F32),
        pltpu.VMEM((OWNERS, 8, 512), F32),
        pltpu.VMEM((chips, 8, 512), F32),
        pltpu.VMEM((chips, 8, 512), F32),
        pltpu.VMEM((OWNERS, 8, 512), F32),
        pltpu.VMEM((HS, GL), F32),
        pltpu.VMEM((HS, GL), F32),
        pltpu.SemaphoreType.DMA((8,)),
    ]
    scratch = [
        rows(BF16), rows(BF16),
        pltpu.SemaphoreType.DMA((4, PIECES)),
        pltpu.VMEM((chunks * 8, C), F32),
        pltpu.VMEM((chunks, HS, width), BF16),
        pltpu.VMEM((chunks, HS, width), BF16),
        rows(BF16), rows(BF16),
        pltpu.VMEM((n, 1024), BF16), pltpu.VMEM((n, 1024), BF16),
        pltpu.VMEM((2, HS, GL), F32),
        pltpu.VMEM((8, 128), F32),
        pltpu.VMEM((8, width), F32),
        pltpu.VMEM((8, width), F32),
        pltpu.VMEM((1, width), F32),
        pltpu.VMEM((chunks, 8, C), F32),
        pltpu.VMEM((head_shards, chunks, 8, C), F32),
        pltpu.SemaphoreType.DMA((2, PIECES)),
        pltpu.VMEM((2, 8, GL), F32),
    ] + scan + scan
    params = dict(vmem_limit_bytes=VMEM_LIMIT)
    if shards > 1:
        params.update(collective_id=0, has_side_effects=True)
    held = [rows(BF16)] * 4 + [
        rows(F32), rows(F32), pltpu.VMEM((chunks, HS, width), F32), rows(F32),
        pltpu.VMEM((2, HS, GL), F32), pltpu.VMEM((8, 128), F32),
    ]
    held = pl.pallas_call(
        functools.partial(
            layer_kernel, shards, head_shards, float(width * head_shards), chunks
        ),
        in_specs=[hbm] * 4 + [vmem, vmem],
        out_specs=[vmem] * len(held),
        out_shape=held,
        scratch_shapes=scratch,
        compiler_params=pltpu.CompilerParams(**params),
        name="layer",
    )(queries, keys, values, d_out, gain, ld_t)
    out = jax.ShapeDtypeStruct((n, width), BF16)
    return pl.pallas_call(
        functools.partial(last_kernel, chunks),
        in_specs=[vmem] * len(held),
        out_specs=[hbm] * 4 + [vmem],
        out_shape=[out] * 4 + [jax.ShapeDtypeStruct((width,), F32)],
        scratch_shapes=[
            rows(BF16), rows(BF16), pltpu.VMEM((2, HS, GL), F32), pltpu.SemaphoreType.DMA((4, chunks))
        ],
        compiler_params=pltpu.CompilerParams(vmem_limit_bytes=LAST_LIMIT),
        name="last",
    )(*held)


LOCAL_CUTS = (2, 6, 10)
GRAD_CUTS = (1, 5, 9)
VMEM_LIMIT = 33 * 1024 * 1024
LAST_LIMIT = 12 * 1024 * 1024


def solution(mesh):
    rows = P("ctx", "head")
    return jax.shard_map(
        functools.partial(body, mesh.shape["ctx"], mesh.shape["head"]),
        mesh=mesh,
        in_specs=(rows, rows, rows, rows, P("head"), rows),
        out_specs=(rows, rows, rows, rows, P("head")),
        check_vma=False,
    )
```

```python
import functools

import jax
import jax.numpy as jnp
from jax import lax
from jax.experimental import pallas as pl
from jax.experimental.pallas import tpu as pltpu
from jax.sharding import PartitionSpec as P

F32 = jnp.float32
BF16 = jnp.bfloat16
C = 128
HS = 96
GL = 384
PIECES = 3
OWNERS = HS // 8
NEG = -1e30
LOG2E = 1.4426950408889634
MESH = pl.DeviceIdType.MESH


def dot(a, b):
    return lax.dot_general(a, b, (((1,), (0,)), ((), ())), preferred_element_type=F32)


def dot_nt(a, b):
    return lax.dot_general(a, b, (((1,), (1,)), ((), ())), preferred_element_type=F32)


def both(hi, lo, w):
    r = dot(jnp.concatenate([hi, lo], axis=0), w)
    return r[: hi.shape[0]] + r[hi.shape[0] :]


def both_nt(hi, lo, w):
    r = dot_nt(jnp.concatenate([hi, lo], axis=0), w)
    return r[: hi.shape[0]] + r[hi.shape[0] :]


def split(x):
    hi = x.astype(BF16)
    lo = (x - hi.astype(F32)).astype(BF16)
    return hi, lo


def lane_mask(lo, hi, rows, dtype):
    lane = lax.broadcasted_iota(jnp.int32, (rows, 128), 1)
    return jnp.where((lane >= lo) & (lane < hi), 1.0, 0.0).astype(dtype)


def head_tiles(x, parity, dtype):
    rows = x.shape[0]
    t0, t1 = x[:, :128], x[:, 128:]
    zero = jnp.zeros((rows, 128), dtype)
    if parity == 0:
        a = [t0 * lane_mask(0, 96, rows, dtype), zero]
        b = [t0 * lane_mask(96, 128, rows, dtype), t1 * lane_mask(0, 64, rows, dtype)]
    else:
        a = [t0 * lane_mask(64, 128, rows, dtype), t1 * lane_mask(0, 32, rows, dtype)]
        b = [zero, t1 * lane_mask(32, 128, rows, dtype)]
    return jnp.concatenate(a, axis=1), jnp.concatenate(b, axis=1)


def stacked(x, parity):
    a, b = head_tiles(x, parity, x.dtype)
    return jnp.concatenate([a, b], axis=0)


def block_state(s, parity):
    a, b = head_tiles(s, parity, s.dtype)
    pad = jnp.zeros((64, 256), s.dtype)
    return jnp.concatenate([a, b, pad] if parity == 0 else [pad, a, b], axis=0)


def compact(u, parity):
    a, _ = head_tiles(u[:HS], parity, F32)
    _, b = head_tiles(u[HS:], parity, F32)
    return a + b


def merge(w0, w1):
    return jnp.concatenate([w0[:, :128], w0[:, 128:] + w1[:, :128], w1[:, 128:]], axis=1)


def group_lanes(cols):
    rows = cols[0].shape[0]
    lane = lax.broadcasted_iota(jnp.int32, (rows, 128), 1)
    return jnp.concatenate(
        [
            jnp.where(lane < 96, cols[0], cols[1]),
            jnp.where(lane < 64, cols[1], cols[2]),
            jnp.where(lane < 32, cols[2], cols[3]),
        ],
        axis=1,
    )


def columns_of(ct):
    full = jnp.concatenate([ct, jnp.zeros((C - 8, C), F32)], axis=0).T
    return [jnp.broadcast_to(full[:, h : h + 1], (C, C)) for h in range(8)]


def window(parity):
    return slice(128 * parity, 128 * parity + 256)


def causal_bias():
    row = lax.broadcasted_iota(jnp.int32, (C, C), 0)
    col = lax.broadcasted_iota(jnp.int32, (C, C), 1)
    return jnp.where(row >= col, 0.0, NEG)


def pair_decay(ct, cols, heads, bias):
    parts = [jnp.exp2(cols[h] - ct[h : h + 1, :] + bias) for h in heads]
    return jnp.concatenate(parts, axis=1)


def turned(x):
    return jnp.concatenate([x[:, :C].T, x[:, C:].T], axis=1)


def token_sums(x):
    acc = x[:, :128]
    for i in range(1, 6):
        acc = acc + x[:, 128 * i : 128 * i + 128]
    return jnp.sum(acc.T, axis=0, keepdims=True)


def wait_bytes(ref, sem):
    pltpu.make_async_copy(ref, ref, sem).wait()


def owner_of(chip):
    y, x = chip // 4, lax.rem(chip, 4)
    return 3 * y + jnp.minimum(lax.rem(x - y + 3, 4), 2), lax.rem(x - y + 4, 4) != 0


class Scan:
    def __init__(self, chips, me, reverse, tots, refs):
        self.chips, self.reverse, self.tots = chips, reverse, tots
        self.swap, self.swapped, self.send, self.taken, self.made, self.given = refs[:6]
        self.turn, self.turned, self.sems = refs[6:]
        self.chip, self.core = me // 2, lax.rem(me, 2)
        self.mine, self.is_owner = owner_of(self.chip)

    def other_core(self, src, dst, j):
        return pltpu.make_async_remote_copy(
            src_ref=src, dst_ref=dst, send_sem=self.sems.at[j], recv_sem=self.sems.at[j + 1],
            device_id={"ctx": 2 * self.chip + 1 - self.core}, device_id_type=MESH,
        )

    def other_chip(self, src, dst, j, chip):
        return pltpu.make_async_remote_copy(
            src_ref=src, dst_ref=dst, send_sem=self.sems.at[j], recv_sem=self.sems.at[j + 1],
            device_id={"ctx": 2 * chip + self.core}, device_id_type=MESH,
        )

    def start(self, state_ref, extra):
        self.swap[:HS, :] = state_ref[1 - self.core]
        self.swap[HS:, :] = extra
        self.other_core(self.swap, self.swapped, 0).start()

    def combine(self, state_ref, extra):
        self.other_core(self.swap, self.swapped, 0).wait_recv()
        low = self.core == 0
        mine, theirs = state_ref[self.core], self.swapped[:HS, :]
        a, b = jnp.where(low, mine, theirs), jnp.where(low, theirs, mine)
        ea, eb = jnp.where(low, extra, self.swapped[HS:, :]), jnp.where(low, self.swapped[HS:, :], extra)
        if self.reverse:
            both_cores = a + jnp.exp2(self.tots[0, 0:1, :]) * b
            tile = (ea + eb)[:, :128]
            self.turn[...] = b
        else:
            self.tots[0] = ea
            self.tots[1] = eb
            both_cores = jnp.exp2(eb[0:1, :]) * a + b
            total = ea[0:1, :] + eb[0:1, :]
            tile = jnp.concatenate(
                [total[:, 128 * i : 128 * i + 128] for i in range(3)] + [jnp.zeros((5, 128), F32)], axis=0
            )
            self.turn[...] = a
        for r in range(OWNERS):
            self.send[r, :, :GL] = both_cores[8 * r : 8 * r + 8]
            self.send[r, :, GL:] = tile

        @pl.loop(1, self.chips)
        def _(i):
            chip = lax.rem(self.chip + i, self.chips)
            r, owns = owner_of(chip)

            @pl.when(owns)
            def _():
                self.other_chip(self.send.at[r], self.taken.at[self.chip], 2, chip).start()

    def middle(self, totals):
        chips, chip, mine = self.chips, self.chip, self.mine

        @pl.when(self.is_owner)
        def _():
            self.taken[chip] = self.send[mine]
            wait_bytes(self.taken.at[pl.ds(0, chips - 1)], self.sems.at[3])

            def step(i, carry):
                acc, tile = carry
                j = chips - 1 - i if self.reverse else i
                self.made[j, :, :GL] = acc
                total = jnp.concatenate([totals[j, t : t + 1, GL:] for t in range(3)], axis=1)
                if self.reverse:
                    tile = tile + self.taken[j, :, GL:]
                return jnp.exp2(total) * acc + self.taken[j, :, :GL], tile

            _, tile = lax.fori_loop(
                0, chips, step, (jnp.zeros((8, GL), F32), jnp.zeros((8, 128), F32)), unroll=4
            )
            for j in range(chips):
                self.made[j, :, GL:] = tile

            @pl.loop(1, chips)
            def _(i):
                to = lax.rem(chip + i, chips)
                self.other_chip(self.made.at[to], self.given.at[mine], 4, to).start()

            self.given[mine] = self.made[chip]

    def gather(self, keep):
        @pl.when(self.is_owner)
        def _():
            wait_bytes(self.given.at[pl.ds(0, OWNERS - 1)], self.sems.at[5])
            wait_bytes(self.send.at[pl.ds(0, OWNERS - 1)], self.sems.at[2])
            wait_bytes(self.made.at[pl.ds(0, self.chips - 1)], self.sems.at[4])

        @pl.when(jnp.logical_not(self.is_owner))
        def _():
            wait_bytes(self.given, self.sems.at[5])
            wait_bytes(self.send, self.sems.at[2])

        low = self.core == 0
        outer = jnp.concatenate([self.given[r, :, :GL] for r in range(OWNERS)], axis=0)
        if self.reverse:
            inner = self.turn[...] + jnp.exp2(self.tots[1, 0:1, :]) * outer
            mine, theirs = jnp.where(low, inner, outer), jnp.where(low, outer, inner)
        else:
            inner = self.turn[...] + jnp.exp2(self.tots[0, 0:1, :]) * outer
            mine, theirs = jnp.where(low, outer, inner), jnp.where(low, inner, outer)
        keep[self.core] = mine
        self.turn[...] = theirs
        self.other_core(self.turn, self.turned, 6).start()

    def finish(self, keep):
        self.other_core(self.turn, self.turned, 6).wait()
        self.other_core(self.swap, self.swapped, 0).wait_send()
        keep[1 - self.core] = self.turned[...]


def rows_of(i):
    return pl.ds(pl.multiple_of(i * C, C), C)


groups = [slice(GL * g, GL * (g + 1)) for g in range(2)]


def layer_kernel(
    shards, head_shards, total_width, chunks, q_in, k_in, v_in, do_in, gain_in, ld_ref,
    out_ref, dq_ref, k_s, v_s, att_s, dv_s, u_s, cexp_s, run_s, dgain_ref,
    q_s, do_s, in_sems, ct_s, shi_s, slo_s, ghi_s, glo_s, phi_s, plo_s,
    own_s, tot_s, start_s, dg_s, gain_ref, sums_s, sums_t, sums_sems,
    tots_s, *scan_refs,
):
    remote = shards > 1
    dk_s = att_s
    if remote:
        me, my_head = lax.axis_index("ctx"), lax.axis_index("head")
        chips = shards // 2
        core = lax.rem(me, 2)
        on = Scan(chips, me, False, tots_s, scan_refs[:9])
        back = Scan(chips, me, True, tots_s, scan_refs[9:])
        barrier = pltpu.get_barrier_semaphore()
        pl.semaphore_signal(
            barrier, inc=1, device_id={"ctx": me + 1 - 2 * core}, device_id_type=MESH
        )

        @pl.loop(1, chips)
        def _(i):
            pl.semaphore_signal(
                barrier, inc=1, device_id={"ctx": lax.rem(me + 2 * i, shards)}, device_id_type=MESH
            )

        @pl.loop(1, head_shards)
        def _(i):
            pl.semaphore_signal(
                barrier, inc=1, device_id={"head": lax.rem(my_head + i, head_shards)},
                device_id_type=MESH,
            )

    per = chunks // PIECES
    inputs = [(k_in, k_s), (v_in, v_s), (q_in, q_s), (do_in, do_s)]

    def arrival(a, b):
        rows = pl.ds(pl.multiple_of(b * per * C, per * C), per * C)
        return pltpu.make_async_copy(inputs[a][0].at[rows], inputs[a][1].at[rows], in_sems.at[a, b])

    for b in range(PIECES):
        arrival(0, b).start()
        arrival(1, b).start()
    for a in (2, 3):
        for b in range(PIECES):
            arrival(a, b).start()
    for j in range(gain_ref.shape[1] // 128):
        gain_ref[:, 128 * j : 128 * j + 128] = gain_in[128 * j : 128 * j + 128].reshape(1, 128)

    row = lax.broadcasted_iota(jnp.int32, (C, C), 0)
    col = lax.broadcasted_iota(jnp.int32, (C, C), 1)
    upper = jnp.where(row <= col, 1.0, 0.0)
    ct_s[...] = LOG2E * lax.dot_general(
        ld_ref[...], upper, (((1,), (0,)), ((), ())), preferred_element_type=F32,
        precision=lax.Precision.HIGHEST,
    )
    own_s[...] = jnp.zeros_like(own_s)
    tot_s[...] = jnp.zeros_like(tot_s)

    def ct_of(i):
        return ct_s[pl.ds(pl.multiple_of(i * 8, 8), 8), :]

    def states(i):
        rows = rows_of(i)
        ct = ct_of(i)
        tot_s[...] += jnp.broadcast_to(ct[:, C - 1 : C], (8, 128))
        cols = columns_of(ct)
        for g, lanes in enumerate(groups):
            cexp = group_lanes(cols[4 * g : 4 * g + 4])
            cexp_s[rows, lanes] = cexp
            end = cexp[C - 1 : C, :]
            v_hi, v_lo = split(v_s[rows, lanes].astype(F32) * jnp.exp2(end - cexp))
            v_tail = jnp.concatenate([v_hi, v_lo], axis=0)
            kt = k_s[rows, lanes].T
            parts = []
            for p in range(2):
                kp = kt[192 * p : 192 * p + 192]
                parts.append(compact(dot(jnp.concatenate([kp, kp], axis=1), v_tail[:, window(p)]), p))
            u = merge(*parts)
            u_s[i, :, lanes] = u
            own_s[g] = jnp.exp2(end) * own_s[g] + u

    def local_rows(i):
        rows = rows_of(i)
        ct = ct_of(i)
        cols = columns_of(ct)
        bias = causal_bias()
        for g, lanes in enumerate(groups):
            q, k, v = q_s[rows, lanes], k_s[rows, lanes], v_s[rows, lanes]
            outs = []
            for p in range(2):
                w = window(p)
                heads = (4 * g + 2 * p, 4 * g + 2 * p + 1)
                scores = dot_nt(q[:, w], stacked(k[:, w], p)) * pair_decay(ct, cols, heads, bias)
                hi, lo = split(scores)
                vs = stacked(v[:, w], p)
                outs.append(dot(hi, vs) + dot(lo, vs))
                pair = slice(256 * (2 * g + p), 256 * (2 * g + p) + 256)
                phi_s[rows, pair] = turned(hi)
                plo_s[rows, pair] = turned(lo)
            att_s[rows, lanes] = merge(*outs)

    def whole_rows(i):
        rows = rows_of(i)
        for g, lanes in enumerate(groups):
            q = q_s[rows, lanes]
            cexp = cexp_s[rows, lanes]
            end = cexp[C - 1 : C, :]
            s = run_s[g]
            s_hi, s_lo = split(s)
            shi_s[i, :, lanes] = s_hi
            slo_s[i, :, lanes] = s_lo
            outs = []
            for p in range(2):
                w = window(p)
                outs.append(dot(q[:, w], block_state(s_hi[:, w], p)) + dot(q[:, w], block_state(s_lo[:, w], p)))
            att_s[rows, lanes] += jnp.exp2(cexp) * merge(*outs)
            run_s[g] = jnp.exp2(end) * s + u_s[i, :, lanes]
        att = att_s[rows, :]
        grown = do_s[rows, :].astype(F32) * gain_ref[...]
        sums_s[i] = jnp.concatenate(
            [token_sums(att * att), token_sums(grown * att), jnp.zeros((6, C), F32)], axis=0
        )

    def sums_copy(b, target):
        part = pl.ds(b * per, per)
        return pltpu.make_async_remote_copy(
            src_ref=sums_s.at[part], dst_ref=sums_t.at[my_head, part], send_sem=sums_sems.at[0, b],
            recv_sem=sums_sems.at[1, b], device_id={"head": target}, device_id_type=MESH,
        )

    def norm_rows(i):
        rows = rows_of(i)
        if remote:
            sums = sums_t[0, i]
            for j in range(1, head_shards):
                sums = sums + sums_t[j, i]
        else:
            sums = sums_s[i]
        rms = jnp.sqrt(sums[0:1, :] / total_width + 1e-06)
        inv = 1.0 / rms
        mean = sums[1:2, :] * inv / total_width
        inv_c = jnp.broadcast_to(inv, (C, C)).T
        coef_c = jnp.broadcast_to(mean * inv * inv, (C, C)).T
        inv_c = jnp.concatenate([inv_c] * 3, axis=1)
        coef_c = jnp.concatenate([coef_c] * 3, axis=1)
        for g, lanes in enumerate(groups):
            att = att_s[rows, lanes]
            up = do_s[rows, lanes].astype(F32)
            gain = gain_ref[:, lanes]
            normed = att * inv_c
            out_ref[rows, lanes] = (normed * gain).astype(BF16)
            dg_s[:, lanes] += jnp.sum((up * normed).reshape(C // 8, 8, GL), axis=0)
            grad = up * gain * inv_c - att * coef_c
            g_hi, g_lo = split(grad)
            ghi_s[rows, lanes] = g_hi
            glo_s[rows, lanes] = g_lo
            cexp = cexp_s[rows, lanes]
            end = cexp[C - 1 : C, :]
            e_hi, e_lo = split(grad * jnp.exp2(cexp))
            e_both = jnp.concatenate([e_hi, e_lo], axis=0)
            qt = q_s[rows, lanes].T
            parts = []
            for p in range(2):
                qp = qt[192 * p : 192 * p + 192]
                parts.append(compact(dot(jnp.concatenate([qp, qp], axis=1), e_both[:, window(p)]), p))
            w = merge(*parts)
            u_s[i, :, lanes] = w
            own_s[g] += jnp.exp2(start_s[0:1, lanes]) * w
            start_s[0:1, lanes] += end

    def grad_rows(i):
        rows = rows_of(i)
        ct = ct_of(i)
        cols = columns_of(ct)
        bias = causal_bias()
        for g, lanes in enumerate(groups):
            q, k, v = q_s[rows, lanes], k_s[rows, lanes], v_s[rows, lanes]
            g_hi, g_lo = ghi_s[rows, lanes], glo_s[rows, lanes]
            from_start = jnp.exp2(cexp_s[rows, lanes])
            s_hi, s_lo = shi_s[i, :, lanes], slo_s[i, :, lanes]
            dqs, olds, dks, dvs = [], [], [], []
            for p in range(2):
                w = window(p)
                heads = (4 * g + 2 * p, 4 * g + 2 * p + 1)
                pair = slice(256 * (2 * g + p), 256 * (2 * g + p) + 256)
                hw, lw = g_hi[:, w], g_lo[:, w]
                hs, ls = stacked(hw, p), stacked(lw, p)
                decay = pair_decay(ct, cols, heads, bias)
                b_hi, b_lo = block_state(s_hi[:, w], p), block_state(s_lo[:, w], p)
                d_hi, d_lo = split(both_nt(hw, lw, stacked(v[:, w], p)) * decay)
                ks = stacked(k[:, w], p)
                dqs.append(dot(d_hi, ks) + dot(d_lo, ks))
                olds.append(both_nt(hw, lw, b_hi) + dot_nt(hw, b_lo))
                dks.append(both(turned(d_hi), turned(d_lo), stacked(q[:, w], p)))
                p_hi, p_lo = phi_s[rows, pair], plo_s[rows, pair]
                dvs.append(both(p_hi, p_lo, hs) + dot(p_hi, ls))
            dq_ref[rows, lanes] = (merge(*dqs) + from_start * merge(*olds)).astype(BF16)
            dk_s[rows, lanes] = merge(*dks)
            dv_s[rows, lanes] = merge(*dvs)

    def over(lo, hi, f):
        pl.loop(lo, hi, unroll=2 if (hi - lo) % 2 == 0 else 1)(f)

    def piece(b, f):
        pl.loop(0, per, unroll=per)(lambda j: f(b * per + j))

    @pl.loop(0, PIECES)
    def _(b):
        arrival(0, b).wait()
        arrival(1, b).wait()
        piece(b, states)

    totals = [
        group_lanes([jnp.broadcast_to(tot_s[h : h + 1, :], (8, 128)) for h in range(4 * g, 4 * g + 4)])
        for g in range(2)
    ]
    if remote:
        low = core == 0
        own_total, other_total = jnp.where(low, *totals), jnp.where(low, *totals[::-1])
        pl.semaphore_wait(barrier, chips + head_shards - 1)
        on.start(own_s, other_total)
    for b in range(PIECES):
        arrival(2, b).wait()
        arrival(3, b).wait()
    cuts = [chunks * c // 12 for c in LOCAL_CUTS]
    over(0, cuts[0], local_rows)
    if remote:
        on.combine(own_s, own_total)
    over(cuts[0], cuts[1], local_rows)
    if remote:
        on.middle(on.taken)
    over(cuts[1], cuts[2], local_rows)
    if remote:
        on.gather(run_s)
    over(cuts[2], chunks, local_rows)
    if remote:
        on.finish(run_s)
    else:
        run_s[...] = jnp.zeros_like(run_s)
    @pl.loop(0, PIECES)
    def _(b):
        piece(b, whole_rows)
        if remote:
            part = pl.ds(b * per, per)
            sums_t[my_head, part] = sums_s[part]

            @pl.loop(1, head_shards)
            def _(i):
                sums_copy(b, lax.rem(my_head + i, head_shards)).start()

    own_s[...] = jnp.zeros_like(own_s)
    start_s[...] = jnp.zeros_like(start_s)
    dg_s[...] = jnp.zeros_like(dg_s)

    @pl.loop(0, PIECES)
    def _(b):
        if remote:
            moved = sums_t.at[pl.ds(0, head_shards - 1), pl.ds(b * per, per)]
            wait_bytes(moved, sums_sems.at[1, b])
            wait_bytes(moved, sums_sems.at[0, b])
        piece(b, norm_rows)

    sums = jnp.sum(dg_s[...], axis=0, keepdims=True)
    tile = jnp.concatenate(
        [sums[:, 128 * i : 128 * i + 128] for i in range(6)] + [jnp.zeros((2, 128), F32)], axis=0
    )
    cuts = [chunks * c // 12 for c in GRAD_CUTS]
    if remote:
        tile = jnp.concatenate([tile, jnp.zeros((8, GL - 128), F32)], axis=1)
        back.start(own_s, tile)
    over(0, cuts[0], grad_rows)
    if remote:
        back.combine(own_s, tile)
    over(cuts[0], cuts[1], grad_rows)
    if remote:
        back.middle(on.taken)
    over(cuts[1], cuts[2], grad_rows)
    if remote:
        back.gather(run_s)
        dgain_ref[...] = back.given[0, :, GL:]
    over(cuts[2], chunks, grad_rows)
    if remote:
        back.finish(run_s)
    else:
        dgain_ref[...] = tile
        run_s[...] = jnp.zeros_like(run_s)


def last_kernel(
    chunks, out_v, dq_v, k_s, v_s, dk_s, dv_s, u_s, cexp_s, state_ref, dgain_v,
    out_hbm, dq_hbm, dk_hbm, dv_hbm, dgain_ref, dk_ref, dv_ref, run_s, sems,
):
    first = [(out_v, out_hbm), (dq_v, dq_hbm)]
    for j, (src, dst) in enumerate(first):
        pltpu.make_async_copy(src, dst, sems.at[j, 0]).start()
    for j in range(dgain_ref.shape[0] // 128):
        dgain_ref[128 * j : 128 * j + 128] = dgain_v[j : j + 1, :].reshape(128)
    run_s[...] = state_ref[...]

    def copies(i):
        rows = rows_of(i)
        return [
            pltpu.make_async_copy(src.at[rows], dst.at[rows], sems.at[2 + j, i])
            for j, (src, dst) in enumerate([(dk_ref, dk_hbm), (dv_ref, dv_hbm)])
        ]

    def last_rows(i):
        rows = rows_of(i)
        for g, lanes in enumerate(groups):
            k, v = k_s[rows, lanes], v_s[rows, lanes]
            cexp = cexp_s[rows, lanes]
            end = cexp[C - 1 : C, :]
            tail = jnp.exp2(end - cexp)
            s = run_s[g]
            s_hi, s_lo = split(s)
            dks, dvs = [], []
            for p in range(2):
                w = window(p)
                b_hi, b_lo = block_state(s_hi[:, w], p), block_state(s_lo[:, w], p)
                dks.append(dot_nt(v[:, w], b_hi) + dot_nt(v[:, w], b_lo))
                dvs.append(dot(k[:, w], b_hi) + dot(k[:, w], b_lo))
            dk_ref[rows, lanes] = (dk_s[rows, lanes] + tail * merge(*dks)).astype(BF16)
            dv_ref[rows, lanes] = (dv_s[rows, lanes] + tail * merge(*dvs)).astype(BF16)
            run_s[g] = jnp.exp2(end) * s + u_s[i, :, lanes]
        for copy in copies(i):
            copy.start()

    pl.loop(0, chunks, unroll=3)(lambda i: last_rows(chunks - 1 - i))
    for j, (src, dst) in enumerate(first):
        pltpu.make_async_copy(src, dst, sems.at[j, 0]).wait()

    @pl.loop(0, chunks)
    def _(i):
        for copy in copies(i):
            copy.wait()


def body(shards, head_shards, queries, keys, values, log_decay, gain, d_out):
    n, width = queries.shape
    chunks = n // C
    ld_t = log_decay.reshape(chunks, C, 8).transpose(0, 2, 1).reshape(chunks * 8, C)
    hbm, vmem = pl.BlockSpec(memory_space=pl.ANY), pl.BlockSpec(memory_space=pltpu.VMEM)
    rows = lambda dtype: pltpu.VMEM((n, width), dtype)
    chips = max(shards // 2, 1)
    scan = [
        pltpu.VMEM((HS + 8, GL), F32),
        pltpu.VMEM((HS + 8, GL), F32),
        pltpu.VMEM((OWNERS, 8, 512), F32),
        pltpu.VMEM((chips, 8, 512), F32),
        pltpu.VMEM((chips, 8, 512), F32),
        pltpu.VMEM((OWNERS, 8, 512), F32),
        pltpu.VMEM((HS, GL), F32),
        pltpu.VMEM((HS, GL), F32),
        pltpu.SemaphoreType.DMA((8,)),
    ]
    scratch = [
        rows(BF16), rows(BF16),
        pltpu.SemaphoreType.DMA((4, PIECES)),
        pltpu.VMEM((chunks * 8, C), F32),
        pltpu.VMEM((chunks, HS, width), BF16),
        pltpu.VMEM((chunks, HS, width), BF16),
        rows(BF16), rows(BF16),
        pltpu.VMEM((n, 1024), BF16), pltpu.VMEM((n, 1024), BF16),
        pltpu.VMEM((2, HS, GL), F32),
        pltpu.VMEM((8, 128), F32),
        pltpu.VMEM((8, width), F32),
        pltpu.VMEM((8, width), F32),
        pltpu.VMEM((1, width), F32),
        pltpu.VMEM((chunks, 8, C), F32),
        pltpu.VMEM((head_shards, chunks, 8, C), F32),
        pltpu.SemaphoreType.DMA((2, PIECES)),
        pltpu.VMEM((2, 8, GL), F32),
    ] + scan + scan
    params = dict(vmem_limit_bytes=VMEM_LIMIT)
    if shards > 1:
        params.update(collective_id=0, has_side_effects=True)
    held = [rows(BF16)] * 4 + [
        rows(F32), rows(F32), pltpu.VMEM((chunks, HS, width), F32), rows(F32),
        pltpu.VMEM((2, HS, GL), F32), pltpu.VMEM((8, 128), F32),
    ]
    held = pl.pallas_call(
        functools.partial(
            layer_kernel, shards, head_shards, float(width * head_shards), chunks
        ),
        in_specs=[hbm] * 4 + [vmem, vmem],
        out_specs=[vmem] * len(held),
        out_shape=held,
        scratch_shapes=scratch,
        compiler_params=pltpu.CompilerParams(**params),
        name="layer",
    )(queries, keys, values, d_out, gain, ld_t)
    out = jax.ShapeDtypeStruct((n, width), BF16)
    return pl.pallas_call(
        functools.partial(last_kernel, chunks),
        in_specs=[vmem] * len(held),
        out_specs=[hbm] * 4 + [vmem],
        out_shape=[out] * 4 + [jax.ShapeDtypeStruct((width,), F32)],
        scratch_shapes=[
            rows(BF16), rows(BF16), pltpu.VMEM((2, HS, GL), F32), pltpu.SemaphoreType.DMA((4, chunks))
        ],
        compiler_params=pltpu.CompilerParams(vmem_limit_bytes=LAST_LIMIT),
        name="last",
    )(*held)


LOCAL_CUTS = (2, 6, 10)
GRAD_CUTS = (2, 6, 10)
VMEM_LIMIT = 33 * 1024 * 1024
LAST_LIMIT = 12 * 1024 * 1024


def solution(mesh):
    rows = P("ctx", "head")
    return jax.shard_map(
        functools.partial(body, mesh.shape["ctx"], mesh.shape["head"]),
        mesh=mesh,
        in_specs=(rows, rows, rows, rows, P("head"), rows),
        out_specs=(rows, rows, rows, rows, P("head")),
        check_vma=False,
    )
```

```python
import functools

import jax
import jax.numpy as jnp
from jax import lax
from jax.experimental import pallas as pl
from jax.experimental.pallas import tpu as pltpu
from jax.sharding import PartitionSpec as P

F32 = jnp.float32
BF16 = jnp.bfloat16
C = 128
HS = 96
GL = 384
PIECES = 3
OWNERS = HS // 8
NEG = -1e30
LOG2E = 1.4426950408889634
MESH = pl.DeviceIdType.MESH


def dot(a, b):
    return lax.dot_general(a, b, (((1,), (0,)), ((), ())), preferred_element_type=F32)


def dot_nt(a, b):
    return lax.dot_general(a, b, (((1,), (1,)), ((), ())), preferred_element_type=F32)


def both(hi, lo, w):
    r = dot(jnp.concatenate([hi, lo], axis=0), w)
    return r[: hi.shape[0]] + r[hi.shape[0] :]


def both_nt(hi, lo, w):
    r = dot_nt(jnp.concatenate([hi, lo], axis=0), w)
    return r[: hi.shape[0]] + r[hi.shape[0] :]


def split(x):
    hi = x.astype(BF16)
    lo = (x - hi.astype(F32)).astype(BF16)
    return hi, lo


def lane_mask(lo, hi, rows, dtype):
    lane = lax.broadcasted_iota(jnp.int32, (rows, 128), 1)
    return jnp.where((lane >= lo) & (lane < hi), 1.0, 0.0).astype(dtype)


def head_tiles(x, parity, dtype):
    rows = x.shape[0]
    t0, t1 = x[:, :128], x[:, 128:]
    zero = jnp.zeros((rows, 128), dtype)
    if parity == 0:
        a = [t0 * lane_mask(0, 96, rows, dtype), zero]
        b = [t0 * lane_mask(96, 128, rows, dtype), t1 * lane_mask(0, 64, rows, dtype)]
    else:
        a = [t0 * lane_mask(64, 128, rows, dtype), t1 * lane_mask(0, 32, rows, dtype)]
        b = [zero, t1 * lane_mask(32, 128, rows, dtype)]
    return jnp.concatenate(a, axis=1), jnp.concatenate(b, axis=1)


def stacked(x, parity):
    a, b = head_tiles(x, parity, x.dtype)
    return jnp.concatenate([a, b], axis=0)


def block_state(s, parity):
    a, b = head_tiles(s, parity, s.dtype)
    pad = jnp.zeros((64, 256), s.dtype)
    return jnp.concatenate([a, b, pad] if parity == 0 else [pad, a, b], axis=0)


def compact(u, parity):
    a, _ = head_tiles(u[:HS], parity, F32)
    _, b = head_tiles(u[HS:], parity, F32)
    return a + b


def merge(w0, w1):
    return jnp.concatenate([w0[:, :128], w0[:, 128:] + w1[:, :128], w1[:, 128:]], axis=1)


def group_lanes(cols):
    rows = cols[0].shape[0]
    lane = lax.broadcasted_iota(jnp.int32, (rows, 128), 1)
    return jnp.concatenate(
        [
            jnp.where(lane < 96, cols[0], cols[1]),
            jnp.where(lane < 64, cols[1], cols[2]),
            jnp.where(lane < 32, cols[2], cols[3]),
        ],
        axis=1,
    )


def columns_of(ct):
    full = jnp.concatenate([ct, jnp.zeros((C - 8, C), F32)], axis=0).T
    return [jnp.broadcast_to(full[:, h : h + 1], (C, C)) for h in range(8)]


def window(parity):
    return slice(128 * parity, 128 * parity + 256)


def causal_bias():
    row = lax.broadcasted_iota(jnp.int32, (C, C), 0)
    col = lax.broadcasted_iota(jnp.int32, (C, C), 1)
    return jnp.where(row >= col, 0.0, NEG)


def pair_decay(ct, cols, heads, bias):
    parts = [jnp.exp2(cols[h] - ct[h : h + 1, :] + bias) for h in heads]
    return jnp.concatenate(parts, axis=1)


def turned(x):
    return jnp.concatenate([x[:, :C].T, x[:, C:].T], axis=1)


def token_sums(x):
    acc = x[:, :128]
    for i in range(1, 6):
        acc = acc + x[:, 128 * i : 128 * i + 128]
    return jnp.sum(acc.T, axis=0, keepdims=True)


def wait_bytes(ref, sem):
    pltpu.make_async_copy(ref, ref, sem).wait()


def owner_of(chip):
    y, x = chip // 4, lax.rem(chip, 4)
    return 3 * y + jnp.minimum(lax.rem(x - y + 3, 4), 2), lax.rem(x - y + 4, 4) != 0


class Scan:
    def __init__(self, chips, me, reverse, tots, refs):
        self.chips, self.reverse, self.tots = chips, reverse, tots
        self.swap, self.swapped, self.send, self.taken, self.made, self.given = refs[:6]
        self.turn, self.turned, self.sems = refs[6:]
        self.chip, self.core = me // 2, lax.rem(me, 2)
        self.mine, self.is_owner = owner_of(self.chip)

    def other_core(self, src, dst, j):
        return pltpu.make_async_remote_copy(
            src_ref=src, dst_ref=dst, send_sem=self.sems.at[j], recv_sem=self.sems.at[j + 1],
            device_id={"ctx": 2 * self.chip + 1 - self.core}, device_id_type=MESH,
        )

    def other_chip(self, src, dst, j, chip):
        return pltpu.make_async_remote_copy(
            src_ref=src, dst_ref=dst, send_sem=self.sems.at[j], recv_sem=self.sems.at[j + 1],
            device_id={"ctx": 2 * chip + self.core}, device_id_type=MESH,
        )

    def start(self, state_ref, extra):
        self.swap[:HS, :] = state_ref[1 - self.core]
        self.swap[HS:, :] = extra
        self.other_core(self.swap, self.swapped, 0).start()

    def combine(self, state_ref, extra):
        self.other_core(self.swap, self.swapped, 0).wait_recv()
        low = self.core == 0
        mine, theirs = state_ref[self.core], self.swapped[:HS, :]
        a, b = jnp.where(low, mine, theirs), jnp.where(low, theirs, mine)
        ea, eb = jnp.where(low, extra, self.swapped[HS:, :]), jnp.where(low, self.swapped[HS:, :], extra)
        if self.reverse:
            both_cores = a + jnp.exp2(self.tots[0, 0:1, :]) * b
            tile = (ea + eb)[:, :128]
            self.turn[...] = b
        else:
            self.tots[0] = ea
            self.tots[1] = eb
            both_cores = jnp.exp2(eb[0:1, :]) * a + b
            total = ea[0:1, :] + eb[0:1, :]
            tile = jnp.concatenate(
                [total[:, 128 * i : 128 * i + 128] for i in range(3)] + [jnp.zeros((5, 128), F32)], axis=0
            )
            self.turn[...] = a
        for r in range(OWNERS):
            self.send[r, :, :GL] = both_cores[8 * r : 8 * r + 8]
            self.send[r, :, GL:] = tile

        @pl.loop(1, self.chips)
        def _(i):
            chip = lax.rem(self.chip + i, self.chips)
            r, owns = owner_of(chip)

            @pl.when(owns)
            def _():
                self.other_chip(self.send.at[r], self.taken.at[self.chip], 2, chip).start()

    def middle(self, totals):
        chips, chip, mine = self.chips, self.chip, self.mine

        @pl.when(self.is_owner)
        def _():
            self.taken[chip] = self.send[mine]
            wait_bytes(self.taken.at[pl.ds(0, chips - 1)], self.sems.at[3])

            def step(i, carry):
                acc, tile = carry
                j = chips - 1 - i if self.reverse else i
                self.made[j, :, :GL] = acc
                total = jnp.concatenate([totals[j, t : t + 1, GL:] for t in range(3)], axis=1)
                if self.reverse:
                    tile = tile + self.taken[j, :, GL:]
                return jnp.exp2(total) * acc + self.taken[j, :, :GL], tile

            _, tile = lax.fori_loop(
                0, chips, step, (jnp.zeros((8, GL), F32), jnp.zeros((8, 128), F32)), unroll=16
            )
            if self.reverse:
                for j in range(chips):
                    self.made[j, :, GL:] = tile

            @pl.loop(1, chips)
            def _(i):
                to = lax.rem(chip + i, chips)
                self.other_chip(self.made.at[to], self.given.at[mine], 4, to).start()

            self.given[mine] = self.made[chip]

    def gather(self, keep):
        @pl.when(self.is_owner)
        def _():
            wait_bytes(self.given.at[pl.ds(0, OWNERS - 1)], self.sems.at[5])
            wait_bytes(self.send.at[pl.ds(0, OWNERS - 1)], self.sems.at[2])
            wait_bytes(self.made.at[pl.ds(0, self.chips - 1)], self.sems.at[4])

        @pl.when(jnp.logical_not(self.is_owner))
        def _():
            wait_bytes(self.given, self.sems.at[5])
            wait_bytes(self.send, self.sems.at[2])

        low = self.core == 0
        outer = jnp.concatenate([self.given[r, :, :GL] for r in range(OWNERS)], axis=0)
        if self.reverse:
            inner = self.turn[...] + jnp.exp2(self.tots[1, 0:1, :]) * outer
            mine, theirs = jnp.where(low, inner, outer), jnp.where(low, outer, inner)
        else:
            inner = self.turn[...] + jnp.exp2(self.tots[0, 0:1, :]) * outer
            mine, theirs = jnp.where(low, outer, inner), jnp.where(low, inner, outer)
        keep[self.core] = mine
        self.turn[...] = theirs
        self.other_core(self.turn, self.turned, 6).start()

    def finish(self, keep):
        self.other_core(self.turn, self.turned, 6).wait()
        self.other_core(self.swap, self.swapped, 0).wait_send()
        keep[1 - self.core] = self.turned[...]


def rows_of(i):
    return pl.ds(pl.multiple_of(i * C, C), C)


groups = [slice(GL * g, GL * (g + 1)) for g in range(2)]


def layer_kernel(
    shards, head_shards, total_width, chunks, q_in, k_in, v_in, do_in, gain_in, ld_ref,
    out_ref, dq_ref, k_s, v_s, att_s, dv_s, u_s, cexp_s, run_s, dgain_ref,
    q_s, do_s, in_sems, ct_s, shi_s, slo_s, ghi_s, glo_s, phi_s, plo_s,
    own_s, tot_s, start_s, dg_s, gain_ref, sums_s, sums_t, sums_sems,
    qt_s, tots_s, *scan_refs,
):
    remote = shards > 1
    dk_s = att_s
    if remote:
        me, my_head = lax.axis_index("ctx"), lax.axis_index("head")
        chips = shards // 2
        core = lax.rem(me, 2)
        on = Scan(chips, me, False, tots_s, scan_refs[:9])
        back = Scan(chips, me, True, tots_s, scan_refs[9:])
        barrier = pltpu.get_barrier_semaphore()
        pl.semaphore_signal(
            barrier, inc=1, device_id={"ctx": me + 1 - 2 * core}, device_id_type=MESH
        )

        @pl.loop(1, chips)
        def _(i):
            pl.semaphore_signal(
                barrier, inc=1, device_id={"ctx": lax.rem(me + 2 * i, shards)}, device_id_type=MESH
            )

        @pl.loop(1, head_shards)
        def _(i):
            pl.semaphore_signal(
                barrier, inc=1, device_id={"head": lax.rem(my_head + i, head_shards)},
                device_id_type=MESH,
            )

    per = chunks // PIECES
    inputs = [(k_in, k_s), (v_in, v_s), (q_in, q_s), (do_in, do_s)]

    def arrival(a, b):
        rows = pl.ds(pl.multiple_of(b * per * C, per * C), per * C)
        return pltpu.make_async_copy(inputs[a][0].at[rows], inputs[a][1].at[rows], in_sems.at[a, b])

    for b in range(PIECES):
        arrival(0, b).start()
        arrival(1, b).start()
    for a in (2, 3):
        for b in range(PIECES):
            arrival(a, b).start()
    for j in range(gain_ref.shape[1] // 128):
        gain_ref[:, 128 * j : 128 * j + 128] = gain_in[128 * j : 128 * j + 128].reshape(1, 128)

    row = lax.broadcasted_iota(jnp.int32, (C, C), 0)
    col = lax.broadcasted_iota(jnp.int32, (C, C), 1)
    upper = jnp.where(row <= col, 1.0, 0.0)
    ct_s[...] = LOG2E * lax.dot_general(
        ld_ref[...], upper, (((1,), (0,)), ((), ())), preferred_element_type=F32,
        precision=lax.Precision.HIGHEST,
    )
    own_s[...] = jnp.zeros_like(own_s)
    tot_s[...] = jnp.zeros_like(tot_s)

    def ct_of(i):
        return ct_s[pl.ds(pl.multiple_of(i * 8, 8), 8), :]

    def exponents(i):
        rows = rows_of(i)
        ct = ct_of(i)
        tot_s[...] += jnp.broadcast_to(ct[:, C - 1 : C], (8, 128))
        cols = columns_of(ct)
        for g, lanes in enumerate(groups):
            cexp_s[rows, lanes] = group_lanes(cols[4 * g : 4 * g + 4])

    def states(i):
        rows = rows_of(i)
        for g, lanes in enumerate(groups):
            cexp = cexp_s[rows, lanes]
            end = cexp[C - 1 : C, :]
            v_hi, v_lo = split(v_s[rows, lanes].astype(F32) * jnp.exp2(end - cexp))
            v_tail = jnp.concatenate([v_hi, v_lo], axis=0)
            kt = k_s[rows, lanes].T
            parts = []
            for p in range(2):
                kp = kt[192 * p : 192 * p + 192]
                parts.append(compact(dot(jnp.concatenate([kp, kp], axis=1), v_tail[:, window(p)]), p))
            u = merge(*parts)
            u_s[i, :, lanes] = u
            own_s[g] = jnp.exp2(end) * own_s[g] + u

    def local_rows(i):
        rows = rows_of(i)
        ct = ct_of(i)
        cols = columns_of(ct)
        bias = causal_bias()
        for g, lanes in enumerate(groups):
            q, k, v = q_s[rows, lanes], k_s[rows, lanes], v_s[rows, lanes]
            qt_s[i, lanes, :] = q.T
            outs = []
            for p in range(2):
                w = window(p)
                heads = (4 * g + 2 * p, 4 * g + 2 * p + 1)
                scores = dot_nt(q[:, w], stacked(k[:, w], p)) * pair_decay(ct, cols, heads, bias)
                hi, lo = split(scores)
                vs = stacked(v[:, w], p)
                outs.append(dot(hi, vs) + dot(lo, vs))
                pair = slice(256 * (2 * g + p), 256 * (2 * g + p) + 256)
                phi_s[rows, pair] = turned(hi)
                plo_s[rows, pair] = turned(lo)
            att_s[rows, lanes] = merge(*outs)

    def whole_rows(i):
        rows = rows_of(i)
        for g, lanes in enumerate(groups):
            q = q_s[rows, lanes]
            cexp = cexp_s[rows, lanes]
            end = cexp[C - 1 : C, :]
            s = run_s[g]
            s_hi, s_lo = split(s)
            shi_s[i, :, lanes] = s_hi
            slo_s[i, :, lanes] = s_lo
            outs = []
            for p in range(2):
                w = window(p)
                outs.append(dot(q[:, w], block_state(s_hi[:, w], p)) + dot(q[:, w], block_state(s_lo[:, w], p)))
            att_s[rows, lanes] += jnp.exp2(cexp) * merge(*outs)
            run_s[g] = jnp.exp2(end) * s + u_s[i, :, lanes]
        att = att_s[rows, :]
        grown = do_s[rows, :].astype(F32) * gain_ref[...]
        sums_s[i] = jnp.concatenate(
            [token_sums(att * att), token_sums(grown * att), jnp.zeros((6, C), F32)], axis=0
        )

    def sums_copy(b, target):
        part = pl.ds(b * per, per)
        return pltpu.make_async_remote_copy(
            src_ref=sums_s.at[part], dst_ref=sums_t.at[my_head, part], send_sem=sums_sems.at[0, b],
            recv_sem=sums_sems.at[1, b], device_id={"head": target}, device_id_type=MESH,
        )

    def norm_rows(i):
        rows = rows_of(i)
        if remote:
            sums = sums_t[0, i]
            for j in range(1, head_shards):
                sums = sums + sums_t[j, i]
        else:
            sums = sums_s[i]
        rms = jnp.sqrt(sums[0:1, :] / total_width + 1e-06)
        inv = 1.0 / rms
        mean = sums[1:2, :] * inv / total_width
        inv_c = jnp.broadcast_to(inv, (C, C)).T
        coef_c = jnp.broadcast_to(mean * inv * inv, (C, C)).T
        inv_c = jnp.concatenate([inv_c] * 3, axis=1)
        coef_c = jnp.concatenate([coef_c] * 3, axis=1)
        for g, lanes in enumerate(groups):
            att = att_s[rows, lanes]
            up = do_s[rows, lanes].astype(F32)
            gain = gain_ref[:, lanes]
            normed = att * inv_c
            out_ref[rows, lanes] = (normed * gain).astype(BF16)
            dg_s[:, lanes] += jnp.sum((up * normed).reshape(C // 8, 8, GL), axis=0)
            grad = up * gain * inv_c - att * coef_c
            g_hi, g_lo = split(grad)
            ghi_s[rows, lanes] = g_hi
            glo_s[rows, lanes] = g_lo
            cexp = cexp_s[rows, lanes]
            end = cexp[C - 1 : C, :]
            e_hi, e_lo = split(grad * jnp.exp2(cexp))
            e_both = jnp.concatenate([e_hi, e_lo], axis=0)
            qt = qt_s[i, lanes, :]
            parts = []
            for p in range(2):
                qp = qt[192 * p : 192 * p + 192]
                parts.append(compact(dot(jnp.concatenate([qp, qp], axis=1), e_both[:, window(p)]), p))
            w = merge(*parts)
            u_s[i, :, lanes] = w
            own_s[g] += jnp.exp2(start_s[0:1, lanes]) * w
            start_s[0:1, lanes] += end

    def grad_rows(i):
        rows = rows_of(i)
        ct = ct_of(i)
        cols = columns_of(ct)
        bias = causal_bias()
        for g, lanes in enumerate(groups):
            q, k, v = q_s[rows, lanes], k_s[rows, lanes], v_s[rows, lanes]
            g_hi, g_lo = ghi_s[rows, lanes], glo_s[rows, lanes]
            from_start = jnp.exp2(cexp_s[rows, lanes])
            s_hi, s_lo = shi_s[i, :, lanes], slo_s[i, :, lanes]
            dqs, olds, dks, dvs = [], [], [], []
            for p in range(2):
                w = window(p)
                heads = (4 * g + 2 * p, 4 * g + 2 * p + 1)
                pair = slice(256 * (2 * g + p), 256 * (2 * g + p) + 256)
                hw, lw = g_hi[:, w], g_lo[:, w]
                hs, ls = stacked(hw, p), stacked(lw, p)
                decay = pair_decay(ct, cols, heads, bias)
                b_hi, b_lo = block_state(s_hi[:, w], p), block_state(s_lo[:, w], p)
                d_hi, d_lo = split(both_nt(hw, lw, stacked(v[:, w], p)) * decay)
                ks = stacked(k[:, w], p)
                dqs.append(dot(d_hi, ks) + dot(d_lo, ks))
                olds.append(both_nt(hw, lw, b_hi) + dot_nt(hw, b_lo))
                dks.append(both(turned(d_hi), turned(d_lo), stacked(q[:, w], p)))
                p_hi, p_lo = phi_s[rows, pair], plo_s[rows, pair]
                dvs.append(both(p_hi, p_lo, hs) + dot(p_hi, ls))
            dq_ref[rows, lanes] = (merge(*dqs) + from_start * merge(*olds)).astype(BF16)
            dk_s[rows, lanes] = merge(*dks)
            dv_s[rows, lanes] = merge(*dvs)

    def over(lo, hi, f):
        pl.loop(lo, hi, unroll=2 if (hi - lo) % 2 == 0 else 1)(f)

    def piece(b, f):
        pl.loop(0, per, unroll=per)(lambda j: f(b * per + j))

    pl.loop(0, PIECES)(lambda b: piece(b, exponents))

    @pl.loop(0, PIECES)
    def _(b):
        arrival(0, b).wait()
        arrival(1, b).wait()
        piece(b, states)

    totals = [
        group_lanes([jnp.broadcast_to(tot_s[h : h + 1, :], (8, 128)) for h in range(4 * g, 4 * g + 4)])
        for g in range(2)
    ]
    if remote:
        low = core == 0
        own_total, other_total = jnp.where(low, *totals), jnp.where(low, *totals[::-1])
        pl.semaphore_wait(barrier, chips + head_shards - 1)
        on.start(own_s, other_total)
    for b in range(PIECES):
        arrival(2, b).wait()
        arrival(3, b).wait()
    cuts = [chunks * c // 12 for c in LOCAL_CUTS]
    over(0, cuts[0], local_rows)
    if remote:
        on.combine(own_s, own_total)
    over(cuts[0], cuts[1], local_rows)
    if remote:
        on.middle(on.taken)
    over(cuts[1], cuts[2], local_rows)
    if remote:
        on.gather(run_s)
    over(cuts[2], chunks, local_rows)
    if remote:
        on.finish(run_s)
    else:
        run_s[...] = jnp.zeros_like(run_s)
    @pl.loop(0, PIECES)
    def _(b):
        piece(b, whole_rows)
        if remote:
            part = pl.ds(b * per, per)
            sums_t[my_head, part] = sums_s[part]

            @pl.loop(1, head_shards)
            def _(i):
                sums_copy(b, lax.rem(my_head + i, head_shards)).start()

    own_s[...] = jnp.zeros_like(own_s)
    start_s[...] = jnp.zeros_like(start_s)
    dg_s[...] = jnp.zeros_like(dg_s)

    @pl.loop(0, PIECES)
    def _(b):
        if remote:
            moved = sums_t.at[pl.ds(0, head_shards - 1), pl.ds(b * per, per)]
            wait_bytes(moved, sums_sems.at[1, b])
            wait_bytes(moved, sums_sems.at[0, b])
        piece(b, norm_rows)

    sums = jnp.sum(dg_s[...], axis=0, keepdims=True)
    tile = jnp.concatenate(
        [sums[:, 128 * i : 128 * i + 128] for i in range(6)] + [jnp.zeros((2, 128), F32)], axis=0
    )
    cuts = [chunks * c // 12 for c in GRAD_CUTS]
    if remote:
        tile = jnp.concatenate([tile, jnp.zeros((8, GL - 128), F32)], axis=1)
        back.start(own_s, tile)
    over(0, cuts[0], grad_rows)
    if remote:
        back.combine(own_s, tile)
    over(cuts[0], cuts[1], grad_rows)
    if remote:
        back.middle(on.taken)
    over(cuts[1], cuts[2], grad_rows)
    if remote:
        back.gather(run_s)
        dgain_ref[...] = back.given[0, :, GL:]
    over(cuts[2], chunks, grad_rows)
    if remote:
        back.finish(run_s)
    else:
        dgain_ref[...] = tile
        run_s[...] = jnp.zeros_like(run_s)


def last_kernel(
    chunks, out_v, dq_v, k_s, v_s, dk_s, dv_s, u_s, cexp_s, state_ref, dgain_v,
    out_hbm, dq_hbm, dk_hbm, dv_hbm, dgain_ref, dk_ref, dv_ref, run_s, sems,
):
    first = [(out_v, out_hbm), (dq_v, dq_hbm)]
    for j, (src, dst) in enumerate(first):
        pltpu.make_async_copy(src, dst, sems.at[j, 0]).start()
    for j in range(dgain_ref.shape[0] // 128):
        dgain_ref[128 * j : 128 * j + 128] = dgain_v[j : j + 1, :].reshape(128)
    run_s[...] = state_ref[...]

    def copies(i):
        rows = rows_of(i)
        return [
            pltpu.make_async_copy(src.at[rows], dst.at[rows], sems.at[2 + j, i])
            for j, (src, dst) in enumerate([(dk_ref, dk_hbm), (dv_ref, dv_hbm)])
        ]

    def last_rows(i):
        rows = rows_of(i)
        for g, lanes in enumerate(groups):
            k, v = k_s[rows, lanes], v_s[rows, lanes]
            cexp = cexp_s[rows, lanes]
            end = cexp[C - 1 : C, :]
            tail = jnp.exp2(end - cexp)
            s = run_s[g]
            s_hi, s_lo = split(s)
            dks, dvs = [], []
            for p in range(2):
                w = window(p)
                b_hi, b_lo = block_state(s_hi[:, w], p), block_state(s_lo[:, w], p)
                dks.append(dot_nt(v[:, w], b_hi) + dot_nt(v[:, w], b_lo))
                dvs.append(dot(k[:, w], b_hi) + dot(k[:, w], b_lo))
            dk_ref[rows, lanes] = (dk_s[rows, lanes] + tail * merge(*dks)).astype(BF16)
            dv_ref[rows, lanes] = (dv_s[rows, lanes] + tail * merge(*dvs)).astype(BF16)
            run_s[g] = jnp.exp2(end) * s + u_s[i, :, lanes]
        for copy in copies(i):
            copy.start()

    pl.loop(0, chunks, unroll=3)(lambda i: last_rows(chunks - 1 - i))
    for j, (src, dst) in enumerate(first):
        pltpu.make_async_copy(src, dst, sems.at[j, 0]).wait()

    @pl.loop(0, chunks)
    def _(i):
        for copy in copies(i):
            copy.wait()


def body(shards, head_shards, queries, keys, values, log_decay, gain, d_out):
    n, width = queries.shape
    chunks = n // C
    ld_t = log_decay.reshape(chunks, C, 8).transpose(0, 2, 1).reshape(chunks * 8, C)
    hbm, vmem = pl.BlockSpec(memory_space=pl.ANY), pl.BlockSpec(memory_space=pltpu.VMEM)
    rows = lambda dtype: pltpu.VMEM((n, width), dtype)
    chips = max(shards // 2, 1)
    scan = lambda sent: [
        pltpu.VMEM((HS + 8, GL), F32),
        pltpu.VMEM((HS + 8, GL), F32),
        pltpu.VMEM((OWNERS, 8, 512), F32),
        pltpu.VMEM((chips, 8, 512), F32),
        pltpu.VMEM((chips, 8, sent), F32),
        pltpu.VMEM((OWNERS, 8, sent), F32),
        pltpu.VMEM((HS, GL), F32),
        pltpu.VMEM((HS, GL), F32),
        pltpu.SemaphoreType.DMA((8,)),
    ]
    scratch = [
        rows(BF16), rows(BF16),
        pltpu.SemaphoreType.DMA((4, PIECES)),
        pltpu.VMEM((chunks * 8, C), F32),
        pltpu.VMEM((chunks, HS, width), BF16),
        pltpu.VMEM((chunks, HS, width), BF16),
        rows(BF16), rows(BF16),
        pltpu.VMEM((n, 1024), BF16), pltpu.VMEM((n, 1024), BF16),
        pltpu.VMEM((2, HS, GL), F32),
        pltpu.VMEM((8, 128), F32),
        pltpu.VMEM((8, width), F32),
        pltpu.VMEM((8, width), F32),
        pltpu.VMEM((1, width), F32),
        pltpu.VMEM((chunks, 8, C), F32),
        pltpu.VMEM((head_shards, chunks, 8, C), F32),
        pltpu.SemaphoreType.DMA((2, PIECES)),
        pltpu.VMEM((chunks, width, C), BF16),
        pltpu.VMEM((2, 8, GL), F32),
    ] + scan(GL) + scan(512)
    params = dict(vmem_limit_bytes=VMEM_LIMIT)
    if shards > 1:
        params.update(collective_id=0, has_side_effects=True)
    held = [rows(BF16)] * 4 + [
        rows(F32), rows(F32), pltpu.VMEM((chunks, HS, width), F32), rows(F32),
        pltpu.VMEM((2, HS, GL), F32), pltpu.VMEM((8, 128), F32),
    ]
    held = pl.pallas_call(
        functools.partial(
            layer_kernel, shards, head_shards, float(width * head_shards), chunks
        ),
        in_specs=[hbm] * 4 + [vmem, vmem],
        out_specs=[vmem] * len(held),
        out_shape=held,
        scratch_shapes=scratch,
        compiler_params=pltpu.CompilerParams(**params),
        name="layer",
    )(queries, keys, values, d_out, gain, ld_t)
    out = jax.ShapeDtypeStruct((n, width), BF16)
    return pl.pallas_call(
        functools.partial(last_kernel, chunks),
        in_specs=[vmem] * len(held),
        out_specs=[hbm] * 4 + [vmem],
        out_shape=[out] * 4 + [jax.ShapeDtypeStruct((width,), F32)],
        scratch_shapes=[
            rows(BF16), rows(BF16), pltpu.VMEM((2, HS, GL), F32), pltpu.SemaphoreType.DMA((4, chunks))
        ],
        compiler_params=pltpu.CompilerParams(vmem_limit_bytes=LAST_LIMIT),
        name="last",
    )(*held)


LOCAL_CUTS = (2, 6, 10)
GRAD_CUTS = (2, 6, 10)
VMEM_LIMIT = 35 * 1024 * 1024
LAST_LIMIT = 12 * 1024 * 1024


def solution(mesh):
    rows = P("ctx", "head")
    return jax.shard_map(
        functools.partial(body, mesh.shape["ctx"], mesh.shape["head"]),
        mesh=mesh,
        in_specs=(rows, rows, rows, rows, P("head"), rows),
        out_specs=(rows, rows, rows, rows, P("head")),
        check_vma=False,
    )
```

```python
import functools

import jax
import jax.numpy as jnp
from jax import lax
from jax.experimental import pallas as pl
from jax.experimental.pallas import tpu as pltpu
from jax.sharding import PartitionSpec as P

F32 = jnp.float32
BF16 = jnp.bfloat16
C = 128
HS = 96
GL = 384
PIECES = 3
OWNERS = HS // 8
NEG = -1e30
LOG2E = 1.4426950408889634
MESH = pl.DeviceIdType.MESH


def dot(a, b):
    return lax.dot_general(a, b, (((1,), (0,)), ((), ())), preferred_element_type=F32)


def dot_nt(a, b):
    return lax.dot_general(a, b, (((1,), (1,)), ((), ())), preferred_element_type=F32)


def both(hi, lo, w):
    r = dot(jnp.concatenate([hi, lo], axis=0), w)
    return r[: hi.shape[0]] + r[hi.shape[0] :]


def both_nt(hi, lo, w):
    r = dot_nt(jnp.concatenate([hi, lo], axis=0), w)
    return r[: hi.shape[0]] + r[hi.shape[0] :]


def split(x):
    hi = x.astype(BF16)
    lo = (x - hi.astype(F32)).astype(BF16)
    return hi, lo


def lane_mask(lo, hi, rows, dtype):
    lane = lax.broadcasted_iota(jnp.int32, (rows, 128), 1)
    return jnp.where((lane >= lo) & (lane < hi), 1.0, 0.0).astype(dtype)


def head_tiles(x, parity, dtype):
    rows = x.shape[0]
    t0, t1 = x[:, :128], x[:, 128:]
    zero = jnp.zeros((rows, 128), dtype)
    if parity == 0:
        a = [t0 * lane_mask(0, 96, rows, dtype), zero]
        b = [t0 * lane_mask(96, 128, rows, dtype), t1 * lane_mask(0, 64, rows, dtype)]
    else:
        a = [t0 * lane_mask(64, 128, rows, dtype), t1 * lane_mask(0, 32, rows, dtype)]
        b = [zero, t1 * lane_mask(32, 128, rows, dtype)]
    return jnp.concatenate(a, axis=1), jnp.concatenate(b, axis=1)


def stacked(x, parity):
    a, b = head_tiles(x, parity, x.dtype)
    return jnp.concatenate([a, b], axis=0)


def block_state(s, parity):
    a, b = head_tiles(s, parity, s.dtype)
    pad = jnp.zeros((64, 256), s.dtype)
    return jnp.concatenate([a, b, pad] if parity == 0 else [pad, a, b], axis=0)


def compact(u, parity):
    a, _ = head_tiles(u[:HS], parity, F32)
    _, b = head_tiles(u[HS:], parity, F32)
    return a + b


def merge(w0, w1):
    return jnp.concatenate([w0[:, :128], w0[:, 128:] + w1[:, :128], w1[:, 128:]], axis=1)


def group_lanes(cols):
    rows = cols[0].shape[0]
    lane = lax.broadcasted_iota(jnp.int32, (rows, 128), 1)
    return jnp.concatenate(
        [
            jnp.where(lane < 96, cols[0], cols[1]),
            jnp.where(lane < 64, cols[1], cols[2]),
            jnp.where(lane < 32, cols[2], cols[3]),
        ],
        axis=1,
    )


def columns_of(ct):
    full = jnp.concatenate([ct, jnp.zeros((C - 8, C), F32)], axis=0).T
    return [jnp.broadcast_to(full[:, h : h + 1], (C, C)) for h in range(8)]


def window(parity):
    return slice(128 * parity, 128 * parity + 256)


def causal_bias():
    row = lax.broadcasted_iota(jnp.int32, (C, C), 0)
    col = lax.broadcasted_iota(jnp.int32, (C, C), 1)
    return jnp.where(row >= col, 0.0, NEG)


def pair_decay(ct, cols, heads, bias):
    parts = [jnp.exp2(cols[h] - ct[h : h + 1, :] + bias) for h in heads]
    return jnp.concatenate(parts, axis=1)


def turned(x):
    return jnp.concatenate([x[:, :C].T, x[:, C:].T], axis=1)


def token_sums(x):
    acc = x[:, :128]
    for i in range(1, 6):
        acc = acc + x[:, 128 * i : 128 * i + 128]
    return jnp.sum(acc.T, axis=0, keepdims=True)


def wait_bytes(ref, sem):
    pltpu.make_async_copy(ref, ref, sem).wait()


def owner_of(chip):
    y, x = chip // 4, lax.rem(chip, 4)
    return 3 * y + jnp.minimum(lax.rem(x - y + 3, 4), 2), lax.rem(x - y + 4, 4) != 0


class Scan:
    def __init__(self, chips, me, reverse, tots, refs):
        self.chips, self.reverse, self.tots = chips, reverse, tots
        self.swap, self.swapped, self.send, self.taken, self.made, self.given = refs[:6]
        self.turn, self.turned, self.sems = refs[6:]
        self.chip, self.core = me // 2, lax.rem(me, 2)
        self.mine, self.is_owner = owner_of(self.chip)

    def other_core(self, src, dst, j):
        return pltpu.make_async_remote_copy(
            src_ref=src, dst_ref=dst, send_sem=self.sems.at[j], recv_sem=self.sems.at[j + 1],
            device_id={"ctx": 2 * self.chip + 1 - self.core}, device_id_type=MESH,
        )

    def other_chip(self, src, dst, j, chip):
        return pltpu.make_async_remote_copy(
            src_ref=src, dst_ref=dst, send_sem=self.sems.at[j], recv_sem=self.sems.at[j + 1],
            device_id={"ctx": 2 * chip + self.core}, device_id_type=MESH,
        )

    def start(self, state_ref, extra):
        self.swap[:HS, :] = state_ref[1 - self.core]
        self.swap[HS:, :] = extra
        self.other_core(self.swap, self.swapped, 0).start()

    def combine(self, state_ref, extra):
        self.other_core(self.swap, self.swapped, 0).wait_recv()
        low = self.core == 0
        mine, theirs = state_ref[self.core], self.swapped[:HS, :]
        a, b = jnp.where(low, mine, theirs), jnp.where(low, theirs, mine)
        ea, eb = jnp.where(low, extra, self.swapped[HS:, :]), jnp.where(low, self.swapped[HS:, :], extra)
        if self.reverse:
            both_cores = a + jnp.exp2(self.tots[0, 0:1, :]) * b
            tile = (ea + eb)[:, :128]
            self.turn[...] = b
        else:
            self.tots[0] = ea
            self.tots[1] = eb
            both_cores = jnp.exp2(eb[0:1, :]) * a + b
            total = ea[0:1, :] + eb[0:1, :]
            tile = jnp.concatenate(
                [total[:, 128 * i : 128 * i + 128] for i in range(3)] + [jnp.zeros((5, 128), F32)], axis=0
            )
            self.turn[...] = a
        for r in range(OWNERS):
            self.send[r, :, :GL] = both_cores[8 * r : 8 * r + 8]
            self.send[r, :, GL:] = tile

        @pl.loop(1, self.chips)
        def _(i):
            chip = lax.rem(self.chip + i, self.chips)
            r, owns = owner_of(chip)

            @pl.when(owns)
            def _():
                self.other_chip(self.send.at[r], self.taken.at[self.chip], 2, chip).start()

    def middle(self, totals):
        chips, chip, mine = self.chips, self.chip, self.mine

        @pl.when(self.is_owner)
        def _():
            self.taken[chip] = self.send[mine]
            wait_bytes(self.taken.at[pl.ds(0, chips - 1)], self.sems.at[3])

            def step(i, carry):
                acc, tile = carry
                j = chips - 1 - i if self.reverse else i
                self.made[j, :, :GL] = acc
                total = jnp.concatenate([totals[j, t : t + 1, GL:] for t in range(3)], axis=1)
                if self.reverse:
                    tile = tile + self.taken[j, :, GL:]
                return jnp.exp2(total) * acc + self.taken[j, :, :GL], tile

            _, tile = lax.fori_loop(
                0, chips, step, (jnp.zeros((8, GL), F32), jnp.zeros((8, 128), F32)), unroll=16
            )
            if self.reverse:
                for j in range(chips):
                    self.made[j, :, GL:] = tile

            @pl.loop(1, chips)
            def _(i):
                to = lax.rem(chip + i, chips)
                self.other_chip(self.made.at[to], self.given.at[mine], 4, to).start()

            self.given[mine] = self.made[chip]

    def gather(self, keep):
        @pl.when(self.is_owner)
        def _():
            wait_bytes(self.given.at[pl.ds(0, OWNERS - 1)], self.sems.at[5])
            wait_bytes(self.send.at[pl.ds(0, OWNERS - 1)], self.sems.at[2])
            wait_bytes(self.made.at[pl.ds(0, self.chips - 1)], self.sems.at[4])

        @pl.when(jnp.logical_not(self.is_owner))
        def _():
            wait_bytes(self.given, self.sems.at[5])
            wait_bytes(self.send, self.sems.at[2])

        low = self.core == 0
        outer = jnp.concatenate([self.given[r, :, :GL] for r in range(OWNERS)], axis=0)
        if self.reverse:
            inner = self.turn[...] + jnp.exp2(self.tots[1, 0:1, :]) * outer
            mine, theirs = jnp.where(low, inner, outer), jnp.where(low, outer, inner)
        else:
            inner = self.turn[...] + jnp.exp2(self.tots[0, 0:1, :]) * outer
            mine, theirs = jnp.where(low, outer, inner), jnp.where(low, inner, outer)
        keep[self.core] = mine
        self.turn[...] = theirs
        self.other_core(self.turn, self.turned, 6).start()

    def finish(self, keep):
        self.other_core(self.turn, self.turned, 6).wait()
        self.other_core(self.swap, self.swapped, 0).wait_send()
        keep[1 - self.core] = self.turned[...]


def rows_of(i):
    return pl.ds(pl.multiple_of(i * C, C), C)


groups = [slice(GL * g, GL * (g + 1)) for g in range(2)]


def layer_kernel(
    shards, head_shards, total_width, chunks, q_in, k_in, v_in, do_in, gain_in, ld_ref,
    out_ref, dq_ref, k_s, v_s, att_s, dv_s, u_s, cexp_s, run_s, dgain_ref,
    q_s, do_s, in_sems, ct_s, shi_s, slo_s, ghi_s, glo_s, phi_s, plo_s,
    own_s, tot_s, start_s, dg_s, gain_ref, sums_s, sums_t, sums_sems,
    qt_s, tots_s, *scan_refs,
):
    remote = shards > 1
    dk_s = att_s
    if remote:
        me, my_head = lax.axis_index("ctx"), lax.axis_index("head")
        chips = shards // 2
        core = lax.rem(me, 2)
        on = Scan(chips, me, False, tots_s, scan_refs[:9])
        back = Scan(chips, me, True, tots_s, scan_refs[9:])
        barrier = pltpu.get_barrier_semaphore()
        pl.semaphore_signal(
            barrier, inc=1, device_id={"ctx": me + 1 - 2 * core}, device_id_type=MESH
        )

        @pl.loop(1, chips)
        def _(i):
            pl.semaphore_signal(
                barrier, inc=1, device_id={"ctx": lax.rem(me + 2 * i, shards)}, device_id_type=MESH
            )

        @pl.loop(1, head_shards)
        def _(i):
            pl.semaphore_signal(
                barrier, inc=1, device_id={"head": lax.rem(my_head + i, head_shards)},
                device_id_type=MESH,
            )

    per = chunks // PIECES
    inputs = [(k_in, k_s), (v_in, v_s), (q_in, q_s), (do_in, do_s)]

    def arrival(a, b):
        rows = pl.ds(pl.multiple_of(b * per * C, per * C), per * C)
        return pltpu.make_async_copy(inputs[a][0].at[rows], inputs[a][1].at[rows], in_sems.at[a, b])

    for b in range(PIECES):
        arrival(0, b).start()
        arrival(1, b).start()
    for a in (2, 3):
        for b in range(PIECES):
            arrival(a, b).start()
    for j in range(gain_ref.shape[1] // 128):
        gain_ref[:, 128 * j : 128 * j + 128] = gain_in[128 * j : 128 * j + 128].reshape(1, 128)

    row = lax.broadcasted_iota(jnp.int32, (C, C), 0)
    col = lax.broadcasted_iota(jnp.int32, (C, C), 1)
    upper = jnp.where(row <= col, 1.0, 0.0)
    ct_s[...] = LOG2E * lax.dot_general(
        ld_ref[...], upper, (((1,), (0,)), ((), ())), preferred_element_type=F32,
        precision=lax.Precision.HIGHEST,
    )
    own_s[...] = jnp.zeros_like(own_s)
    tot_s[...] = jnp.zeros_like(tot_s)

    def ct_of(i):
        return ct_s[pl.ds(pl.multiple_of(i * 8, 8), 8), :]

    def exponents(i):
        rows = rows_of(i)
        ct = ct_of(i)
        tot_s[...] += jnp.broadcast_to(ct[:, C - 1 : C], (8, 128))
        cols = columns_of(ct)
        for g, lanes in enumerate(groups):
            cexp_s[rows, lanes] = group_lanes(cols[4 * g : 4 * g + 4])

    def states(i):
        rows = rows_of(i)
        for g, lanes in enumerate(groups):
            cexp = cexp_s[rows, lanes]
            end = cexp[C - 1 : C, :]
            v_hi, v_lo = split(v_s[rows, lanes].astype(F32) * jnp.exp2(end - cexp))
            v_tail = jnp.concatenate([v_hi, v_lo], axis=0)
            kt = k_s[rows, lanes].T
            parts = []
            for p in range(2):
                kp = kt[192 * p : 192 * p + 192]
                parts.append(compact(dot(jnp.concatenate([kp, kp], axis=1), v_tail[:, window(p)]), p))
            u = merge(*parts)
            u_s[i, :, lanes] = u
            own_s[g] = jnp.exp2(end) * own_s[g] + u

    def local_rows(i):
        rows = rows_of(i)
        ct = ct_of(i)
        cols = columns_of(ct)
        bias = causal_bias()
        for g, lanes in enumerate(groups):
            q, k, v = q_s[rows, lanes], k_s[rows, lanes], v_s[rows, lanes]
            qt_s[i, lanes, :] = q.T
            outs = []
            for p in range(2):
                w = window(p)
                heads = (4 * g + 2 * p, 4 * g + 2 * p + 1)
                scores = dot_nt(q[:, w], stacked(k[:, w], p)) * pair_decay(ct, cols, heads, bias)
                hi, lo = split(scores)
                vs = stacked(v[:, w], p)
                outs.append(dot(hi, vs) + dot(lo, vs))
                pair = slice(256 * (2 * g + p), 256 * (2 * g + p) + 256)
                phi_s[rows, pair] = turned(hi)
                plo_s[rows, pair] = turned(lo)
            att_s[rows, lanes] = merge(*outs)

    def whole_rows(i):
        rows = rows_of(i)
        for g, lanes in enumerate(groups):
            q = q_s[rows, lanes]
            cexp = cexp_s[rows, lanes]
            end = cexp[C - 1 : C, :]
            s = run_s[g]
            s_hi, s_lo = split(s)
            shi_s[i, :, lanes] = s_hi
            slo_s[i, :, lanes] = s_lo
            outs = []
            for p in range(2):
                w = window(p)
                outs.append(dot(q[:, w], block_state(s_hi[:, w], p)) + dot(q[:, w], block_state(s_lo[:, w], p)))
            att_s[rows, lanes] += jnp.exp2(cexp) * merge(*outs)
            run_s[g] = jnp.exp2(end) * s + u_s[i, :, lanes]
        att = att_s[rows, :]
        grown = do_s[rows, :].astype(F32) * gain_ref[...]
        sums_s[i] = jnp.concatenate(
            [token_sums(att * att), token_sums(grown * att), jnp.zeros((6, C), F32)], axis=0
        )

    def sums_copy(b, target):
        part = pl.ds(b * per, per)
        return pltpu.make_async_remote_copy(
            src_ref=sums_s.at[part], dst_ref=sums_t.at[my_head, part], send_sem=sums_sems.at[0, b],
            recv_sem=sums_sems.at[1, b], device_id={"head": target}, device_id_type=MESH,
        )

    def norm_rows(i):
        rows = rows_of(i)
        if remote:
            sums = sums_t[0, i]
            for j in range(1, head_shards):
                sums = sums + sums_t[j, i]
        else:
            sums = sums_s[i]
        rms = jnp.sqrt(sums[0:1, :] / total_width + 1e-06)
        inv = 1.0 / rms
        mean = sums[1:2, :] * inv / total_width
        inv_c = jnp.broadcast_to(inv, (C, C)).T
        coef_c = jnp.broadcast_to(mean * inv * inv, (C, C)).T
        inv_c = jnp.concatenate([inv_c] * 3, axis=1)
        coef_c = jnp.concatenate([coef_c] * 3, axis=1)
        for g, lanes in enumerate(groups):
            att = att_s[rows, lanes]
            up = do_s[rows, lanes].astype(F32)
            gain = gain_ref[:, lanes]
            normed = att * inv_c
            out_ref[rows, lanes] = (normed * gain).astype(BF16)
            dg_s[:, lanes] += jnp.sum((up * normed).reshape(C // 8, 8, GL), axis=0)
            grad = up * gain * inv_c - att * coef_c
            g_hi, g_lo = split(grad)
            ghi_s[rows, lanes] = g_hi
            glo_s[rows, lanes] = g_lo
            cexp = cexp_s[rows, lanes]
            end = cexp[C - 1 : C, :]
            e_hi, e_lo = split(grad * jnp.exp2(cexp))
            e_both = jnp.concatenate([e_hi, e_lo], axis=0)
            qt = qt_s[i, lanes, :]
            parts = []
            for p in range(2):
                qp = qt[192 * p : 192 * p + 192]
                parts.append(compact(dot(jnp.concatenate([qp, qp], axis=1), e_both[:, window(p)]), p))
            w = merge(*parts)
            u_s[i, :, lanes] = w
            own_s[g] += jnp.exp2(start_s[0:1, lanes]) * w
            start_s[0:1, lanes] += end

    def grad_rows(i):
        rows = rows_of(i)
        ct = ct_of(i)
        cols = columns_of(ct)
        bias = causal_bias()
        for g, lanes in enumerate(groups):
            q, k, v = q_s[rows, lanes], k_s[rows, lanes], v_s[rows, lanes]
            g_hi, g_lo = ghi_s[rows, lanes], glo_s[rows, lanes]
            from_start = jnp.exp2(cexp_s[rows, lanes])
            s_hi, s_lo = shi_s[i, :, lanes], slo_s[i, :, lanes]
            dqs, olds, dks, dvs = [], [], [], []
            for p in range(2):
                w = window(p)
                heads = (4 * g + 2 * p, 4 * g + 2 * p + 1)
                pair = slice(256 * (2 * g + p), 256 * (2 * g + p) + 256)
                hw, lw = g_hi[:, w], g_lo[:, w]
                hs, ls = stacked(hw, p), stacked(lw, p)
                decay = pair_decay(ct, cols, heads, bias)
                b_hi, b_lo = block_state(s_hi[:, w], p), block_state(s_lo[:, w], p)
                d_hi, d_lo = split(both_nt(hw, lw, stacked(v[:, w], p)) * decay)
                ks = stacked(k[:, w], p)
                dqs.append(dot(d_hi, ks) + dot(d_lo, ks))
                olds.append(both_nt(hw, lw, b_hi) + dot_nt(hw, b_lo))
                dks.append(both(turned(d_hi), turned(d_lo), stacked(q[:, w], p)))
                p_hi, p_lo = phi_s[rows, pair], plo_s[rows, pair]
                dvs.append(both(p_hi, p_lo, hs) + dot(p_hi, ls))
            dq_ref[rows, lanes] = (merge(*dqs) + from_start * merge(*olds)).astype(BF16)
            dk_s[rows, lanes] = merge(*dks)
            dv_s[rows, lanes] = merge(*dvs)

    def over(lo, hi, f):
        pl.loop(lo, hi, unroll=2 if (hi - lo) % 2 == 0 else 1)(f)

    def piece(b, f):
        pl.loop(0, per, unroll=per)(lambda j: f(b * per + j))

    pl.loop(0, PIECES)(lambda b: piece(b, exponents))

    @pl.loop(0, PIECES)
    def _(b):
        arrival(0, b).wait()
        arrival(1, b).wait()
        piece(b, states)

    totals = [
        group_lanes([jnp.broadcast_to(tot_s[h : h + 1, :], (8, 128)) for h in range(4 * g, 4 * g + 4)])
        for g in range(2)
    ]
    if remote:
        low = core == 0
        own_total, other_total = jnp.where(low, *totals), jnp.where(low, *totals[::-1])
        pl.semaphore_wait(barrier, chips + head_shards - 1)
        on.start(own_s, other_total)
    for b in range(PIECES):
        arrival(2, b).wait()
        arrival(3, b).wait()
    cuts = [chunks * c // 12 for c in LOCAL_CUTS]
    over(0, cuts[0], local_rows)
    if remote:
        on.combine(own_s, own_total)
    over(cuts[0], cuts[1], local_rows)
    if remote:
        on.middle(on.taken)
    over(cuts[1], cuts[2], local_rows)
    if remote:
        on.gather(run_s)
    over(cuts[2], chunks, local_rows)
    if remote:
        on.finish(run_s)
    else:
        run_s[...] = jnp.zeros_like(run_s)
    @pl.loop(0, PIECES)
    def _(b):
        piece(b, whole_rows)
        if remote:
            part = pl.ds(b * per, per)
            sums_t[my_head, part] = sums_s[part]

            @pl.loop(1, head_shards)
            def _(i):
                sums_copy(b, lax.rem(my_head + i, head_shards)).start()

    own_s[...] = jnp.zeros_like(own_s)
    start_s[...] = jnp.zeros_like(start_s)
    dg_s[...] = jnp.zeros_like(dg_s)

    @pl.loop(0, PIECES)
    def _(b):
        if remote:
            moved = sums_t.at[pl.ds(0, head_shards - 1), pl.ds(b * per, per)]
            wait_bytes(moved, sums_sems.at[1, b])
            wait_bytes(moved, sums_sems.at[0, b])
        piece(b, norm_rows)

    sums = jnp.sum(dg_s[...], axis=0, keepdims=True)
    tile = jnp.concatenate(
        [sums[:, 128 * i : 128 * i + 128] for i in range(6)] + [jnp.zeros((2, 128), F32)], axis=0
    )
    cuts = [chunks * c // 12 for c in GRAD_CUTS]
    if remote:
        tile = jnp.concatenate([tile, jnp.zeros((8, GL - 128), F32)], axis=1)
        back.start(own_s, tile)
    over(0, cuts[0], grad_rows)
    if remote:
        back.combine(own_s, tile)
    over(cuts[0], cuts[1], grad_rows)
    if remote:
        back.middle(on.taken)
    over(cuts[1], cuts[2], grad_rows)
    if remote:
        back.gather(run_s)
        dgain_ref[...] = back.given[0, :, GL:]
    over(cuts[2], chunks, grad_rows)
    if remote:
        back.finish(run_s)
    else:
        dgain_ref[...] = tile
        run_s[...] = jnp.zeros_like(run_s)


def last_kernel(
    chunks, out_v, dq_v, k_s, v_s, dk_s, dv_s, u_s, cexp_s, state_ref, dgain_v,
    out_hbm, dq_hbm, dk_hbm, dv_hbm, dgain_ref, dk_ref, dv_ref, run_s, sems,
):
    first = [(out_v, out_hbm), (dq_v, dq_hbm)]
    for j, (src, dst) in enumerate(first):
        pltpu.make_async_copy(src, dst, sems.at[j, 0]).start()
    for j in range(dgain_ref.shape[0] // 128):
        dgain_ref[128 * j : 128 * j + 128] = dgain_v[j : j + 1, :].reshape(128)
    run_s[...] = state_ref[...]

    def copies(i):
        rows = rows_of(i)
        return [
            pltpu.make_async_copy(src.at[rows], dst.at[rows], sems.at[2 + j, i])
            for j, (src, dst) in enumerate([(dk_ref, dk_hbm), (dv_ref, dv_hbm)])
        ]

    def last_rows(i):
        rows = rows_of(i)
        for g, lanes in enumerate(groups):
            k, v = k_s[rows, lanes], v_s[rows, lanes]
            cexp = cexp_s[rows, lanes]
            end = cexp[C - 1 : C, :]
            tail = jnp.exp2(end - cexp)
            s = run_s[g]
            s_hi, s_lo = split(s)
            dks, dvs = [], []
            for p in range(2):
                w = window(p)
                b_hi, b_lo = block_state(s_hi[:, w], p), block_state(s_lo[:, w], p)
                dks.append(dot_nt(v[:, w], b_hi) + dot_nt(v[:, w], b_lo))
                dvs.append(dot(k[:, w], b_hi) + dot(k[:, w], b_lo))
            dk_ref[rows, lanes] = (dk_s[rows, lanes] + tail * merge(*dks)).astype(BF16)
            dv_ref[rows, lanes] = (dv_s[rows, lanes] + tail * merge(*dvs)).astype(BF16)
            run_s[g] = jnp.exp2(end) * s + u_s[i, :, lanes]
        for copy in copies(i):
            copy.start()

    pl.loop(0, chunks, unroll=3)(lambda i: last_rows(chunks - 1 - i))
    for j, (src, dst) in enumerate(first):
        pltpu.make_async_copy(src, dst, sems.at[j, 0]).wait()

    @pl.loop(0, chunks)
    def _(i):
        for copy in copies(i):
            copy.wait()


def body(shards, head_shards, queries, keys, values, log_decay, gain, d_out):
    n, width = queries.shape
    chunks = n // C
    ld_t = log_decay.reshape(chunks, C, 8).transpose(0, 2, 1).reshape(chunks * 8, C)
    hbm, vmem = pl.BlockSpec(memory_space=pl.ANY), pl.BlockSpec(memory_space=pltpu.VMEM)
    rows = lambda dtype: pltpu.VMEM((n, width), dtype)
    chips = max(shards // 2, 1)
    scan = lambda sent: [
        pltpu.VMEM((HS + 8, GL), F32),
        pltpu.VMEM((HS + 8, GL), F32),
        pltpu.VMEM((OWNERS, 8, 512), F32),
        pltpu.VMEM((chips, 8, 512), F32),
        pltpu.VMEM((chips, 8, sent), F32),
        pltpu.VMEM((OWNERS, 8, sent), F32),
        pltpu.VMEM((HS, GL), F32),
        pltpu.VMEM((HS, GL), F32),
        pltpu.SemaphoreType.DMA((8,)),
    ]
    scratch = [
        rows(BF16), rows(BF16),
        pltpu.SemaphoreType.DMA((4, PIECES)),
        pltpu.VMEM((chunks * 8, C), F32),
        pltpu.VMEM((chunks, HS, width), BF16),
        pltpu.VMEM((chunks, HS, width), BF16),
        rows(BF16), rows(BF16),
        pltpu.VMEM((n, 1024), BF16), pltpu.VMEM((n, 1024), BF16),
        pltpu.VMEM((2, HS, GL), F32),
        pltpu.VMEM((8, 128), F32),
        pltpu.VMEM((8, width), F32),
        pltpu.VMEM((8, width), F32),
        pltpu.VMEM((1, width), F32),
        pltpu.VMEM((chunks, 8, C), F32),
        pltpu.VMEM((head_shards, chunks, 8, C), F32),
        pltpu.SemaphoreType.DMA((2, PIECES)),
        pltpu.VMEM((chunks, width, C), BF16),
        pltpu.VMEM((2, 8, GL), F32),
    ] + scan(GL) + scan(512)
    params = dict(vmem_limit_bytes=VMEM_LIMIT)
    if shards > 1:
        params.update(collective_id=0, has_side_effects=True)
    held = [rows(BF16)] * 4 + [
        rows(F32), rows(F32), pltpu.VMEM((chunks, HS, width), F32), rows(F32),
        pltpu.VMEM((2, HS, GL), F32), pltpu.VMEM((8, 128), F32),
    ]
    held = pl.pallas_call(
        functools.partial(
            layer_kernel, shards, head_shards, float(width * head_shards), chunks
        ),
        in_specs=[hbm] * 4 + [vmem, vmem],
        out_specs=[vmem] * len(held),
        out_shape=held,
        scratch_shapes=scratch,
        compiler_params=pltpu.CompilerParams(**params),
        name="layer",
    )(queries, keys, values, d_out, gain, ld_t)
    out = jax.ShapeDtypeStruct((n, width), BF16)
    return pl.pallas_call(
        functools.partial(last_kernel, chunks),
        in_specs=[vmem] * len(held),
        out_specs=[hbm] * 4 + [vmem],
        out_shape=[out] * 4 + [jax.ShapeDtypeStruct((width,), F32)],
        scratch_shapes=[
            rows(BF16), rows(BF16), pltpu.VMEM((2, HS, GL), F32), pltpu.SemaphoreType.DMA((4, chunks))
        ],
        compiler_params=pltpu.CompilerParams(vmem_limit_bytes=LAST_LIMIT),
        name="last",
    )(*held)


LOCAL_CUTS = (2, 6, 12)
GRAD_CUTS = (2, 6, 10)
VMEM_LIMIT = 35 * 1024 * 1024
LAST_LIMIT = 12 * 1024 * 1024


def solution(mesh):
    rows = P("ctx", "head")
    return jax.shard_map(
        functools.partial(body, mesh.shape["ctx"], mesh.shape["head"]),
        mesh=mesh,
        in_specs=(rows, rows, rows, rows, P("head"), rows),
        out_specs=(rows, rows, rows, rows, P("head")),
        check_vma=False,
    )
```
